128 devices in a mesh: tx: 16 (over x, z), ty: 8 (over y, core).
Axes of the slice: x: 4, y: 4, z: 4, core: 2. Of those that a mesh axis runs over, the one named last changes fastest.
Arguments:
- points: bfloat16 [64, 393216], P(None, ('tx', 'ty')), may hold values from -10 to 10
- right_side: float32 [393216], P(('tx', 'ty')), may hold values from -4 to 6
- near_list: int32 [384, 6], P(('tx', 'ty')), may hold values from -1 to 383, as said below
- leaf_skeleton: int32 [384, 256], P(('tx', 'ty')), may hold values from 0 to 1023, as said below
- top_index: int32 [4096], P(('tx', 'ty')), may hold values from 0 to 767, as said below
Outputs:
- solution_field: float32 [393216], P(('tx', 'ty'))
- residual: float32 [393216], P(('tx', 'ty'))
The draws below stay inside these ranges and needn't reach their ends.
Inputs may be any that keep to these rules, and one draw needn't show every extreme that they name: `near_list`: each non-empty entry names a leaf of the device with the same ty index whose tx index lies at most 2 away along tx, counted cyclically. The lists are symmetric: m stands in l's list exactly as often as l stands in m's. In every draw the leaves of some device fill all 6 slots. `leaf_skeleton`: each row names 256 different points. `top_index`: each block of 32 entries names different entries.
All inputs are finite; a program needn't handle non-finite values.
Results may differ from the reference program's by a relative error of at most 0.0003.
Values may be sent and summed in bfloat16 or wider, within the bound.
A program may use at most 64 MiB of HBM per device.

```python
import math
import jax
import jax.numpy as jnp
from jax import lax

D = 64
LEAF = 1024
SKEL = 256
GSKEL = 256
NNEAR = 6
REACH = 2
ITERS = 2
LDEV = 3
LEAVES = 384
POINTS = 393216
GROUPS = 16
GLEAVES = 24
TSK = 32
N_TX = 16
N_TY = 8


def draw_points(key, part):
    key = jax.random.fold_in(key, 15)
    key_list = jax.random.split(key, 3)
    kernel_width = 20.0
    log_ratio = math.log(LEAF / 3.2)
    spread = (2.0 * D - math.sqrt(4.0 * D * D - 16.0 * D * log_ratio)) / (8.0 * D)
    jitter_scale = math.sqrt(kernel_width * spread)
    offset_scale = math.sqrt(kernel_width / (4.0 * D))
    radius = math.sqrt(kernel_width / 4.0)
    leaf_ids = jnp.arange(LEAVES, dtype=jnp.int32)
    device_id = leaf_ids // LDEV
    row_id = device_id // N_TY
    col_id = device_id % N_TY
    angles_row = row_id.astype(jnp.float32) * (2.0 * math.pi / N_TX)
    circle = jnp.concatenate([radius * jnp.cos(angles_row)[None, :], radius * jnp.sin(angles_row)[None, :], jnp.zeros((D - 2, LEAVES), jnp.float32)], axis=0)
    col_offsets = offset_scale * jnp.clip(jax.random.normal(key_list[0], (D, N_TY), jnp.float32), -3.0, 3.0)
    leaf_offsets = offset_scale * jnp.clip(jax.random.normal(key_list[1], (D, LEAVES), jnp.float32), -3.0, 3.0)
    centres = circle + col_offsets[:, col_id] + leaf_offsets
    jitter = jitter_scale * jnp.clip(jax.random.normal(key_list[2], (D, LEAVES, LEAF), jnp.float32), -4.5, 4.5)
    return (centres[:, :, None] + jitter).reshape(D, POINTS).astype(jnp.bfloat16)


def draw_right_side(key, part):
    key = jax.random.fold_in(key, 11)
    rough = jnp.clip(jax.random.normal(key, (POINTS,), jnp.float32), -4.5, 4.5)
    return 1.0 + rough


def draw_near_list(key, part):
    key = jax.random.fold_in(key, 12)
    key_list = jax.random.split(key, 4)
    half_count = NNEAR // 2
    step_row = jax.random.randint(key_list[0], (half_count,), -REACH, REACH + 1)
    step_leaf = jax.random.randint(key_list[1], (half_count,), 0, LDEV)
    step_row = jnp.where((step_row == 0) & (step_leaf == 0), 1, step_row)
    leaf_ids = jnp.arange(LEAVES, dtype=jnp.int32)
    device_id = leaf_ids // LDEV
    local_id = leaf_ids % LDEV
    row_id = device_id // N_TY
    col_id = device_id % N_TY

    def partner(sign_value):
        new_row = (row_id[:, None] + sign_value * step_row[None, :]) % N_TX
        new_leaf = (local_id[:, None] + sign_value * step_leaf[None, :]) % LDEV
        return ((new_row * N_TY + col_id[:, None]) * LDEV + new_leaf).astype(jnp.int32)
    forward = partner(1)
    backward = partner(-1)
    hot_device = jax.random.randint(key_list[2], (), 0, N_TX * N_TY)
    edge_bits = jax.random.randint(key_list[3], (LEAVES, half_count), 0, 4) == 0
    is_hot = device_id == hot_device
    edges = edge_bits | is_hot[:, None] | is_hot[forward]
    forward_slot = jnp.where(edges, forward, -1)
    back_edges = edges[backward, jnp.arange(half_count, dtype=jnp.int32)[None, :]]
    backward_slot = jnp.where(back_edges, backward, -1)
    return jnp.stack([forward_slot, backward_slot], axis=2).reshape(LEAVES, NNEAR).astype(jnp.int32)


def draw_leaf_skeleton(key, part):
    key = jax.random.fold_in(key, 13)
    key_list = jax.random.split(key, LEAVES)
    picked = jax.vmap(lambda one_key: jax.random.permutation(one_key, LEAF)[:SKEL])(key_list)
    return picked.astype(jnp.int32)


def draw_top_index(key, part):
    key = jax.random.fold_in(key, 14)
    key_list = jax.random.split(key, GROUPS * N_TY)
    picked = jax.vmap(lambda one_key: jax.random.permutation(one_key, LDEV * SKEL)[:TSK])(key_list)
    return picked.reshape(GROUPS * GSKEL).astype(jnp.int32)


def setup_inputs(seed: int = 0) -> dict:
    keys = jax.random.split(jax.random.key(seed), 6)
    return {
        "points": draw_points(jax.random.fold_in(keys[5], 71), 0),
        "right_side": draw_right_side(jax.random.fold_in(keys[5], 71), 0),
        "near_list": draw_near_list(jax.random.fold_in(keys[5], 71), 0),
        "leaf_skeleton": draw_leaf_skeleton(jax.random.fold_in(keys[5], 71), 0),
        "top_index": draw_top_index(jax.random.fold_in(keys[5], 71), 0),
    }


width_inv = 1.0 / 20.0
far_weight = 32.0
highest = lax.Precision.HIGHEST


def kernel(targets, sources):
    inner_prod = lax.dot_general(targets, sources, (((0,), (0,)), ((), ())), preferred_element_type=jnp.float32)
    target_sq = jnp.sum(jnp.square(targets.astype(jnp.float32)), axis=0)
    source_sq = jnp.sum(jnp.square(sources.astype(jnp.float32)), axis=0)
    return jnp.exp((2.0 * inner_prod - target_sq[:, None] - source_sq[None, :]) * width_inv)


def apply_block(targets, sources, vector):
    return jnp.dot(kernel(targets, sources), vector, precision=highest)


def column_block(array, index):
    return lax.dynamic_index_in_dim(array, index, 1, keepdims=False)


def skeletons(points, leaf_skeleton):
    blocks = points.reshape(D, LEAVES, LEAF)
    picked = jax.vmap(lambda source, chosen: jnp.take(source, chosen, axis=1), in_axes=(1, 0), out_axes=1)(blocks, leaf_skeleton)
    return picked.reshape(D, LEAVES * SKEL)


def near_part(points, near_list, vector):
    blocks = points.reshape(D, LEAVES, LEAF)
    values = vector.reshape(LEAVES, LEAF)

    def one_leaf(leaf_id):
        own_block = column_block(blocks, leaf_id)
        slot_row = near_list[leaf_id]
        degree = jnp.sum((slot_row >= 0).astype(jnp.float32))
        running = degree * apply_block(own_block, own_block, values[leaf_id])

        def add_slot(running, slot_id):
            other = jnp.maximum(slot_id, 0)

            def live_term():
                return apply_block(own_block, column_block(blocks, other), values[other])

            def dead_term():
                return jnp.zeros((LEAF,), jnp.float32)

            return running + lax.cond(slot_id >= 0, live_term, dead_term), None

        running, unused = lax.scan(add_slot, running, slot_row)
        return running

    totals = lax.map(one_leaf, jnp.arange(LEAVES, dtype=jnp.int32))
    return totals.reshape(POINTS) / NNEAR


def far_part(points, leaf_skeleton, top_index, vector):
    blocks = points.reshape(D, LEAVES, LEAF)
    skeleton = skeletons(points, leaf_skeleton)
    skel_blocks = skeleton.reshape(D, LEAVES, SKEL)
    values = vector.reshape(LEAVES, LEAF)
    scale_leaf = 0.25
    scale_group = LEAF / (GLEAVES * SKEL)
    scale_top = LEAF / (GROUPS * GSKEL)

    def up_leaf(leaf_id):
        return apply_block(column_block(skel_blocks, leaf_id), column_block(blocks, leaf_id), values[leaf_id])

    weights = lax.map(up_leaf, jnp.arange(LEAVES, dtype=jnp.int32)) * scale_leaf
    block_count = GROUPS * N_TY
    top_cols = (jnp.arange(block_count, dtype=jnp.int32)[:, None] * (LDEV * SKEL) + top_index.reshape(block_count, TSK)).reshape(GROUPS * GSKEL)
    top_points = jnp.take(skeleton, top_cols, axis=1)
    group_skel = skeleton.reshape(D, GROUPS, GLEAVES * SKEL)
    group_top = top_points.reshape(D, GROUPS, GSKEL)
    group_weights = weights.reshape(GROUPS, GLEAVES * SKEL)

    def up_group(group):
        return apply_block(column_block(group_top, group), column_block(group_skel, group), group_weights[group])

    upper_sums = lax.map(up_group, jnp.arange(GROUPS, dtype=jnp.int32)) * scale_group
    flat_upper = upper_sums.reshape(GROUPS * GSKEL)

    def across(group):
        return apply_block(column_block(group_top, group), top_points, flat_upper)

    middle = lax.map(across, jnp.arange(GROUPS, dtype=jnp.int32)) * scale_top

    def down_group(group):
        return apply_block(column_block(group_skel, group), column_block(group_top, group), middle[group])

    lower_part = lax.map(down_group, jnp.arange(GROUPS, dtype=jnp.int32)) * scale_group
    lower_part = lower_part.reshape(LEAVES, SKEL)

    def down_leaf(leaf_id):
        return apply_block(column_block(blocks, leaf_id), column_block(skel_blocks, leaf_id), lower_part[leaf_id])

    result = lax.map(down_leaf, jnp.arange(LEAVES, dtype=jnp.int32)) * scale_leaf
    return result.reshape(POINTS)


def reference(points, right_side, near_list, leaf_skeleton, top_index):
    def operate(vector):
        return vector + near_part(points, near_list, vector) + far_weight * far_part(points, leaf_skeleton, top_index, vector)

    solution_field = jnp.zeros_like(right_side)
    residual = right_side
    direction = right_side
    norm_now = jnp.sum(residual * residual)
    for step in range(ITERS):
        image = operate(direction)
        alpha = norm_now / jnp.sum(direction * image)
        solution_field = solution_field + alpha * direction
        residual = residual - alpha * image
        norm_next = jnp.sum(residual * residual)
        direction = residual + (norm_next / norm_now) * direction
        norm_now = norm_next
    return solution_field, residual
```

```python
import functools
import math

import jax
import jax.numpy as jnp
from jax import lax
from jax.experimental import pallas as pl
from jax.experimental.pallas import tpu as pltpu
from jax.sharding import PartitionSpec as P

F32 = jnp.float32
BF16 = jnp.bfloat16
HI = lax.Precision.HIGHEST

D = 64
LEAF = 1024
HALF = 512
SKEL = 256
LDEV = 3
HALVES = LDEV * 2
SLOTS = 6
TSK = 32
N_TX = 16
N_TY = 8
GSKEL = TSK * N_TY
REACH = 2
GAPS = 2 * REACH + 1
ROWS = 8 * GAPS
MINE = 8 * REACH
QUADS = LDEV * SLOTS * 2
CHUNK = 128

SCALE = 2.0 * math.log2(math.e) / 20.0
A_LEAF = 0.25
E_GROUP = LEAF / (LDEV * N_TY * SKEL)
E_TOP = LEAF / (N_TX * GSKEL)
FAR = 32.0


def split3(x):
    high = x.astype(BF16)
    rest = x - high.astype(F32)
    mid = rest.astype(BF16)
    low = (rest - mid.astype(F32)).astype(BF16)
    return high, mid, low


def aux_rows(coords, first):
    wide = coords.astype(F32)
    norm = (-0.5 * SCALE) * jnp.sum(wide * wide, axis=0, keepdims=True)
    high, mid, low = [t.astype(F32) for t in split3(norm)]
    row = lax.broadcasted_iota(jnp.int32, (16, coords.shape[1]), 0)
    lead = 0 if first else 3
    ones = jnp.where((row >= 3 - lead) & (row < 6 - lead), 1.0, 0.0)
    parts = jnp.where(row == lead, high, jnp.where(row == lead + 1, mid, jnp.where(row == lead + 2, low, ones)))
    return parts


def source_form(coords, aux):
    pad = jnp.zeros((48, coords.shape[1]), BF16)
    return jnp.concatenate([coords, coords, coords, aux, pad], axis=0)


def target_form(coords):
    high, mid, low = split3(coords.astype(F32) * SCALE)
    pad = jnp.zeros((48, coords.shape[1]), F32)
    aux = aux_rows(coords, True)
    stack = jnp.concatenate([high.astype(F32), mid.astype(F32), low.astype(F32), aux, pad], axis=0)
    return stack.T.astype(BF16)


def lane_aux(wide, first):
    norm = (-0.5 * SCALE) * jnp.sum(wide * wide, axis=1, keepdims=True)
    high, mid, low = [t.astype(F32) for t in split3(norm)]
    lane = lax.broadcasted_iota(jnp.int32, wide.shape, 1) - D
    lead = 0 if first else 3
    ones = jnp.where((lane >= 3 - lead) & (lane < 6 - lead), 1.0, 0.0)
    return jnp.where(lane == lead, high, jnp.where(lane == lead + 1, mid, jnp.where(lane == lead + 2, low, ones)))


def row_targets(raw):
    wide = raw.astype(F32)
    high, mid, low = [t.astype(F32) for t in split3(wide * SCALE)]
    left = high + pltpu.roll(mid, D, 1)
    right = low + lane_aux(wide, True)
    return jnp.concatenate([left, right], axis=1).astype(BF16)


def row_sources(raw):
    wide = raw.astype(F32)
    left = wide + pltpu.roll(wide, D, 1)
    right = wide + lane_aux(wide, False)
    return jnp.concatenate([left, right], axis=1).astype(BF16)


def to_row(columns):
    ones = jnp.ones((8, 128), F32)
    return lax.dot_general(
        ones, columns, (((1,), (1,)), ((), ())), precision=HI, preferred_element_type=F32
    )[0:1]


def to_column(row):
    parts = []
    for start in range(0, row.shape[1], 128):
        piece = jnp.broadcast_to(row[:, start : start + 128], (128, 128))
        parts.append(piece.T)
    return jnp.concatenate(parts, axis=0) if len(parts) > 1 else parts[0]


def fold_lanes(tile):
    total = tile[:, 0:128]
    for start in range(128, tile.shape[1], 128):
        total = total + tile[:, start : start + 128]
    return total


def fold_rows(tile):
    return jnp.sum(tile.reshape(tile.shape[0] // 8, 8, tile.shape[1]), axis=0)


def tile_lanes(column, width):
    return jnp.concatenate([column] * (width // 128), axis=1)


def body(
    pts_in, rhs_in, near, skel_in, top_in, x_out, r_out,
    pts, aux, vals, taug, vb, acc, kq, kd, ka, ku, kc, cbuf, moh,
    zsend, zin, skp, gg, gt, psend, pin, usend, uin, wsend, win, s_one, s_ty, s_tx, s_two,
    pt_s, pt_r, va_s, va_r, z_s, z_r, g_s, g_r, p_s, p_r, u_s, u_r, w_s, w_r, a_s, a_r, b_s, b_r,
):
    my_tx = lax.axis_index("tx")
    my_ty = lax.axis_index("ty")

    def tx_at(step):
        return lax.rem(my_tx + (step + N_TX), N_TX)

    def ty_at(step):
        return lax.rem(my_ty + (step + N_TY), N_TY)

    def send(src, dst, s_sem, r_sem, **where):
        copy = pltpu.make_async_remote_copy(
            src_ref=src, dst_ref=dst, send_sem=s_sem, recv_sem=r_sem,
            device_id=where, device_id_type=pl.DeviceIdType.MESH,
        )
        return copy

    barrier = pltpu.get_barrier_semaphore()
    for step in range(1, N_TX):
        pl.semaphore_signal(barrier, inc=1, device_id={"tx": tx_at(step)}, device_id_type=pl.DeviceIdType.MESH)
    for step in range(1, N_TY):
        pl.semaphore_signal(barrier, inc=1, device_id={"ty": ty_at(step)}, device_id_type=pl.DeviceIdType.MESH)
    for half in range(HALVES):
        vals[0, MINE + half] = rhs_in[half]
    for half in range(HALVES, 8):
        vals[0, MINE + half] = jnp.zeros((1, HALF), F32)
        vals[1, MINE + half] = jnp.zeros((1, HALF), F32)
    for half in range(HALVES):
        pts[MINE + half] = pts_in[:, half * HALF : (half + 1) * HALF]
    pl.semaphore_wait(barrier, N_TX - 1 + N_TY - 1)

    remote_gaps = [1, -1, 2, -2]
    copies = []
    for number, gap in enumerate(remote_gaps):
        place = 8 * (gap + REACH)
        copy = send(vals.at[0, pl.ds(MINE, 8)], vals.at[0, pl.ds(place, 8)], va_s.at[0, number], va_r.at[0, number], tx=tx_at(-gap))
        copy.start()
        copies.append(copy)
    point_copies = []
    for number, gap in enumerate(remote_gaps):
        place = 8 * (gap + REACH)
        copy = send(
            pts.at[pl.ds(MINE, HALVES)], pts.at[pl.ds(place, HALVES)], pt_s.at[number], pt_r.at[number], tx=tx_at(-gap)
        )
        copy.start()
        point_copies.append(copy)
    value_copies = {0: copies}

    def slot(leaf, number, half):
        named = near[leaf, number]
        live = named >= 0
        named = jnp.maximum(named, 0)
        place = lax.rem(lax.div(named, LDEV * N_TY) - my_tx + (N_TX + REACH), N_TX)
        other = lax.rem(named, LDEV)
        same = place == REACH
        itself = live & same & (other == leaf)
        use = live & jnp.logical_not(itself) & (place < GAPS)
        back = jnp.where((place < REACH) | (same & (other < leaf)), 1, 0)
        other_half = half + back - 2 * half * back
        index = jnp.where(use, 8 * place + 2 * other + other_half, MINE)
        return index, jnp.where(use, 1.0, 0.0), jnp.where(live, 1.0, 0.0) + jnp.where(itself, 1.0, 0.0)

    def split_quad(quad):
        return lax.div(quad, 2 * SLOTS), lax.rem(lax.div(quad, 2), SLOTS), lax.rem(quad, 2)

    def degree(leaf):
        total = 0.0
        for number in range(SLOTS):
            total = total + slot(leaf, number, 0)[2]
        return total

    sub = lax.broadcasted_iota(jnp.int32, (ROWS, 128), 0)
    lane = lax.broadcasted_iota(jnp.int32, (ROWS, 128), 1)

    def mark(quad, table):
        index, use, unused = slot(*split_quad(quad))
        return jnp.where((lane == quad) & (sub == index), use, table)

    table = lax.fori_loop(0, QUADS, mark, jnp.zeros((ROWS, 128), F32))
    for leaf in range(LDEV):
        table = jnp.where((lane == QUADS + leaf) & (sub == MINE + 2 * leaf + 1), degree(leaf), table)
    moh[...] = table
    cbuf[pl.ds(QUADS, 128 - QUADS)] = jnp.zeros((128 - QUADS, HALF), F32)

    def own_forms(half, carry):
        coords = pts[MINE + half]
        taug[half] = target_form(coords)
        aux[MINE + half] = aux_rows(coords, False).astype(BF16)
        return carry

    skp[pl.ds(D, 128 - D)] = jnp.zeros((128 - D, LDEV * SKEL), BF16)
    for leaf in range(LDEV):
        chosen = skel_in[leaf : leaf + 1]
        picked = jnp.zeros((D, SKEL), F32)
        for half in range(2):
            place = lax.broadcasted_iota(jnp.int32, (HALF, SKEL), 0) + half * HALF
            hot = jnp.where(place == chosen, 1.0, 0.0).astype(BF16)
            picked = picked + jnp.dot(pts[MINE + 2 * leaf + half], hot, preferred_element_type=F32)
        skp[0:D, leaf * SKEL : (leaf + 1) * SKEL] = picked.astype(BF16)
    wide_lane = lax.broadcasted_iota(jnp.int32, (1, LDEV * SKEL), 1)
    hot_rows = [jnp.where(wide_lane == top_in[t], 1.0, 0.0) for t in range(TSK)]
    hot = jnp.concatenate(hot_rows, axis=0).astype(BF16)
    mine_top = lax.dot_general(
        hot, skp[...], (((1,), (1,)), ((), ())), preferred_element_type=F32
    ).astype(BF16)
    gg[my_ty] = mine_top
    gt[my_tx] = mine_top
    group_copies = []
    for step in range(1, N_TY):
        copy = send(gg.at[my_ty], gg.at[my_ty], g_s.at[step], g_r.at[step], ty=ty_at(step))
        copy.start()
        group_copies.append(copy)
    for step in range(1, N_TX):
        copy = send(gt.at[my_tx], gt.at[my_tx], g_s.at[N_TY + step], g_r.at[N_TY + step], tx=tx_at(step))
        copy.start()
        group_copies.append(copy)

    lax.fori_loop(0, HALVES, own_forms, 0)

    def spread(it):
        def step(half, carry):
            vb[half] = to_column(vals[it, MINE + half])
            return carry
        lax.fori_loop(0, HALVES, step, 0)

    def skeleton_form(leaf):
        coords = skp[0:D, leaf * SKEL : (leaf + 1) * SKEL]
        return source_form(coords, aux_rows(coords, False).astype(BF16))

    def up_leaf(it):
        parts = []
        for leaf in range(LDEV):
            if it == 0:
                form = skeleton_form(leaf)
            total = jnp.zeros((8, SKEL), F32)
            for half in range(2):
                row = 2 * leaf + half
                if it == 0:
                    ka[row] = jnp.exp2(jnp.dot(taug[row], form, preferred_element_type=F32))
                total = total + fold_rows(ka[row] * tile_lanes(vb[row], SKEL))
            parts.append(jnp.sum(total, axis=0, keepdims=True))
        return jnp.concatenate(parts, axis=1) * A_LEAF

    narrow = lax.broadcasted_iota(jnp.int32, (1, 128), 1)

    def up_group(it, weights):
        partial = to_row(fold_lanes(ku[...] * weights)) * E_GROUP
        for part in range(N_TY):
            tile = partial[:, 128 * (part // 4) : 128 * (part // 4) + 128]
            shift = (128 - TSK * (part % 4)) % 128
            if shift:
                tile = pltpu.roll(tile, shift, 1)
            psend[it, part] = jnp.where(narrow < TSK, tile, 0.0)
        out = []
        pin[it, my_ty] = psend[it, my_ty]
        for step in range(1, N_TY):
            copy = send(psend.at[it, ty_at(step)], pin.at[it, my_ty], p_s.at[it, step], p_r.at[it, step], ty=ty_at(step))
            copy.start()
            out.append(copy)
        return out

    def over_top(it, waiting):
        for copy in waiting:
            copy.wait()
        usend[it] = jnp.sum(pin[it], axis=0)
        uin[it, my_tx] = usend[it]
        out = []
        for step in range(1, N_TX):
            copy = send(usend.at[it], uin.at[it, my_tx], u_s.at[it, step], u_r.at[it, step], tx=tx_at(step))
            copy.start()
            out.append(copy)
        return out

    def across(it, waiting):
        for copy in waiting:
            copy.wait()
        tiles = []
        for tile in range(4):
            total = uin[it, 4 * tile]
            for k in range(1, 4):
                total = total + pltpu.roll(uin[it, 4 * tile + k], TSK * k, 1)
            tiles.append(total)
        upper = jnp.concatenate(tiles, axis=1)
        wsend[it] = to_row(fold_lanes(kc[...] * upper)) * E_TOP
        win[it, my_ty] = wsend[it]
        out = []
        for step in range(1, N_TY):
            copy = send(wsend.at[it], win.at[it, my_ty], w_s.at[it, step], w_r.at[it, step], ty=ty_at(step))
            copy.start()
            out.append(copy)
        return out

    def down(it, waiting):
        for copy in waiting:
            copy.wait()
        middle = to_column(jnp.sum(win[it], axis=0))
        lower = fold_rows(ku[...] * tile_lanes(middle, LDEV * SKEL))
        lower = jnp.sum(lower, axis=0, keepdims=True) * (E_GROUP * A_LEAF * FAR * SLOTS)
        for leaf in range(LDEV):
            weights = lower[:, leaf * SKEL : (leaf + 1) * SKEL]
            for half in range(2):
                row = 2 * leaf + half
                acc[row] += fold_lanes(ka[row] * weights)

    def quadrant(it, store, index, row, form, values, fresh, both):
        total = jnp.zeros((8, HALF), F32)
        for start in range(0, HALF, CHUNK):
            rows = pl.ds(start, CHUNK)
            if it == 0:
                tile = jnp.exp2(jnp.dot(taug[row, rows], form, preferred_element_type=F32))
                store[index, rows] = tile
            else:
                tile = store[index, rows]
            part = fold_lanes(tile * values)
            if fresh:
                acc[row, rows] = part
            else:
                acc[row, rows] += part
            if both:
                total = total + fold_rows(tile * tile_lanes(vb[row, rows], HALF))
        return jnp.sum(total, axis=0, keepdims=True)

    def form_of(index):
        return source_form(pts[index], aux[index])

    def diagonal(it):
        def step(leaf, carry):
            weight = degree(leaf)
            low, high = 2 * leaf, 2 * leaf + 1
            form_low = form_of(MINE + low) if it == 0 else None
            form_high = form_of(MINE + high) if it == 0 else None
            v_low = vals[it, MINE + low] * weight
            v_high = vals[it, MINE + high] * weight
            quadrant(it, kd, 3 * leaf, low, form_low, v_low, True, False)
            quadrant(it, kd, 3 * leaf + 1, high, form_high, v_high, True, False)
            cbuf[pl.ds(QUADS + leaf, 1)] = quadrant(it, kd, 3 * leaf + 2, low, form_high, v_high, False, True)
            return carry
        lax.fori_loop(0, LDEV, step, 0)

    def slots(it, start, stop):
        def step(quad, carry):
            leaf, number, half = split_quad(quad)
            index, use, unused = slot(leaf, number, half)
            form = form_of(index) if it == 0 else None
            values = vals[it, index] * use
            cbuf[pl.ds(quad, 1)] = quadrant(it, kq, quad, 2 * leaf + half, form, values, False, True)
            return carry
        lax.fori_loop(start, stop, step, 0)

    def send_back(it):
        parts = jnp.dot(moh[...], cbuf[...], precision=HI, preferred_element_type=F32)
        for place in range(GAPS):
            zsend[it, place] = parts[8 * place : 8 * place + 8]
        out = []
        for number, gap in enumerate(remote_gaps):
            copy = send(
                zsend.at[it, gap + REACH], zin.at[it, REACH - gap], z_s.at[it, number], z_r.at[it, number], tx=tx_at(gap)
            )
            copy.start()
            out.append(copy)
        return out

    def finish(it, waiting):
        rows = [to_row(acc[half]) for half in range(HALVES)]
        for copy in waiting:
            copy.wait()
        total = zsend[it, REACH]
        for gap in remote_gaps:
            total = total + zin[it, REACH - gap]
        own = jnp.concatenate(rows + [jnp.zeros((8 - HALVES, HALF), F32)], axis=0)
        return (own + total) * (1.0 / SLOTS)

    def own_rows(it):
        return jnp.concatenate([vals[it, MINE + half] for half in range(8)], axis=0)

    def pack(*sums):
        row = jnp.zeros((1, 128), F32)
        for number, value in enumerate(sums):
            row = jnp.where(narrow == number, value, row)
        return row

    def sum_first(number, row):
        s_one[number] = row
        s_ty[number, my_ty] = row
        out = []
        for step in range(1, N_TY):
            copy = send(s_one.at[number], s_ty.at[number, my_ty], a_s.at[number, step], a_r.at[number, step], ty=ty_at(step))
            copy.start()
            out.append(copy)
        return out

    def sum_second(number, waiting):
        for copy in waiting:
            copy.wait()
        row = jnp.sum(s_ty[number], axis=0)
        s_two[number] = row
        s_tx[number, my_tx] = row
        out = []
        for step in range(1, N_TX):
            copy = send(s_two.at[number], s_tx.at[number, my_tx], b_s.at[number, step], b_r.at[number, step], tx=tx_at(step))
            copy.start()
            out.append(copy)
        return out

    def sum_last(number, waiting, count):
        for copy in waiting:
            copy.wait()
        row = jnp.sum(s_tx[number], axis=0)
        return [jnp.sum(jnp.where(narrow == k, row, 0.0), axis=1, keepdims=True) for k in range(count)]

    def dot(one, two):
        return jnp.sum(jnp.sum(one * two, axis=0, keepdims=True), axis=1, keepdims=True)

    spread(0)
    weights = up_leaf(0)
    for copy in group_copies:
        copy.wait()
    group_targets = row_targets(gg[...].reshape(GSKEL, 128))
    group_sources = row_sources(gt[...].reshape(N_TX * TSK, 128))
    for leaf in range(LDEV):
        ku[:, leaf * SKEL : (leaf + 1) * SKEL] = jnp.exp2(
            jnp.dot(group_targets, skeleton_form(leaf), preferred_element_type=F32)
        )
    kc[...] = jnp.exp2(
        lax.dot_general(group_targets, group_sources, (((1,), (1,)), ((), ())), preferred_element_type=F32)
    )
    flight = up_group(0, weights)
    diagonal(0)
    flight = over_top(0, flight)
    for copy in point_copies:
        copy.wait()
    for place in range(GAPS):
        if place != REACH:
            def remote_aux(half, carry, place=place):
                aux[8 * place + half] = aux_rows(pts[8 * place + half], False).astype(BF16)
                return carry
            lax.fori_loop(0, HALVES, remote_aux, 0)
    for copy in value_copies[0]:
        copy.wait()
    flight = across(0, flight)
    slots(0, 0, QUADS)
    back = send_back(0)
    down(0, flight)
    start = own_rows(0)
    first = start + finish(0, back)
    for half in range(HALVES):
        vals[1, MINE + half] = first[half : half + 1]

    copies = []
    for number, gap in enumerate(remote_gaps):
        place = 8 * (gap + REACH)
        copy = send(vals.at[1, pl.ds(MINE, 8)], vals.at[1, pl.ds(place, 8)], va_s.at[1, number], va_r.at[1, number], tx=tx_at(-gap))
        copy.start()
        copies.append(copy)
    sums = sum_first(0, pack(dot(start, start), dot(start, first)))
    spread(1)
    flight = up_group(1, up_leaf(1))
    diagonal(1)
    flight = over_top(1, flight)
    sums = sum_second(0, sums)
    for copy in copies:
        copy.wait()
    slots(1, 0, QUADS // 2)
    flight = across(1, flight)
    norm, curve = sum_last(0, sums, 2)
    alpha = norm / curve
    left = start - alpha * first
    sums = sum_first(1, pack(dot(left, left)))
    slots(1, QUADS // 2, QUADS)
    sums = sum_second(1, sums)
    back = send_back(1)
    down(1, flight)
    second = first + finish(1, back)
    (norm_next,) = sum_last(1, sums, 1)
    beta = norm_next / norm
    direction = left + beta * start
    image = (1.0 + beta) * first - alpha * second
    sums = sum_first(2, pack(dot(direction, image)))
    sums = sum_second(2, sums)
    (curve,) = sum_last(2, sums, 1)
    step = norm_next / curve
    x_out[...] = (alpha * start + step * direction)[0:HALVES]
    r_out[...] = (left - step * image)[0:HALVES]


def on_device(points, right_side, near_list, leaf_skeleton, top_index):
    vmem = pl.BlockSpec(memory_space=pltpu.VMEM)
    smem = pl.BlockSpec(memory_space=pltpu.SMEM)
    dma = pltpu.SemaphoreType.DMA
    out = jax.ShapeDtypeStruct((HALVES, HALF), F32)
    solution_field, residual = pl.pallas_call(
        body,
        out_shape=(out, out),
        in_specs=[vmem, vmem, smem, vmem, smem],
        out_specs=(vmem, vmem),
        scratch_shapes=[
            pltpu.VMEM((ROWS, D, HALF), BF16),
            pltpu.VMEM((ROWS, 16, HALF), BF16),
            pltpu.VMEM((2, ROWS, 1, HALF), F32),
            pltpu.VMEM((HALVES, HALF, 256), BF16),
            pltpu.VMEM((HALVES, HALF, 128), F32),
            pltpu.VMEM((HALVES, HALF, 128), F32),
            pltpu.VMEM((QUADS, HALF, HALF), F32),
            pltpu.VMEM((3 * LDEV, HALF, HALF), F32),
            pltpu.VMEM((HALVES, HALF, SKEL), F32),
            pltpu.VMEM((GSKEL, LDEV * SKEL), F32),
            pltpu.VMEM((GSKEL, N_TX * TSK), F32),
            pltpu.VMEM((128, HALF), F32),
            pltpu.VMEM((ROWS, 128), F32),
            pltpu.VMEM((2, GAPS, 8, HALF), F32),
            pltpu.VMEM((2, GAPS, 8, HALF), F32),
            pltpu.VMEM((128, LDEV * SKEL), BF16),
            pltpu.VMEM((N_TY, TSK, 128), BF16),
            pltpu.VMEM((N_TX, TSK, 128), BF16),
            pltpu.VMEM((2, N_TY, 1, 128), F32),
            pltpu.VMEM((2, N_TY, 1, 128), F32),
            pltpu.VMEM((2, 1, 128), F32),
            pltpu.VMEM((2, N_TX, 1, 128), F32),
            pltpu.VMEM((2, 1, GSKEL), F32),
            pltpu.VMEM((2, N_TY, 1, GSKEL), F32),
            pltpu.VMEM((3, 1, 128), F32),
            pltpu.VMEM((3, N_TY, 1, 128), F32),
            pltpu.VMEM((3, N_TX, 1, 128), F32),
            pltpu.VMEM((3, 1, 128), F32),
            dma((4,)), dma((4,)),
            dma((2, 4)), dma((2, 4)),
            dma((2, 4)), dma((2, 4)),
            dma((N_TX + N_TY,)), dma((N_TX + N_TY,)),
            dma((2, N_TY)), dma((2, N_TY)),
            dma((2, N_TX)), dma((2, N_TX)),
            dma((2, N_TY)), dma((2, N_TY)),
            dma((3, N_TY)), dma((3, N_TY)),
            dma((3, N_TX)), dma((3, N_TX)),
        ],
        compiler_params=pltpu.CompilerParams(
            collective_id=0, has_side_effects=True, vmem_limit_bytes=64 * 1024 * 1024 - 512 * 1024
        ),
        name="ridge_cg",
    )(points, right_side.reshape(HALVES, 1, HALF), near_list, leaf_skeleton, top_index)
    return solution_field.reshape(-1), residual.reshape(-1)


def solution(mesh):
    placed = (
        P(None, ("tx", "ty")),
        P(("tx", "ty")),
        P(("tx", "ty"), None),
        P(("tx", "ty"), None),
        P(("tx", "ty")),
    )
    return jax.shard_map(
        on_device,
        mesh=mesh,
        in_specs=placed,
        out_specs=(P(("tx", "ty")), P(("tx", "ty"))),
        check_vma=False,
    )
```

```python
import functools
import math

import jax
import jax.numpy as jnp
from jax import lax
from jax.experimental import pallas as pl
from jax.experimental.pallas import tpu as pltpu
from jax.sharding import PartitionSpec as P

F32 = jnp.float32
BF16 = jnp.bfloat16
HI = lax.Precision.HIGHEST

D = 64
LEAF = 1024
HALF = 512
SKEL = 256
LDEV = 3
HALVES = LDEV * 2
SLOTS = 6
TSK = 32
N_TX = 16
N_TY = 8
GSKEL = TSK * N_TY
REACH = 2
GAPS = 2 * REACH + 1
ROWS = 8 * GAPS
MINE = 8 * REACH
QUADS = LDEV * SLOTS * 2
CHUNK = 128
WAVES = 2
PART = HALF // WAVES
WIDE = SLOTS * PART

SCALE = 2.0 * math.log2(math.e) / 20.0
A_LEAF = 0.25
E_GROUP = LEAF / (LDEV * N_TY * SKEL)
E_TOP = LEAF / (N_TX * GSKEL)
FAR = 32.0


def split3(x):
    high = x.astype(BF16)
    rest = x - high.astype(F32)
    mid = rest.astype(BF16)
    low = (rest - mid.astype(F32)).astype(BF16)
    return high, mid, low


def aux_rows(coords, first):
    wide = coords.astype(F32)
    norm = (-0.5 * SCALE) * jnp.sum(wide * wide, axis=0, keepdims=True)
    high, mid, low = [t.astype(F32) for t in split3(norm)]
    row = lax.broadcasted_iota(jnp.int32, (16, coords.shape[1]), 0)
    lead = 0 if first else 3
    ones = jnp.where((row >= 3 - lead) & (row < 6 - lead), 1.0, 0.0)
    parts = jnp.where(row == lead, high, jnp.where(row == lead + 1, mid, jnp.where(row == lead + 2, low, ones)))
    return parts


def source_form(coords, aux):
    pad = jnp.zeros((48, coords.shape[1]), BF16)
    return jnp.concatenate([coords, coords, coords, aux, pad], axis=0)


def target_form(coords):
    high, mid, low = split3(coords.astype(F32) * SCALE)
    pad = jnp.zeros((48, coords.shape[1]), F32)
    aux = aux_rows(coords, True)
    stack = jnp.concatenate([high.astype(F32), mid.astype(F32), low.astype(F32), aux, pad], axis=0)
    return stack.T.astype(BF16)


def lane_aux(wide, first):
    norm = (-0.5 * SCALE) * jnp.sum(wide * wide, axis=1, keepdims=True)
    high, mid, low = [t.astype(F32) for t in split3(norm)]
    lane = lax.broadcasted_iota(jnp.int32, wide.shape, 1) - D
    lead = 0 if first else 3
    ones = jnp.where((lane >= 3 - lead) & (lane < 6 - lead), 1.0, 0.0)
    return jnp.where(lane == lead, high, jnp.where(lane == lead + 1, mid, jnp.where(lane == lead + 2, low, ones)))


def row_targets(raw):
    wide = raw.astype(F32)
    high, mid, low = [t.astype(F32) for t in split3(wide * SCALE)]
    left = high + pltpu.roll(mid, D, 1)
    right = low + lane_aux(wide, True)
    return jnp.concatenate([left, right], axis=1).astype(BF16)


def row_sources(raw):
    wide = raw.astype(F32)
    left = wide + pltpu.roll(wide, D, 1)
    right = wide + lane_aux(wide, False)
    return jnp.concatenate([left, right], axis=1).astype(BF16)


def to_row(columns):
    ones = jnp.ones((8, 128), F32)
    return lax.dot_general(
        ones, columns, (((1,), (1,)), ((), ())), precision=HI, preferred_element_type=F32
    )[0:1]


def to_column(row):
    parts = []
    for start in range(0, row.shape[1], 128):
        piece = jnp.broadcast_to(row[:, start : start + 128], (128, 128))
        parts.append(piece.T)
    return jnp.concatenate(parts, axis=0) if len(parts) > 1 else parts[0]


def fold_lanes(tile):
    total = tile[:, 0:128]
    for start in range(128, tile.shape[1], 128):
        total = total + tile[:, start : start + 128]
    return total


def fold_rows(tile):
    return jnp.sum(tile.reshape(tile.shape[0] // 8, 8, tile.shape[1]), axis=0)


def tile_lanes(column, width):
    return jnp.concatenate([column] * (width // 128), axis=1)


def body(
    pts_in, rhs_in, near, skel_in, top_in, x_out, r_out,
    pts_a, pts_b, aux_a, aux_b, vals, taug, vb, acc, kq, kd, ke, ka, ku, kc, cbuf, moh,
    zsend, zin, skp, gg, gt, psend, pin, usend, uin, wsend, win, s_one, s_ty, s_tx, s_two,
    pt_s, pt_r, va_s, va_r, z_s, z_r, g_s, g_r, p_s, p_r, u_s, u_r, w_s, w_r, a_s, a_r, b_s, b_r,
):
    my_tx = lax.axis_index("tx")
    my_ty = lax.axis_index("ty")
    pts = (pts_a, pts_b)
    aux = (aux_a, aux_b)

    def tx_at(step):
        return lax.rem(my_tx + (step + N_TX), N_TX)

    def ty_at(step):
        return lax.rem(my_ty + (step + N_TY), N_TY)

    def send(src, dst, s_sem, r_sem, **where):
        copy = pltpu.make_async_remote_copy(
            src_ref=src, dst_ref=dst, send_sem=s_sem, recv_sem=r_sem,
            device_id=where, device_id_type=pl.DeviceIdType.MESH,
        )
        return copy

    barrier = pltpu.get_barrier_semaphore()
    for step in range(1, N_TX):
        pl.semaphore_signal(barrier, inc=1, device_id={"tx": tx_at(step)}, device_id_type=pl.DeviceIdType.MESH)
    for step in range(1, N_TY):
        pl.semaphore_signal(barrier, inc=1, device_id={"ty": ty_at(step)}, device_id_type=pl.DeviceIdType.MESH)
    for half in range(HALVES):
        vals[0, MINE + half] = rhs_in[half]
    for half in range(HALVES, 8):
        vals[0, MINE + half] = jnp.zeros((1, HALF), F32)
        vals[1, MINE + half] = jnp.zeros((1, HALF), F32)
    for half in range(HALVES):
        for wave in range(WAVES):
            start = half * HALF + wave * PART
            pts[wave][MINE + half] = pts_in[:, start : start + PART]

    remote_gaps = [1, -1, 2, -2]

    def point_copy(wave, leaf, number):
        gap = remote_gaps[number]
        source = 8 * (REACH if number < 2 else REACH + gap // 2) + 2 * leaf
        place = 8 * (gap + REACH) + 2 * leaf
        return send(
            pts[wave].at[pl.ds(source, 2)], pts[wave].at[pl.ds(place, 2)],
            pt_s.at[wave, number, leaf], pt_r.at[wave, number, leaf],
            tx=tx_at(-1 if gap > 0 else 1),
        )

    points_out = {}

    def send_points(wave):
        for leaf in range(LDEV):
            for number in range(2):
                copy = point_copy(wave, leaf, number)
                copy.start()
                points_out[wave, leaf, number] = copy

    def pass_on(wave, leaf):
        for number in range(2):
            points_out[wave, leaf, number].wait_recv()
            copy = point_copy(wave, leaf, number + 2)
            copy.start()
            points_out[wave, leaf, number + 2] = copy

    def points_here(wave):
        for leaf in range(LDEV):
            for number in range(4):
                copy = points_out[wave, leaf, number]
                if number >= 2:
                    copy.wait_recv()
                copy.wait_send()

    def send_values(it):
        copies = []
        for number, gap in enumerate(remote_gaps):
            place = 8 * (gap + REACH)
            copy = send(
                vals.at[it, pl.ds(MINE, 8)], vals.at[it, pl.ds(place, 8)],
                va_s.at[it, number], va_r.at[it, number], tx=tx_at(-gap),
            )
            copy.start()
            copies.append(copy)
        return copies

    def slot(leaf, number, half):
        named = near[leaf, number]
        live = named >= 0
        named = jnp.maximum(named, 0)
        place = lax.rem(lax.div(named, LDEV * N_TY) - my_tx + (N_TX + REACH), N_TX)
        other = lax.rem(named, LDEV)
        same = place == REACH
        itself = live & same & (other == leaf)
        use = live & jnp.logical_not(itself) & (place < GAPS)
        back = jnp.where((place < REACH) | (same & (other < leaf)), 1, 0)
        other_half = half + back - 2 * half * back
        index = jnp.where(use, 8 * place + 2 * other + other_half, MINE)
        return index, jnp.where(use, 1.0, 0.0), jnp.where(live, 1.0, 0.0) + jnp.where(itself, 1.0, 0.0)

    def split_quad(quad):
        return lax.div(quad, 2 * SLOTS), lax.rem(lax.div(quad, 2), SLOTS), lax.rem(quad, 2)

    def degree(leaf):
        total = 0.0
        for number in range(SLOTS):
            total = total + slot(leaf, number, 0)[2]
        return total

    sub = lax.broadcasted_iota(jnp.int32, (ROWS, 128), 0)
    lane = lax.broadcasted_iota(jnp.int32, (ROWS, 128), 1)

    def mark(quad, table):
        index, use, unused = slot(*split_quad(quad))
        return jnp.where((lane == quad) & (sub == index), use, table)

    table = lax.fori_loop(0, QUADS, mark, jnp.zeros((ROWS, 128), F32))
    for leaf in range(LDEV):
        table = jnp.where((lane == QUADS + leaf) & (sub == MINE + 2 * leaf + 1), degree(leaf), table)
    moh[...] = table
    cbuf[pl.ds(QUADS, 128 - QUADS)] = jnp.zeros((128 - QUADS, HALF), F32)

    def own_half(half):
        return jnp.concatenate([pts[wave][MINE + half] for wave in range(WAVES)], axis=1)

    def own_forms(half, carry):
        taug[half] = target_form(own_half(half))
        for wave in range(WAVES):
            aux[wave][MINE + half] = aux_rows(pts[wave][MINE + half], False).astype(BF16)
        return carry

    skp[pl.ds(D, 128 - D)] = jnp.zeros((128 - D, LDEV * SKEL), BF16)
    for leaf in range(LDEV):
        chosen = skel_in[leaf : leaf + 1]
        picked = jnp.zeros((D, SKEL), F32)
        for half in range(2):
            place = lax.broadcasted_iota(jnp.int32, (HALF, SKEL), 0) + half * HALF
            hot = jnp.where(place == chosen, 1.0, 0.0).astype(BF16)
            picked = picked + jnp.dot(own_half(2 * leaf + half), hot, preferred_element_type=F32)
        skp[0:D, leaf * SKEL : (leaf + 1) * SKEL] = picked.astype(BF16)
    wide_lane = lax.broadcasted_iota(jnp.int32, (1, LDEV * SKEL), 1)
    hot_rows = [jnp.where(wide_lane == top_in[t], 1.0, 0.0) for t in range(TSK)]
    hot = jnp.concatenate(hot_rows, axis=0).astype(BF16)
    mine_top = lax.dot_general(
        hot, skp[...], (((1,), (1,)), ((), ())), preferred_element_type=F32
    ).astype(BF16)
    gg[my_ty] = mine_top
    gt[my_tx] = mine_top

    def send_top():
        near_copies, far_copies = [], []
        for step in range(1, N_TY):
            copy = send(gg.at[my_ty], gg.at[my_ty], g_s.at[step], g_r.at[step], ty=ty_at(step))
            copy.start()
            near_copies.append(copy)
        for step in range(1, N_TX):
            copy = send(gt.at[my_tx], gt.at[my_tx], g_s.at[N_TY + step], g_r.at[N_TY + step], tx=tx_at(step))
            copy.start()
            far_copies.append(copy)
        return near_copies, far_copies

    lax.fori_loop(0, HALVES, own_forms, 0)

    def spread(it):
        def step(half, carry):
            vb[half] = to_column(vals[it, MINE + half])
            return carry
        lax.fori_loop(0, HALVES, step, 0)

    def skeleton_form(leaf):
        coords = skp[0:D, leaf * SKEL : (leaf + 1) * SKEL]
        return source_form(coords, aux_rows(coords, False).astype(BF16))

    def up_leaf(it):
        parts = []
        for leaf in range(LDEV):
            if it == 0:
                form = skeleton_form(leaf)
            total = jnp.zeros((8, SKEL), F32)
            for half in range(2):
                row = 2 * leaf + half
                if it == 0:
                    ka[row] = jnp.exp2(jnp.dot(taug[row], form, preferred_element_type=F32))
                total = total + fold_rows(ka[row] * tile_lanes(vb[row], SKEL))
            parts.append(jnp.sum(total, axis=0, keepdims=True))
        return jnp.concatenate(parts, axis=1) * A_LEAF

    narrow = lax.broadcasted_iota(jnp.int32, (1, 128), 1)

    def up_group(it, weights):
        partial = to_row(fold_lanes(ku[...] * weights)) * E_GROUP
        for part in range(N_TY):
            tile = partial[:, 128 * (part // 4) : 128 * (part // 4) + 128]
            shift = (128 - TSK * (part % 4)) % 128
            if shift:
                tile = pltpu.roll(tile, shift, 1)
            psend[it, part] = jnp.where(narrow < TSK, tile, 0.0)
        out = []
        pin[it, my_ty] = psend[it, my_ty]
        for step in range(1, N_TY):
            copy = send(psend.at[it, ty_at(step)], pin.at[it, my_ty], p_s.at[it, step], p_r.at[it, step], ty=ty_at(step))
            copy.start()
            out.append(copy)
        return out

    def over_top(it, waiting):
        for copy in waiting:
            copy.wait()
        usend[it] = jnp.sum(pin[it], axis=0)
        uin[it, my_tx] = usend[it]
        out = []
        for step in range(1, N_TX):
            copy = send(usend.at[it], uin.at[it, my_tx], u_s.at[it, step], u_r.at[it, step], tx=tx_at(step))
            copy.start()
            out.append(copy)
        return out

    def across(it, waiting):
        for copy in waiting:
            copy.wait()
        tiles = []
        for tile in range(4):
            total = uin[it, 4 * tile]
            for k in range(1, 4):
                total = total + pltpu.roll(uin[it, 4 * tile + k], TSK * k, 1)
            tiles.append(total)
        upper = jnp.concatenate(tiles, axis=1)
        wsend[it] = to_row(fold_lanes(kc[...] * upper)) * E_TOP
        win[it, my_ty] = wsend[it]
        out = []
        for step in range(1, N_TY):
            copy = send(wsend.at[it], win.at[it, my_ty], w_s.at[it, step], w_r.at[it, step], ty=ty_at(step))
            copy.start()
            out.append(copy)
        return out

    def down(it, waiting):
        for copy in waiting:
            copy.wait()
        middle = to_column(jnp.sum(win[it], axis=0))
        lower = fold_rows(ku[...] * tile_lanes(middle, LDEV * SKEL))
        lower = jnp.sum(lower, axis=0, keepdims=True) * (E_GROUP * A_LEAF * FAR * SLOTS)
        for leaf in range(LDEV):
            weights = lower[:, leaf * SKEL : (leaf + 1) * SKEL]
            for half in range(2):
                row = 2 * leaf + half
                acc[row] += fold_lanes(ka[row] * weights)

    def stretch(it, store, row, form, values, fresh, first):
        width = values.shape[1]
        total = jnp.zeros((8, width - first), F32)
        for start in range(0, HALF, CHUNK):
            rows = pl.ds(start, CHUNK)
            if it == 0:
                tile = jnp.exp2(jnp.dot(taug[row, rows], form, preferred_element_type=F32))
                store[rows] = tile
            else:
                tile = store[rows]
            part = fold_lanes(tile * values)
            if fresh:
                acc[row, rows] = part
            else:
                acc[row, rows] += part
            if first < width:
                total = total + fold_rows(tile[:, first:] * tile_lanes(vb[row, rows], width - first))
        return jnp.sum(total, axis=0, keepdims=True) if first < width else None

    def form_of(wave, index):
        return source_form(pts[wave][index], aux[wave][index])

    def diagonal(it):
        def step(leaf, carry):
            weight = degree(leaf)
            low, high = 2 * leaf, 2 * leaf + 1
            form = None
            if it == 0:
                form = jnp.concatenate(
                    [form_of(wave, MINE + half) for half in (low, high) for wave in range(WAVES)], axis=1
                )
            values = jnp.concatenate([vals[it, MINE + low], vals[it, MINE + high]], axis=1) * weight
            cbuf[pl.ds(QUADS + leaf, 1)] = stretch(it, kd.at[leaf], low, form, values, True, HALF)
            if it == 0:
                form = form[:, HALF:]
            stretch(it, ke.at[leaf], high, form, values[:, HALF:], True, HALF)
            return carry
        lax.fori_loop(0, LDEV, step, 0)

    def slots(it, wave, start, stop):
        def step(row, carry):
            leaf, half = lax.div(row, 2), lax.rem(row, 2)
            forms, values = [], []
            for number in range(SLOTS):
                index, use, unused = slot(leaf, number, half)
                if it == 0:
                    forms.append(form_of(wave, index))
                values.append(vals[it, index][:, wave * PART : (wave + 1) * PART] * use)
            form = jnp.concatenate(forms, axis=1) if it == 0 else None
            total = stretch(it, kq.at[wave, row], row, form, jnp.concatenate(values, axis=1), False, 0)
            for number in range(SLOTS):
                place = 2 * SLOTS * leaf + 2 * number + half
                cbuf[pl.ds(place, 1), wave * PART : (wave + 1) * PART] = total[:, number * PART : (number + 1) * PART]
            return carry
        lax.fori_loop(start, stop, step, 0)

    def send_back(it):
        parts = jnp.dot(moh[...], cbuf[...], precision=HI, preferred_element_type=F32)
        for place in range(GAPS):
            zsend[it, place] = parts[8 * place : 8 * place + 8]
        out = []
        for number, gap in enumerate(remote_gaps):
            copy = send(
                zsend.at[it, gap + REACH], zin.at[it, REACH - gap], z_s.at[it, number], z_r.at[it, number], tx=tx_at(gap)
            )
            copy.start()
            out.append(copy)
        return out

    def near_rows(it):
        rows = [to_row(acc[half]) for half in range(HALVES)]
        own = jnp.concatenate(rows + [jnp.zeros((8 - HALVES, HALF), F32)], axis=0)
        given = jnp.zeros((1, 1), F32)
        for place in range(GAPS):
            if place != REACH:
                theirs = jnp.concatenate([vals[it, 8 * place + half] for half in range(8)], axis=0)
                given = given + dot(zsend[it, place], theirs)
        return (own + zsend[it, REACH]) * (1.0 / SLOTS), given * (1.0 / SLOTS)

    def near_back(it, waiting):
        for copy in waiting:
            copy.wait()
        total = zin[it, 0]
        for place in range(1, GAPS):
            if place != REACH:
                total = total + zin[it, place]
        return total * (1.0 / SLOTS)

    def own_rows(it):
        return jnp.concatenate([vals[it, MINE + half] for half in range(8)], axis=0)

    def pack(*sums):
        row = jnp.zeros((1, 128), F32)
        for number, value in enumerate(sums):
            row = jnp.where(narrow == number, value, row)
        return row

    def sum_first(number, row):
        s_one[number] = row
        s_ty[number, my_ty] = row
        out = []
        for step in range(1, N_TY):
            copy = send(s_one.at[number], s_ty.at[number, my_ty], a_s.at[number, step], a_r.at[number, step], ty=ty_at(step))
            copy.start()
            out.append(copy)
        return out

    def sum_second(number, waiting):
        for copy in waiting:
            copy.wait()
        row = jnp.sum(s_ty[number], axis=0)
        s_two[number] = row
        s_tx[number, my_tx] = row
        out = []
        for step in range(1, N_TX):
            copy = send(s_two.at[number], s_tx.at[number, my_tx], b_s.at[number, step], b_r.at[number, step], tx=tx_at(step))
            copy.start()
            out.append(copy)
        return out

    def sum_last(number, waiting, count):
        for copy in waiting:
            copy.wait()
        row = jnp.sum(s_tx[number], axis=0)
        return [jnp.sum(jnp.where(narrow == k, row, 0.0), axis=1, keepdims=True) for k in range(count)]

    def dot(one, two):
        return jnp.sum(jnp.sum(one * two, axis=0, keepdims=True), axis=1, keepdims=True)

    lax.fori_loop(0, HALVES, own_forms, 0)
    spread(0)
    weights = up_leaf(0)
    start = own_rows(0)
    pl.semaphore_wait(barrier, N_TX - 1 + N_TY - 1)

    group_near, group_far = send_top()
    values_out = send_values(0)
    send_points(0)
    diagonal(0)
    for copy in group_near:
        copy.wait()
    group_targets = row_targets(gg[...].reshape(GSKEL, 128))
    for leaf in range(LDEV):
        ku[:, leaf * SKEL : (leaf + 1) * SKEL] = jnp.exp2(
            jnp.dot(group_targets, skeleton_form(leaf), preferred_element_type=F32)
        )
    flight = up_group(0, weights)
    for leaf in range(LDEV):
        pass_on(0, leaf)
    send_points(1)
    for copy in group_far:
        copy.wait()
    group_sources = row_sources(gt[...].reshape(N_TX * TSK, 128))
    kc[...] = jnp.exp2(
        lax.dot_general(group_targets, group_sources, (((1,), (1,)), ((), ())), preferred_element_type=F32)
    )
    flight = over_top(0, flight)

    def remote_aux(wave):
        for place in range(GAPS):
            if place != REACH:
                def one(half, carry, place=place):
                    aux[wave][8 * place + half] = aux_rows(pts[wave][8 * place + half], False).astype(BF16)
                    return carry
                lax.fori_loop(0, HALVES, one, 0)

    points_here(0)
    remote_aux(0)
    for copy in values_out:
        copy.wait()
    slots(0, 0, 0, 2)
    pass_on(1, 0)
    flight = across(0, flight)
    slots(0, 0, 2, 4)
    pass_on(1, 1)
    slots(0, 0, 4, 6)
    pass_on(1, 2)
    down(0, flight)
    points_here(1)
    remote_aux(1)
    slots(0, 1, 0, HALVES)
    back = send_back(0)
    partial, given = near_rows(0)
    local = start + partial
    sums = sum_first(0, pack(dot(start, start), dot(start, local) + given))
    first = local + near_back(0, back)
    for half in range(HALVES):
        vals[1, MINE + half] = first[half : half + 1]

    values_out = send_values(1)
    spread(1)
    flight = up_group(1, up_leaf(1))
    sums = sum_second(0, sums)
    diagonal(1)
    flight = over_top(1, flight)
    norm, curve = sum_last(0, sums, 2)
    alpha = norm / curve
    left = start - alpha * first
    sums = sum_first(1, pack(dot(left, left)))
    for copy in values_out:
        copy.wait()
    slots(1, 0, 0, HALVES)
    sums = sum_second(1, sums)
    flight = across(1, flight)
    slots(1, 1, 0, HALVES)
    back = send_back(1)
    down(1, flight)
    partial, given = near_rows(1)
    second = first + partial + near_back(1, back)
    (norm_next,) = sum_last(1, sums, 1)
    beta = norm_next / norm
    direction = left + beta * start
    image = (1.0 + beta) * first - alpha * second
    sums = sum_first(2, pack(dot(direction, image)))
    sums = sum_second(2, sums)
    (curve,) = sum_last(2, sums, 1)
    step = norm_next / curve
    x_out[...] = (alpha * start + step * direction)[0:HALVES]
    r_out[...] = (left - step * image)[0:HALVES]


def on_device(points, right_side, near_list, leaf_skeleton, top_index):
    vmem = pl.BlockSpec(memory_space=pltpu.VMEM)
    smem = pl.BlockSpec(memory_space=pltpu.SMEM)
    dma = pltpu.SemaphoreType.DMA
    out = jax.ShapeDtypeStruct((HALVES, HALF), F32)
    solution_field, residual = pl.pallas_call(
        body,
        out_shape=(out, out),
        in_specs=[vmem, vmem, smem, vmem, smem],
        out_specs=(vmem, vmem),
        scratch_shapes=[
            pltpu.VMEM((ROWS, D, PART), BF16),
            pltpu.VMEM((ROWS, D, PART), BF16),
            pltpu.VMEM((ROWS, 16, PART), BF16),
            pltpu.VMEM((ROWS, 16, PART), BF16),
            pltpu.VMEM((2, ROWS, 1, HALF), F32),
            pltpu.VMEM((HALVES, HALF, 256), BF16),
            pltpu.VMEM((HALVES, HALF, 128), F32),
            pltpu.VMEM((HALVES, HALF, 128), F32),
            pltpu.VMEM((WAVES, HALVES, HALF, WIDE), F32),
            pltpu.VMEM((LDEV, HALF, LEAF), F32),
            pltpu.VMEM((LDEV, HALF, HALF), F32),
            pltpu.VMEM((HALVES, HALF, SKEL), F32),
            pltpu.VMEM((GSKEL, LDEV * SKEL), F32),
            pltpu.VMEM((GSKEL, N_TX * TSK), F32),
            pltpu.VMEM((128, HALF), F32),
            pltpu.VMEM((ROWS, 128), F32),
            pltpu.VMEM((2, GAPS, 8, HALF), F32),
            pltpu.VMEM((2, GAPS, 8, HALF), F32),
            pltpu.VMEM((128, LDEV * SKEL), BF16),
            pltpu.VMEM((N_TY, TSK, 128), BF16),
            pltpu.VMEM((N_TX, TSK, 128), BF16),
            pltpu.VMEM((2, N_TY, 1, 128), F32),
            pltpu.VMEM((2, N_TY, 1, 128), F32),
            pltpu.VMEM((2, 1, 128), F32),
            pltpu.VMEM((2, N_TX, 1, 128), F32),
            pltpu.VMEM((2, 1, GSKEL), F32),
            pltpu.VMEM((2, N_TY, 1, GSKEL), F32),
            pltpu.VMEM((3, 1, 128), F32),
            pltpu.VMEM((3, N_TY, 1, 128), F32),
            pltpu.VMEM((3, N_TX, 1, 128), F32),
            pltpu.VMEM((3, 1, 128), F32),
            dma((WAVES, 4, LDEV)), dma((WAVES, 4, LDEV)),
            dma((2, 4)), dma((2, 4)),
            dma((2, 4)), dma((2, 4)),
            dma((N_TX + N_TY,)), dma((N_TX + N_TY,)),
            dma((2, N_TY)), dma((2, N_TY)),
            dma((2, N_TX)), dma((2, N_TX)),
            dma((2, N_TY)), dma((2, N_TY)),
            dma((3, N_TY)), dma((3, N_TY)),
            dma((3, N_TX)), dma((3, N_TX)),
        ],
        compiler_params=pltpu.CompilerParams(
            collective_id=0, has_side_effects=True, vmem_limit_bytes=64 * 1024 * 1024 - 512 * 1024
        ),
        name="ridge_cg",
    )(points, right_side.reshape(HALVES, 1, HALF), near_list, leaf_skeleton, top_index)
    return solution_field.reshape(-1), residual.reshape(-1)


def solution(mesh):
    placed = (
        P(None, ("tx", "ty")),
        P(("tx", "ty")),
        P(("tx", "ty"), None),
        P(("tx", "ty"), None),
        P(("tx", "ty")),
    )
    return jax.shard_map(
        on_device,
        mesh=mesh,
        in_specs=placed,
        out_specs=(P(("tx", "ty")), P(("tx", "ty"))),
        check_vma=False,
    )
```

```python
import functools
import math

import jax
import jax.numpy as jnp
from jax import lax
from jax.experimental import pallas as pl
from jax.experimental.pallas import tpu as pltpu
from jax.sharding import PartitionSpec as P

F32 = jnp.float32
BF16 = jnp.bfloat16
HI = lax.Precision.HIGHEST

D = 64
LEAF = 1024
HALF = 512
SKEL = 256
LDEV = 3
HALVES = LDEV * 2
SLOTS = 6
TSK = 32
N_TX = 16
N_TY = 8
GSKEL = TSK * N_TY
REACH = 2
GAPS = 2 * REACH + 1
ROWS = 8 * GAPS
MINE = 8 * REACH
QUADS = 8 * HALVES
CHUNK = 128
PARTS = (256, 128, 128)
STARTS = (0, 256, 384)
WAVES = len(PARTS)

SCALE = 2.0 * math.log2(math.e) / 20.0
A_LEAF = 0.25
E_GROUP = LEAF / (LDEV * N_TY * SKEL)
E_TOP = LEAF / (N_TX * GSKEL)
FAR = 32.0


def split3(x):
    high = x.astype(BF16)
    rest = x - high.astype(F32)
    mid = rest.astype(BF16)
    low = (rest - mid.astype(F32)).astype(BF16)
    return high, mid, low


def aux_rows(coords, first):
    wide = coords.astype(F32)
    norm = (-0.5 * SCALE) * jnp.sum(wide * wide, axis=0, keepdims=True)
    high, mid, low = [t.astype(F32) for t in split3(norm)]
    row = lax.broadcasted_iota(jnp.int32, (16, coords.shape[1]), 0)
    lead = 0 if first else 3
    ones = jnp.where((row >= 3 - lead) & (row < 6 - lead), 1.0, 0.0)
    parts = jnp.where(row == lead, high, jnp.where(row == lead + 1, mid, jnp.where(row == lead + 2, low, ones)))
    return parts


def source_form(coords, aux):
    pad = jnp.zeros((48, coords.shape[1]), BF16)
    return jnp.concatenate([coords, coords, coords, aux, pad], axis=0)


def target_form(coords):
    high, mid, low = split3(coords.astype(F32) * SCALE)
    pad = jnp.zeros((48, coords.shape[1]), F32)
    aux = aux_rows(coords, True)
    stack = jnp.concatenate([high.astype(F32), mid.astype(F32), low.astype(F32), aux, pad], axis=0)
    return stack.T.astype(BF16)


def lane_aux(wide, first):
    norm = (-0.5 * SCALE) * jnp.sum(wide * wide, axis=1, keepdims=True)
    high, mid, low = [t.astype(F32) for t in split3(norm)]
    lane = lax.broadcasted_iota(jnp.int32, wide.shape, 1) - D
    lead = 0 if first else 3
    ones = jnp.where((lane >= 3 - lead) & (lane < 6 - lead), 1.0, 0.0)
    return jnp.where(lane == lead, high, jnp.where(lane == lead + 1, mid, jnp.where(lane == lead + 2, low, ones)))


def row_targets(raw):
    wide = raw.astype(F32)
    high, mid, low = [t.astype(F32) for t in split3(wide * SCALE)]
    left = high + pltpu.roll(mid, D, 1)
    right = low + lane_aux(wide, True)
    return jnp.concatenate([left, right], axis=1).astype(BF16)


def row_sources(raw):
    wide = raw.astype(F32)
    left = wide + pltpu.roll(wide, D, 1)
    right = wide + lane_aux(wide, False)
    return jnp.concatenate([left, right], axis=1).astype(BF16)


def to_row(columns):
    ones = jnp.ones((8, 128), F32)
    return lax.dot_general(
        ones, columns, (((1,), (1,)), ((), ())), precision=HI, preferred_element_type=F32
    )[0:1]


def to_column(row):
    parts = []
    for start in range(0, row.shape[1], 128):
        piece = jnp.broadcast_to(row[:, start : start + 128], (128, 128))
        parts.append(piece.T)
    return jnp.concatenate(parts, axis=0) if len(parts) > 1 else parts[0]


def fold_lanes(tile):
    total = tile[:, 0:128]
    for start in range(128, tile.shape[1], 128):
        total = total + tile[:, start : start + 128]
    return total


def fold_rows(tile):
    return jnp.sum(tile.reshape(tile.shape[0] // 8, 8, tile.shape[1]), axis=0)


def tile_lanes(column, width):
    return jnp.concatenate([column] * (width // 128), axis=1)


def body(
    pts_hbm, rhs_hbm, near_hbm, skel_hbm, top_hbm, x_out, r_out,
    rhs_in, near, skel_in, top_in, in_s,
    pts_a, pts_b, pts_c, aux_a, aux_b, aux_c, vals, taug, vb, acc, kq_a, kq_b, kq_c, kd, ke, ka, ku, kc, cbuf, moh,
    zsend, zin, skp, gg, gt, psend, pin, usend, uin, wsend, win, s_one, s_ty, s_tx, s_two,
    pt_s, pt_r, va_s, va_r, z_s, z_r, g_s, g_r, p_s, p_r, u_s, u_r, w_s, w_r, a_s, a_r, b_s, b_r,
):
    my_tx = lax.axis_index("tx")
    my_ty = lax.axis_index("ty")
    pts = (pts_a, pts_b, pts_c)
    aux = (aux_a, aux_b, aux_c)
    kq = (kq_a, kq_b, kq_c)

    def tx_at(step):
        return lax.rem(my_tx + (step + N_TX), N_TX)

    def ty_at(step):
        return lax.rem(my_ty + (step + N_TY), N_TY)

    def send(src, dst, s_sem, r_sem, **where):
        copy = pltpu.make_async_remote_copy(
            src_ref=src, dst_ref=dst, send_sem=s_sem, recv_sem=r_sem,
            device_id=where, device_id_type=pl.DeviceIdType.MESH,
        )
        return copy

    def settle(space, sem):
        pltpu.make_async_copy(space, space, sem).wait()

    def settle_both(space, pair):
        settle(space, pair[0])
        settle(space, pair[1])

    barrier = pltpu.get_barrier_semaphore()
    for step in range(1, N_TX):
        pl.semaphore_signal(barrier, inc=1, device_id={"tx": tx_at(step)}, device_id_type=pl.DeviceIdType.MESH)
    for step in range(1, N_TY):
        pl.semaphore_signal(barrier, inc=1, device_id={"ty": ty_at(step)}, device_id_type=pl.DeviceIdType.MESH)
    loads = [
        pltpu.make_async_copy(near_hbm, near, in_s.at[0]),
        pltpu.make_async_copy(top_hbm, top_in, in_s.at[1]),
        pltpu.make_async_copy(skel_hbm, skel_in, in_s.at[2]),
        pltpu.make_async_copy(rhs_hbm, rhs_in, in_s.at[3]),
    ]
    for copy in loads:
        copy.start()
    for wave in range(WAVES):
        for half in range(HALVES):
            start = half * HALF + STARTS[wave]
            pltpu.make_async_copy(
                pts_hbm.at[:, pl.ds(start, PARTS[wave])], pts[wave].at[MINE + half], in_s.at[4 + wave]
            ).start()
    for half in range(HALVES, 8):
        vals[0, MINE + half] = jnp.zeros((1, HALF), F32)
        vals[1, MINE + half] = jnp.zeros((1, HALF), F32)
    for copy in loads:
        copy.wait()
    for wave in range(WAVES):
        settle(pts[wave].at[pl.ds(MINE, HALVES)], in_s.at[4 + wave])
    for half in range(HALVES):
        vals[0, MINE + half] = rhs_in[pl.ds(half * HALF, HALF)].reshape(1, HALF)

    remote_gaps = [1, -1, 2, -2]

    def point_copy(wave, leaf, number):
        gap = remote_gaps[number]
        source = 8 * (REACH if number < 2 else REACH + gap // 2) + 2 * leaf
        place = 8 * (gap + REACH) + 2 * leaf
        return send(
            pts[wave].at[pl.ds(source, 2)], pts[wave].at[pl.ds(place, 2)],
            pt_s.at[wave], pt_r.at[wave, number, leaf] if number < 2 else pt_r.at[wave, 2, 0],
            tx=tx_at(-1 if gap > 0 else 1),
        )

    points_out = {}

    def send_points(wave):
        for leaf in range(LDEV):
            for number in range(2):
                copy = point_copy(wave, leaf, number)
                copy.start()
                points_out[wave, leaf, number] = copy

    def pass_on(wave, leaf):
        for number in range(2):
            points_out[wave, leaf, number].wait_recv()
            point_copy(wave, leaf, number + 2).start()

    def points_here(wave):
        settle(pts[wave].at[pl.ds(0, 2 * HALVES)], pt_r.at[wave, 2, 0])

    def points_gone(wave):
        settle(pts[wave].at[pl.ds(0, 4 * HALVES)], pt_s.at[wave])

    def send_values(it):
        for gap in remote_gaps:
            place = 8 * (gap + REACH)
            send(
                vals.at[it, pl.ds(MINE, 8)], vals.at[it, pl.ds(place, 8)], va_s.at[it], va_r.at[it], tx=tx_at(-gap)
            ).start()

    def values_here(it):
        four = vals.at[it, pl.ds(0, 8 * (GAPS - 1))]
        settle_both(four, (va_s.at[it], va_r.at[it]))

    def slot(leaf, number, half):
        named = near[leaf, number]
        live = named >= 0
        named = jnp.maximum(named, 0)
        place = lax.rem(lax.div(named, LDEV * N_TY) - my_tx + (N_TX + REACH), N_TX)
        other = lax.rem(named, LDEV)
        same = place == REACH
        itself = live & same & (other == leaf)
        use = live & jnp.logical_not(itself) & (place < GAPS)
        back = jnp.where((place < REACH) | (same & (other < leaf)), 1, 0)
        other_half = half + back - 2 * half * back
        index = jnp.where(use, 8 * place + 2 * other + other_half, MINE)
        return index, jnp.where(use, 1.0, 0.0), jnp.where(live, 1.0, 0.0) + jnp.where(itself, 1.0, 0.0)

    def degree(leaf):
        total = 0.0
        for number in range(SLOTS):
            total = total + slot(leaf, number, 0)[2]
        return total

    sub = lax.broadcasted_iota(jnp.int32, (ROWS, 128), 0)
    lane = lax.broadcasted_iota(jnp.int32, (ROWS, 128), 1)

    def mark(row, table):
        for number in range(SLOTS):
            index, use, unused = slot(lax.div(row, 2), number, lax.rem(row, 2))
            table = jnp.where((lane == 8 * row + number) & (sub == index), use, table)
        return table

    table = lax.fori_loop(0, HALVES, mark, jnp.zeros((ROWS, 128), F32))
    for leaf in range(LDEV):
        table = jnp.where((lane == QUADS + leaf) & (sub == MINE + 2 * leaf + 1), degree(leaf), table)
    moh[...] = table
    cbuf[pl.ds(QUADS, 128 - QUADS)] = jnp.zeros((128 - QUADS, HALF), F32)

    def own_half(half):
        return jnp.concatenate([pts[wave][MINE + half] for wave in range(WAVES)], axis=1)

    def own_forms(half, carry):
        taug[half] = target_form(own_half(half))
        for wave in range(WAVES):
            aux[wave][MINE + half] = aux_rows(pts[wave][MINE + half], False).astype(BF16)
        return carry

    skp[pl.ds(D, 128 - D)] = jnp.zeros((128 - D, LDEV * SKEL), BF16)
    for leaf in range(LDEV):
        chosen = skel_in[leaf : leaf + 1]
        picked = jnp.zeros((D, SKEL), F32)
        for half in range(2):
            place = lax.broadcasted_iota(jnp.int32, (HALF, SKEL), 0) + half * HALF
            hot = jnp.where(place == chosen, 1.0, 0.0).astype(BF16)
            picked = picked + jnp.dot(own_half(2 * leaf + half), hot, preferred_element_type=F32)
        skp[0:D, leaf * SKEL : (leaf + 1) * SKEL] = picked.astype(BF16)
    wide_lane = lax.broadcasted_iota(jnp.int32, (1, LDEV * SKEL), 1)
    hot_rows = [jnp.where(wide_lane == top_in[t], 1.0, 0.0) for t in range(TSK)]
    hot = jnp.concatenate(hot_rows, axis=0).astype(BF16)
    mine_top = lax.dot_general(
        hot, skp[...], (((1,), (1,)), ((), ())), preferred_element_type=F32
    ).astype(BF16)
    gg[my_ty] = mine_top
    gt[my_tx] = mine_top

    def send_top_near():
        for step in range(1, N_TY):
            send(gg.at[my_ty], gg.at[my_ty], g_s.at[0], g_r.at[0], ty=ty_at(step)).start()

    def send_top_far():
        for step in range(1, N_TX):
            send(gt.at[my_tx], gt.at[my_tx], g_s.at[1], g_r.at[1], tx=tx_at(step)).start()

    def spread(it):
        def step(half, carry):
            vb[half] = to_column(vals[it, MINE + half])
            return carry
        lax.fori_loop(0, HALVES, step, 0)

    def skeleton_form(leaf):
        coords = skp[0:D, leaf * SKEL : (leaf + 1) * SKEL]
        return source_form(coords, aux_rows(coords, False).astype(BF16))

    def up_leaf(it):
        parts = []
        for leaf in range(LDEV):
            if it == 0:
                form = skeleton_form(leaf)
            total = jnp.zeros((8, SKEL), F32)
            for half in range(2):
                row = 2 * leaf + half
                if it == 0:
                    ka[row] = jnp.exp2(jnp.dot(taug[row], form, preferred_element_type=F32))
                total = total + fold_rows(ka[row] * tile_lanes(vb[row], SKEL))
            parts.append(jnp.sum(total, axis=0, keepdims=True))
        return jnp.concatenate(parts, axis=1) * A_LEAF

    narrow = lax.broadcasted_iota(jnp.int32, (1, 128), 1)

    def up_group(it, weights):
        partial = to_row(fold_lanes(ku[...] * weights)) * E_GROUP
        for part in range(N_TY):
            tile = partial[:, 128 * (part // 4) : 128 * (part // 4) + 128]
            shift = (128 - TSK * (part % 4)) % 128
            if shift:
                tile = pltpu.roll(tile, shift, 1)
            psend[it, part] = jnp.where(narrow < TSK, tile, 0.0)
        pin[it, my_ty] = psend[it, my_ty]
        for step in range(1, N_TY):
            send(psend.at[it, ty_at(step)], pin.at[it, my_ty], p_s.at[it], p_r.at[it], ty=ty_at(step)).start()

    def over_top(it):
        settle_both(pin.at[it, pl.ds(0, N_TY - 1)], (p_s.at[it], p_r.at[it]))
        usend[it] = jnp.sum(pin[it], axis=0)
        uin[it, my_tx] = usend[it]
        for step in range(1, N_TX):
            send(usend.at[it], uin.at[it, my_tx], u_s.at[it], u_r.at[it], tx=tx_at(step)).start()

    def across(it):
        settle_both(uin.at[it, pl.ds(0, N_TX - 1)], (u_s.at[it], u_r.at[it]))
        tiles = []
        for tile in range(4):
            total = uin[it, 4 * tile]
            for k in range(1, 4):
                total = total + pltpu.roll(uin[it, 4 * tile + k], TSK * k, 1)
            tiles.append(total)
        upper = jnp.concatenate(tiles, axis=1)
        wsend[it] = to_row(fold_lanes(kc[...] * upper)) * E_TOP
        win[it, my_ty] = wsend[it]
        for step in range(1, N_TY):
            send(wsend.at[it], win.at[it, my_ty], w_s.at[it], w_r.at[it], ty=ty_at(step)).start()

    def down(it):
        settle_both(win.at[it, pl.ds(0, N_TY - 1)], (w_s.at[it], w_r.at[it]))
        middle = to_column(jnp.sum(win[it], axis=0))
        lower = fold_rows(ku[...] * tile_lanes(middle, LDEV * SKEL))
        lower = jnp.sum(lower, axis=0, keepdims=True) * (E_GROUP * A_LEAF * FAR * SLOTS)
        for leaf in range(LDEV):
            weights = lower[:, leaf * SKEL : (leaf + 1) * SKEL]
            for half in range(2):
                row = 2 * leaf + half
                acc[row] += fold_lanes(ka[row] * weights)

    def stretch(it, store, row, form, values, fresh, first):
        width = values.shape[1]
        total = jnp.zeros((8, width - first), F32)
        for start in range(0, HALF, CHUNK):
            rows = pl.ds(start, CHUNK)
            if it == 0:
                tile = jnp.exp2(jnp.dot(taug[row, rows], form, preferred_element_type=F32))
                store[rows] = tile
            else:
                tile = store[rows]
            part = fold_lanes(tile * values)
            if fresh:
                acc[row, rows] = part
            else:
                acc[row, rows] += part
            if first < width:
                total = total + fold_rows(tile[:, first:] * tile_lanes(vb[row, rows], width - first))
        return jnp.sum(total, axis=0, keepdims=True) if first < width else None

    def form_of(wave, index):
        return source_form(pts[wave][index], aux[wave][index])

    def diagonal(it):
        def step(leaf, carry):
            weight = degree(leaf)
            low, high = 2 * leaf, 2 * leaf + 1
            form = None
            if it == 0:
                form = jnp.concatenate(
                    [form_of(wave, MINE + half) for half in (low, high) for wave in range(WAVES)], axis=1
                )
            values = jnp.concatenate([vals[it, MINE + low], vals[it, MINE + high]], axis=1) * weight
            cbuf[pl.ds(QUADS + leaf, 1)] = stretch(it, kd.at[leaf], low, form, values, True, HALF)
            if it == 0:
                form = form[:, HALF:]
            stretch(it, ke.at[leaf], high, form, values[:, HALF:], True, HALF)
            return carry
        lax.fori_loop(0, LDEV, step, 0)

    def slots(it, wave, start, stop):
        part = PARTS[wave]

        def step(row, carry):
            leaf, half = lax.div(row, 2), lax.rem(row, 2)
            forms, values = [], []
            for number in range(SLOTS):
                index, use, unused = slot(leaf, number, half)
                if it == 0:
                    forms.append(form_of(wave, index))
                values.append(vals[it, index][:, STARTS[wave] : STARTS[wave] + PARTS[wave]] * use)
            form = jnp.concatenate(forms, axis=1) if it == 0 else None
            total = stretch(it, kq[wave].at[row], row, form, jnp.concatenate(values, axis=1), False, 0)
            rows = [total[:, number * part : (number + 1) * part] for number in range(SLOTS)]
            rows.append(jnp.zeros((8 - SLOTS, part), F32))
            cbuf[pl.ds(pl.multiple_of(8 * row, 8), 8), STARTS[wave] : STARTS[wave] + part] = jnp.concatenate(rows, axis=0)
            return carry
        lax.fori_loop(start, stop, step, 0)

    def send_back(it):
        parts = jnp.dot(moh[...], cbuf[...], precision=HI, preferred_element_type=F32)
        for place in range(GAPS):
            zsend[it, place] = parts[8 * place : 8 * place + 8]
        for gap in remote_gaps:
            send(zsend.at[it, gap + REACH], zin.at[it, REACH - gap], z_s.at[it], z_r.at[it], tx=tx_at(gap)).start()

    def near_rows(it):
        rows = [to_row(acc[half]) for half in range(HALVES)]
        own = jnp.concatenate(rows + [jnp.zeros((8 - HALVES, HALF), F32)], axis=0)
        return (own + zsend[it, REACH]) * (1.0 / SLOTS)

    def near_back(it):
        settle_both(zin.at[it, pl.ds(0, GAPS - 1)], (z_s.at[it], z_r.at[it]))
        total = zin[it, 0]
        for place in range(1, GAPS):
            if place != REACH:
                total = total + zin[it, place]
        return total * (1.0 / SLOTS)

    def own_rows(it):
        return jnp.concatenate([vals[it, MINE + half] for half in range(8)], axis=0)

    def pack(*sums):
        row = jnp.zeros((1, 128), F32)
        for number, value in enumerate(sums):
            row = jnp.where(narrow == number, value, row)
        return row

    def sum_first(number, row):
        s_one[number] = row
        s_ty[number, my_ty] = row
        for step in range(1, N_TY):
            send(s_one.at[number], s_ty.at[number, my_ty], a_s.at[number], a_r.at[number], ty=ty_at(step)).start()

    def sum_second(number):
        settle_both(s_ty.at[number, pl.ds(0, N_TY - 1)], (a_s.at[number], a_r.at[number]))
        row = jnp.sum(s_ty[number], axis=0)
        s_two[number] = row
        s_tx[number, my_tx] = row
        for step in range(1, N_TX):
            send(s_two.at[number], s_tx.at[number, my_tx], b_s.at[number], b_r.at[number], tx=tx_at(step)).start()

    def sum_last(number, count):
        settle_both(s_tx.at[number, pl.ds(0, N_TX - 1)], (b_s.at[number], b_r.at[number]))
        row = jnp.sum(s_tx[number], axis=0)
        return [jnp.sum(jnp.where(narrow == k, row, 0.0), axis=1, keepdims=True) for k in range(count)]

    def dot(one, two):
        return jnp.sum(jnp.sum(one * two, axis=0, keepdims=True), axis=1, keepdims=True)

    def remote_aux(wave):
        for place in range(GAPS):
            if place != REACH:
                def one(half, carry, place=place):
                    aux[wave][8 * place + half] = aux_rows(pts[wave][8 * place + half], False).astype(BF16)
                    return carry
                lax.fori_loop(0, HALVES, one, 0)

    lax.fori_loop(0, HALVES, own_forms, 0)
    spread(0)
    start = own_rows(0)
    pl.semaphore_wait(barrier, N_TX - 1 + N_TY - 1)

    send_points(0)
    send_top_near()
    send_points(1)
    send_top_far()
    send_values(0)
    weights = up_leaf(0)
    settle_both(gg.at[pl.ds(0, N_TY - 1)], (g_s.at[0], g_r.at[0]))
    group_targets = row_targets(gg[...].reshape(GSKEL, 128))
    pass_on(0, 0)
    for leaf in range(LDEV):
        ku[:, leaf * SKEL : (leaf + 1) * SKEL] = jnp.exp2(
            jnp.dot(group_targets, skeleton_form(leaf), preferred_element_type=F32)
        )
    up_group(0, weights)
    pass_on(0, 1)
    pass_on(0, 2)
    send_points(2)
    diagonal(0)
    for leaf in range(LDEV):
        pass_on(1, leaf)
    settle_both(gt.at[pl.ds(0, N_TX - 1)], (g_s.at[1], g_r.at[1]))
    group_sources = row_sources(gt[...].reshape(N_TX * TSK, 128))
    kc[...] = jnp.exp2(
        lax.dot_general(group_targets, group_sources, (((1,), (1,)), ((), ())), preferred_element_type=F32)
    )
    over_top(0)
    values_here(0)
    points_here(0)
    remote_aux(0)
    slots(0, 0, 0, 1)
    for leaf in range(LDEV):
        pass_on(2, leaf)
    slots(0, 0, 1, HALVES)
    across(0)
    points_here(1)
    remote_aux(1)
    slots(0, 1, 0, HALVES)
    points_here(2)
    remote_aux(2)
    slots(0, 2, 0, HALVES)
    send_back(0)
    down(0)
    first = start + near_rows(0) + near_back(0)
    for half in range(HALVES):
        vals[1, MINE + half] = first[half : half + 1]

    for wave in range(WAVES):
        points_gone(wave)

    send_values(1)
    sum_first(0, pack(dot(start, start), dot(start, first), dot(first, first)))
    spread(1)
    up_group(1, up_leaf(1))
    diagonal(1)
    values_here(1)
    sum_second(0)
    slots(1, 0, 0, 1)
    over_top(1)
    slots(1, 0, 1, HALVES)
    slots(1, 1, 0, HALVES)
    slots(1, 2, 0, HALVES)
    send_back(1)
    norm, curve, square = sum_last(0, 3)
    alpha = norm / curve
    beta = (alpha * alpha * square - norm) / norm
    left = start - alpha * first
    direction = left + beta * start
    across(1)
    down(1)
    second = first + near_rows(1) + near_back(1)
    image = (1.0 + beta) * first - alpha * second
    sum_first(1, pack(dot(direction, image), dot(left, left)))
    sum_second(1)
    curve, norm_next = sum_last(1, 2)
    step = norm_next / curve
    x_rows = alpha * start + step * direction
    r_rows = left - step * image
    for half in range(HALVES):
        x_out[pl.ds(half * HALF, HALF)] = x_rows[half]
        r_out[pl.ds(half * HALF, HALF)] = r_rows[half]


def on_device(points, right_side, near_list, leaf_skeleton, top_index):
    vmem = pl.BlockSpec(memory_space=pltpu.VMEM)
    dma = pltpu.SemaphoreType.DMA
    out = jax.ShapeDtypeStruct((HALVES * HALF,), F32)
    solution_field, residual = pl.pallas_call(
        body,
        out_shape=(out, out),
        in_specs=[pl.BlockSpec(memory_space=pl.ANY)] * 5,
        out_specs=(vmem, vmem),
        scratch_shapes=[
            pltpu.VMEM((HALVES * HALF,), F32),
            pltpu.SMEM((LDEV, SLOTS), jnp.int32),
            pltpu.VMEM((LDEV, SKEL), jnp.int32),
            pltpu.SMEM((TSK,), jnp.int32),
            dma((4 + WAVES,)),
            *[pltpu.VMEM((ROWS, D, part), BF16) for part in PARTS],
            *[pltpu.VMEM((ROWS, 16, part), BF16) for part in PARTS],
            pltpu.VMEM((2, ROWS, 1, HALF), F32),
            pltpu.VMEM((HALVES, HALF, 256), BF16),
            pltpu.VMEM((HALVES, HALF, 128), F32),
            pltpu.VMEM((HALVES, HALF, 128), F32),
            *[pltpu.VMEM((HALVES, HALF, SLOTS * part), F32) for part in PARTS],
            pltpu.VMEM((LDEV, HALF, LEAF), F32),
            pltpu.VMEM((LDEV, HALF, HALF), F32),
            pltpu.VMEM((HALVES, HALF, SKEL), F32),
            pltpu.VMEM((GSKEL, LDEV * SKEL), F32),
            pltpu.VMEM((GSKEL, N_TX * TSK), F32),
            pltpu.VMEM((128, HALF), F32),
            pltpu.VMEM((ROWS, 128), F32),
            pltpu.VMEM((2, GAPS, 8, HALF), F32),
            pltpu.VMEM((2, GAPS, 8, HALF), F32),
            pltpu.VMEM((128, LDEV * SKEL), BF16),
            pltpu.VMEM((N_TY, TSK, 128), BF16),
            pltpu.VMEM((N_TX, TSK, 128), BF16),
            pltpu.VMEM((2, N_TY, 1, 128), F32),
            pltpu.VMEM((2, N_TY, 1, 128), F32),
            pltpu.VMEM((2, 1, 128), F32),
            pltpu.VMEM((2, N_TX, 1, 128), F32),
            pltpu.VMEM((2, 1, GSKEL), F32),
            pltpu.VMEM((2, N_TY, 1, GSKEL), F32),
            pltpu.VMEM((2, 1, 128), F32),
            pltpu.VMEM((2, N_TY, 1, 128), F32),
            pltpu.VMEM((2, N_TX, 1, 128), F32),
            pltpu.VMEM((2, 1, 128), F32),
            dma((WAVES,)), dma((WAVES, 3, LDEV)),
            *[dma((2,))] * 16,
        ],
        compiler_params=pltpu.CompilerParams(
            collective_id=0, has_side_effects=True, vmem_limit_bytes=64 * 1024 * 1024 - 512 * 1024
        ),
        name="ridge_cg",
    )(points, right_side, near_list, leaf_skeleton, top_index)
    return solution_field, residual


def solution(mesh):
    placed = (
        P(None, ("tx", "ty")),
        P(("tx", "ty")),
        P(("tx", "ty"), None),
        P(("tx", "ty"), None),
        P(("tx", "ty")),
    )
    return jax.shard_map(
        on_device,
        mesh=mesh,
        in_specs=placed,
        out_specs=(P(("tx", "ty")), P(("tx", "ty"))),
        check_vma=False,
    )
```

```python
import functools
import math

import jax
import jax.numpy as jnp
from jax import lax
from jax.experimental import pallas as pl
from jax.experimental.pallas import tpu as pltpu
from jax.sharding import PartitionSpec as P

F32 = jnp.float32
BF16 = jnp.bfloat16
HI = lax.Precision.HIGHEST

D = 64
LEAF = 1024
HALF = 512
SKEL = 256
LDEV = 3
HALVES = LDEV * 2
SLOTS = 6
TSK = 32
N_TX = 16
N_TY = 8
GSKEL = TSK * N_TY
REACH = 2
GAPS = 2 * REACH + 1
ROWS = 8 * GAPS
MINE = 8 * REACH
QUADS = 8 * HALVES
CHUNK = 128
PARTS = (256, 128, 128)
STARTS = (0, 256, 384)
WAVES = len(PARTS)

SCALE = 2.0 * math.log2(math.e) / 20.0
A_LEAF = 0.25
E_GROUP = LEAF / (LDEV * N_TY * SKEL)
E_TOP = LEAF / (N_TX * GSKEL)
FAR = 32.0


def split3(x):
    high = x.astype(BF16)
    rest = x - high.astype(F32)
    mid = rest.astype(BF16)
    low = (rest - mid.astype(F32)).astype(BF16)
    return high, mid, low


def aux_rows(coords, first):
    wide = coords.astype(F32)
    norm = (-0.5 * SCALE) * jnp.sum(wide * wide, axis=0, keepdims=True)
    high, mid, low = [t.astype(F32) for t in split3(norm)]
    row = lax.broadcasted_iota(jnp.int32, (16, coords.shape[1]), 0)
    lead = 0 if first else 3
    ones = jnp.where((row >= 3 - lead) & (row < 6 - lead), 1.0, 0.0)
    parts = jnp.where(row == lead, high, jnp.where(row == lead + 1, mid, jnp.where(row == lead + 2, low, ones)))
    return parts


def source_form(coords, aux):
    pad = jnp.zeros((48, coords.shape[1]), BF16)
    return jnp.concatenate([coords, coords, coords, aux, pad], axis=0)


def target_form(coords):
    high, mid, low = split3(coords.astype(F32) * SCALE)
    pad = jnp.zeros((48, coords.shape[1]), F32)
    aux = aux_rows(coords, True)
    stack = jnp.concatenate([high.astype(F32), mid.astype(F32), low.astype(F32), aux, pad], axis=0)
    return stack.T.astype(BF16)


def lane_aux(wide, first):
    norm = (-0.5 * SCALE) * jnp.sum(wide * wide, axis=1, keepdims=True)
    high, mid, low = [t.astype(F32) for t in split3(norm)]
    lane = lax.broadcasted_iota(jnp.int32, wide.shape, 1) - D
    lead = 0 if first else 3
    ones = jnp.where((lane >= 3 - lead) & (lane < 6 - lead), 1.0, 0.0)
    return jnp.where(lane == lead, high, jnp.where(lane == lead + 1, mid, jnp.where(lane == lead + 2, low, ones)))


def row_targets(raw):
    wide = raw.astype(F32)
    high, mid, low = [t.astype(F32) for t in split3(wide * SCALE)]
    left = high + pltpu.roll(mid, D, 1)
    right = low + lane_aux(wide, True)
    return jnp.concatenate([left, right], axis=1).astype(BF16)


def row_sources(raw):
    wide = raw.astype(F32)
    left = wide + pltpu.roll(wide, D, 1)
    right = wide + lane_aux(wide, False)
    return jnp.concatenate([left, right], axis=1).astype(BF16)


def to_row(columns):
    ones = jnp.ones((8, 384), BF16)
    parts = jnp.concatenate(split3(columns), axis=1)
    return lax.dot_general(
        ones, parts, (((1,), (1,)), ((), ())), preferred_element_type=F32
    )[0:1]


def to_column(row):
    parts = []
    for start in range(0, row.shape[1], 128):
        piece = jnp.broadcast_to(row[:, start : start + 128], (128, 128))
        parts.append(piece.T)
    return jnp.concatenate(parts, axis=0) if len(parts) > 1 else parts[0]


def fold_lanes(tile):
    total = tile[:, 0:128]
    for start in range(128, tile.shape[1], 128):
        total = total + tile[:, start : start + 128]
    return total


def fold_rows(tile):
    return jnp.sum(tile.reshape(tile.shape[0] // 8, 8, tile.shape[1]), axis=0)


def tile_lanes(column, width):
    return jnp.concatenate([column] * (width // 128), axis=1)


def body(
    pts_hbm, rhs_hbm, near_hbm, skel_hbm, top_hbm, x_out, r_out,
    rhs_in, near, skel_in, top_in, in_s,
    pts_a, pts_b, pts_c, aux_a, aux_b, aux_c, vals, taug, vb, acc, kq_a, kq_b, kq_c, kd, ke, ka, ku, kc, cbuf, moh,
    zsend, zin, skp, gg, gt, psend, pin, ufull, usend, uin, wsend, win, s_one, s_ty, s_tx, s_two,
    pt_s, pt_r, va_s, va_r, z_s, z_r, g_s, g_r, p_s, p_r, u_s, u_r, w_s, w_r, a_s, a_r, b_s, b_r,
):
    my_tx = lax.axis_index("tx")
    my_ty = lax.axis_index("ty")
    pts = (pts_a, pts_b, pts_c)
    aux = (aux_a, aux_b, aux_c)
    kq = (kq_a, kq_b, kq_c)

    def tx_at(step):
        return lax.rem(my_tx + (step + N_TX), N_TX)

    def ty_at(step):
        return lax.rem(my_ty + (step + N_TY), N_TY)

    def send(src, dst, s_sem, r_sem, **where):
        copy = pltpu.make_async_remote_copy(
            src_ref=src, dst_ref=dst, send_sem=s_sem, recv_sem=r_sem,
            device_id=where, device_id_type=pl.DeviceIdType.MESH,
        )
        return copy

    def settle(space, sem):
        pltpu.make_async_copy(space, space, sem).wait()

    def settle_both(space, pair):
        settle(space, pair[0])
        settle(space, pair[1])

    barrier = pltpu.get_barrier_semaphore()
    for step in range(1, N_TX):
        pl.semaphore_signal(barrier, inc=1, device_id={"tx": tx_at(step)}, device_id_type=pl.DeviceIdType.MESH)
    for step in range(1, N_TY):
        pl.semaphore_signal(barrier, inc=1, device_id={"ty": ty_at(step)}, device_id_type=pl.DeviceIdType.MESH)
    loads = [
        pltpu.make_async_copy(near_hbm, near, in_s.at[0]),
        pltpu.make_async_copy(top_hbm, top_in, in_s.at[1]),
        pltpu.make_async_copy(skel_hbm, skel_in, in_s.at[2]),
        pltpu.make_async_copy(rhs_hbm, rhs_in, in_s.at[3]),
    ]
    for copy in loads:
        copy.start()
    for wave in range(WAVES):
        for half in range(HALVES):
            start = half * HALF + STARTS[wave]
            pltpu.make_async_copy(
                pts_hbm.at[:, pl.ds(start, PARTS[wave])], pts[wave].at[MINE + half], in_s.at[4 + wave]
            ).start()
    for half in range(HALVES, 8):
        vals[0, MINE + half] = jnp.zeros((1, HALF), F32)
        vals[1, MINE + half] = jnp.zeros((1, HALF), F32)
    for copy in loads:
        copy.wait()
    for wave in range(WAVES):
        settle(pts[wave].at[pl.ds(MINE, HALVES)], in_s.at[4 + wave])
    for half in range(HALVES):
        vals[0, MINE + half] = rhs_in[pl.ds(half * HALF, HALF)].reshape(1, HALF)

    remote_gaps = [1, -1, 2, -2]

    def point_copy(wave, leaf, number):
        gap = remote_gaps[number]
        source = 8 * (REACH if number < 2 else REACH + gap // 2) + 2 * leaf
        place = 8 * (gap + REACH) + 2 * leaf
        return send(
            pts[wave].at[pl.ds(source, 2)], pts[wave].at[pl.ds(place, 2)],
            pt_s.at[wave], pt_r.at[wave, number, leaf] if number < 2 else pt_r.at[wave, 2, 0],
            tx=tx_at(-1 if gap > 0 else 1),
        )

    points_out = {}

    def send_points(wave):
        for leaf in range(LDEV):
            for number in range(2):
                copy = point_copy(wave, leaf, number)
                copy.start()
                points_out[wave, leaf, number] = copy

    def pass_on(wave, leaf):
        for number in range(2):
            points_out[wave, leaf, number].wait_recv()
            point_copy(wave, leaf, number + 2).start()

    def points_here(wave):
        settle(pts[wave].at[pl.ds(0, 2 * HALVES)], pt_r.at[wave, 2, 0])

    def points_gone(wave):
        settle(pts[wave].at[pl.ds(0, 4 * HALVES)], pt_s.at[wave])

    def send_values(it):
        for gap in remote_gaps:
            place = 8 * (gap + REACH)
            send(
                vals.at[it, pl.ds(MINE, 8)], vals.at[it, pl.ds(place, 8)], va_s.at[it], va_r.at[it], tx=tx_at(-gap)
            ).start()

    def values_here(it):
        four = vals.at[it, pl.ds(0, 8 * (GAPS - 1))]
        settle_both(four, (va_s.at[it], va_r.at[it]))

    def slot(leaf, number, half):
        named = near[leaf, number]
        live = named >= 0
        named = jnp.maximum(named, 0)
        place = lax.rem(lax.div(named, LDEV * N_TY) - my_tx + (N_TX + REACH), N_TX)
        other = lax.rem(named, LDEV)
        same = place == REACH
        itself = live & same & (other == leaf)
        use = live & jnp.logical_not(itself) & (place < GAPS)
        back = jnp.where((place < REACH) | (same & (other < leaf)), 1, 0)
        other_half = half + back - 2 * half * back
        index = jnp.where(use, 8 * place + 2 * other + other_half, MINE)
        return index, jnp.where(use, 1.0, 0.0), jnp.where(live, 1.0, 0.0) + jnp.where(itself, 1.0, 0.0)

    def degree(leaf):
        total = 0.0
        for number in range(SLOTS):
            total = total + slot(leaf, number, 0)[2]
        return total

    sub = lax.broadcasted_iota(jnp.int32, (ROWS, 128), 0)
    lane = lax.broadcasted_iota(jnp.int32, (ROWS, 128), 1)

    def mark(row, table):
        for number in range(SLOTS):
            index, use, unused = slot(lax.div(row, 2), number, lax.rem(row, 2))
            table = jnp.where((lane == 8 * row + number) & (sub == index), use, table)
        return table

    table = lax.fori_loop(0, HALVES, mark, jnp.zeros((ROWS, 128), F32))
    for leaf in range(LDEV):
        table = jnp.where((lane == QUADS + leaf) & (sub == MINE + 2 * leaf + 1), degree(leaf), table)
    moh[...] = table
    cbuf[pl.ds(QUADS, 128 - QUADS)] = jnp.zeros((128 - QUADS, HALF), F32)

    def own_half(half):
        return jnp.concatenate([pts[wave][MINE + half] for wave in range(WAVES)], axis=1)

    def own_forms(half, carry):
        taug[half] = target_form(own_half(half))
        for wave in range(WAVES):
            aux[wave][MINE + half] = aux_rows(pts[wave][MINE + half], False).astype(BF16)
        return carry

    skp[pl.ds(D, 128 - D)] = jnp.zeros((128 - D, LDEV * SKEL), BF16)
    for leaf in range(LDEV):
        chosen = skel_in[leaf : leaf + 1]
        picked = jnp.zeros((D, SKEL), F32)
        for half in range(2):
            place = lax.broadcasted_iota(jnp.int32, (HALF, SKEL), 0) + half * HALF
            hot = jnp.where(place == chosen, 1.0, 0.0).astype(BF16)
            picked = picked + jnp.dot(own_half(2 * leaf + half), hot, preferred_element_type=F32)
        skp[0:D, leaf * SKEL : (leaf + 1) * SKEL] = picked.astype(BF16)
    wide_lane = lax.broadcasted_iota(jnp.int32, (1, LDEV * SKEL), 1)
    hot_rows = [jnp.where(wide_lane == top_in[t], 1.0, 0.0) for t in range(TSK)]
    hot = jnp.concatenate(hot_rows, axis=0).astype(BF16)
    mine_top = lax.dot_general(
        hot, skp[...], (((1,), (1,)), ((), ())), preferred_element_type=F32
    ).astype(BF16)
    gg[my_ty] = mine_top
    gt[my_tx] = mine_top

    def send_top_near():
        for step in range(1, N_TY):
            send(gg.at[my_ty], gg.at[my_ty], g_s.at[0], g_r.at[0], ty=ty_at(step)).start()

    def send_top_far():
        for step in range(1, N_TX):
            send(gt.at[my_tx], gt.at[my_tx], g_s.at[1], g_r.at[1], tx=tx_at(step)).start()

    def spread(it):
        def step(half, carry):
            vb[half] = to_column(vals[it, MINE + half])
            return carry
        lax.fori_loop(0, HALVES, step, 0)

    def skeleton_form(leaf):
        coords = skp[0:D, leaf * SKEL : (leaf + 1) * SKEL]
        return source_form(coords, aux_rows(coords, False).astype(BF16))

    def up_leaf(it):
        parts = []
        for leaf in range(LDEV):
            if it == 0:
                form = skeleton_form(leaf)
            total = jnp.zeros((8, SKEL), F32)
            for half in range(2):
                row = 2 * leaf + half
                if it == 0:
                    ka[row] = jnp.exp2(jnp.dot(taug[row], form, preferred_element_type=F32))
                total = total + fold_rows(ka[row] * tile_lanes(vb[row], SKEL))
            parts.append(jnp.sum(total, axis=0, keepdims=True))
        return jnp.concatenate(parts, axis=1) * A_LEAF

    narrow = lax.broadcasted_iota(jnp.int32, (1, 128), 1)

    def by_part(row):
        rows = []
        for part in range(N_TY):
            tile = row[:, 128 * (part // 4) : 128 * (part // 4) + 128]
            shift = (128 - TSK * (part % 4)) % 128
            if shift:
                tile = pltpu.roll(tile, shift, 1)
            rows.append(jnp.where(narrow < TSK, tile, 0.0))
        return rows

    def up_group(it, weights):
        partial = to_row(fold_lanes(ku[...] * weights)) * E_GROUP
        for part, row in enumerate(by_part(partial)):
            psend[it, part] = row
            pin[it, my_ty, part] = row
        for step in range(1, N_TY):
            send(psend.at[it], pin.at[it, my_ty], p_s.at[it], p_r.at[it], ty=ty_at(step)).start()

    def over_top(it):
        settle_both(pin.at[it, pl.ds(0, N_TY - 1)], (p_s.at[it], p_r.at[it]))
        ufull[it] = jnp.sum(pin[it], axis=0)
        usend[it] = ufull[it, my_ty]
        uin[it, my_tx] = usend[it]
        for step in range(1, N_TX):
            send(usend.at[it], uin.at[it, my_tx], u_s.at[it], u_r.at[it], tx=tx_at(step)).start()

    def across(it):
        settle_both(uin.at[it, pl.ds(0, N_TX - 1)], (u_s.at[it], u_r.at[it]))
        tiles = []
        for tile in range(4):
            total = uin[it, 4 * tile]
            for k in range(1, 4):
                total = total + pltpu.roll(uin[it, 4 * tile + k], TSK * k, 1)
            tiles.append(total)
        upper = jnp.concatenate(tiles, axis=1)
        wsend[it] = to_row(fold_lanes(kc[...] * upper)) * E_TOP
        win[it, my_ty] = wsend[it]
        for step in range(1, N_TY):
            send(wsend.at[it], win.at[it, my_ty], w_s.at[it], w_r.at[it], ty=ty_at(step)).start()

    def down(it):
        settle_both(win.at[it, pl.ds(0, N_TY - 1)], (w_s.at[it], w_r.at[it]))
        middle = to_column(jnp.sum(win[it], axis=0))
        lower = fold_rows(ku[...] * tile_lanes(middle, LDEV * SKEL))
        lower = jnp.sum(lower, axis=0, keepdims=True) * (E_GROUP * A_LEAF * FAR * SLOTS)
        for leaf in range(LDEV):
            weights = lower[:, leaf * SKEL : (leaf + 1) * SKEL]
            for half in range(2):
                row = 2 * leaf + half
                acc[row] = fold_lanes(ka[row] * weights)

    def stretch(it, store, row, form, values, fresh, first):
        width = values.shape[1]
        total = jnp.zeros((8, width - first), F32)
        for start in range(0, HALF, CHUNK):
            rows = pl.ds(start, CHUNK)
            if it == 0:
                tile = jnp.exp2(jnp.dot(taug[row, rows], form, preferred_element_type=F32))
                store[rows] = tile
            else:
                tile = store[rows]
            part = fold_lanes(tile * values)
            if fresh:
                acc[row, rows] = part
            else:
                acc[row, rows] += part
            if first < width:
                total = total + fold_rows(tile[:, first:] * tile_lanes(vb[row, rows], width - first))
        return jnp.sum(total, axis=0, keepdims=True) if first < width else None

    def form_of(wave, index):
        return source_form(pts[wave][index], aux[wave][index])

    def diagonal(it):
        def step(leaf, carry):
            weight = degree(leaf)
            low, high = 2 * leaf, 2 * leaf + 1
            form = None
            if it == 0:
                form = jnp.concatenate(
                    [form_of(wave, MINE + half) for half in (low, high) for wave in range(WAVES)], axis=1
                )
            values = jnp.concatenate([vals[it, MINE + low], vals[it, MINE + high]], axis=1) * weight
            cbuf[pl.ds(QUADS + leaf, 1)] = stretch(it, kd.at[leaf], low, form, values, True, HALF)
            if it == 0:
                form = form[:, HALF:]
            stretch(it, ke.at[leaf], high, form, values[:, HALF:], True, HALF)
            return carry
        lax.fori_loop(0, LDEV, step, 0)

    def slots(it, wave, start, stop):
        part = PARTS[wave]

        def step(row, carry):
            leaf, half = lax.div(row, 2), lax.rem(row, 2)
            forms, values = [], []
            for number in range(SLOTS):
                index, use, unused = slot(leaf, number, half)
                if it == 0:
                    forms.append(form_of(wave, index))
                values.append(vals[it, index][:, STARTS[wave] : STARTS[wave] + PARTS[wave]] * use)
            form = jnp.concatenate(forms, axis=1) if it == 0 else None
            total = stretch(it, kq[wave].at[row], row, form, jnp.concatenate(values, axis=1), False, 0)
            rows = [total[:, number * part : (number + 1) * part] for number in range(SLOTS)]
            rows.append(jnp.zeros((8 - SLOTS, part), F32))
            cbuf[pl.ds(pl.multiple_of(8 * row, 8), 8), STARTS[wave] : STARTS[wave] + part] = jnp.concatenate(rows, axis=0)
            return carry
        lax.fori_loop(start, stop, step, 0)

    def send_back(it):
        parts = jnp.dot(moh[...], cbuf[...], precision=HI, preferred_element_type=F32)
        for place in range(GAPS):
            zsend[it, place] = parts[8 * place : 8 * place + 8]
        for gap in remote_gaps:
            send(zsend.at[it, gap + REACH], zin.at[it, REACH - gap], z_s.at[it], z_r.at[it], tx=tx_at(gap)).start()

    def rows_of_acc():
        rows = [to_row(acc[half]) for half in range(HALVES)]
        return jnp.concatenate(rows + [jnp.zeros((8 - HALVES, HALF), F32)], axis=0) * (1.0 / SLOTS)

    def near_rows(it):
        return rows_of_acc() + zsend[it, REACH] * (1.0 / SLOTS)

    def near_back(it):
        settle_both(zin.at[it, pl.ds(0, GAPS - 1)], (z_s.at[it], z_r.at[it]))
        total = zin[it, 0]
        for place in range(1, GAPS):
            if place != REACH:
                total = total + zin[it, place]
        return total * (1.0 / SLOTS)

    def own_rows(it):
        return jnp.concatenate([vals[it, MINE + half] for half in range(8)], axis=0)

    def pack(*sums):
        row = jnp.zeros((1, 128), F32)
        for number, value in enumerate(sums):
            row = jnp.where(narrow == number, value, row)
        return row

    def sum_first(number, row):
        s_one[number] = row
        s_ty[number, my_ty] = row
        for step in range(1, N_TY):
            send(s_one.at[number], s_ty.at[number, my_ty], a_s.at[number], a_r.at[number], ty=ty_at(step)).start()

    def sum_second(number):
        settle_both(s_ty.at[number, pl.ds(0, N_TY - 1)], (a_s.at[number], a_r.at[number]))
        row = jnp.sum(s_ty[number], axis=0)
        s_two[number] = row
        s_tx[number, my_tx] = row
        for step in range(1, N_TX):
            send(s_two.at[number], s_tx.at[number, my_tx], b_s.at[number], b_r.at[number], tx=tx_at(step)).start()

    def sum_last(number, count):
        settle_both(s_tx.at[number, pl.ds(0, N_TX - 1)], (b_s.at[number], b_r.at[number]))
        row = jnp.sum(s_tx[number], axis=0)
        return [jnp.sum(jnp.where(narrow == k, row, 0.0), axis=1, keepdims=True) for k in range(count)]

    def total_of(tile):
        return jnp.sum(jnp.sum(tile, axis=0, keepdims=True), axis=1, keepdims=True)

    def dot(one, two):
        return total_of(one * two)

    def remote_aux(wave):
        for place in range(GAPS):
            if place != REACH:
                def one(half, carry, place=place):
                    aux[wave][8 * place + half] = aux_rows(pts[wave][8 * place + half], False).astype(BF16)
                    return carry
                lax.fori_loop(0, HALVES, one, 0)

    lax.fori_loop(0, HALVES, own_forms, 0)
    spread(0)
    start = own_rows(0)
    pl.semaphore_wait(barrier, N_TX - 1 + N_TY - 1)

    send_points(0)
    send_top_near()
    send_points(1)
    send_top_far()
    send_values(0)
    weights = up_leaf(0)
    settle_both(gg.at[pl.ds(0, N_TY - 1)], (g_s.at[0], g_r.at[0]))
    group_targets = row_targets(gg[...].reshape(GSKEL, 128))
    pass_on(0, 0)
    for leaf in range(LDEV):
        ku[:, leaf * SKEL : (leaf + 1) * SKEL] = jnp.exp2(
            jnp.dot(group_targets, skeleton_form(leaf), preferred_element_type=F32)
        )
    up_group(0, weights)
    pass_on(0, 1)
    pass_on(0, 2)
    send_points(2)
    diagonal(0)
    for leaf in range(LDEV):
        pass_on(1, leaf)
    settle_both(gt.at[pl.ds(0, N_TX - 1)], (g_s.at[1], g_r.at[1]))
    group_sources = row_sources(gt[...].reshape(N_TX * TSK, 128))
    kc[...] = jnp.exp2(
        lax.dot_general(group_targets, group_sources, (((1,), (1,)), ((), ())), preferred_element_type=F32)
    )
    over_top(0)
    values_here(0)
    points_here(0)
    remote_aux(0)
    slots(0, 0, 0, 1)
    for leaf in range(LDEV):
        pass_on(2, leaf)
    slots(0, 0, 1, HALVES)
    across(0)
    points_here(1)
    remote_aux(1)
    slots(0, 1, 0, HALVES)
    points_here(2)
    remote_aux(2)
    slots(0, 2, 0, HALVES)
    send_back(0)
    own_first = start + near_rows(0)
    down(0)
    first = own_first + rows_of_acc() + near_back(0)
    for half in range(HALVES):
        vals[1, MINE + half] = first[half : half + 1]

    for wave in range(WAVES):
        points_gone(wave)

    send_values(1)
    sum_first(0, pack(dot(start, start), dot(start, first), dot(first, first)))
    spread(1)
    up_group(1, up_leaf(1))
    diagonal(1)
    values_here(1)
    sum_second(0)
    slots(1, 0, 0, 2)
    over_top(1)
    slots(1, 0, 2, HALVES)
    slots(1, 1, 0, HALVES)
    slots(1, 2, 0, HALVES)
    send_back(1)
    own_second = first + near_rows(1)
    norm, curve, square = sum_last(0, 3)
    alpha = norm / curve
    beta = (alpha * alpha * square - norm) / norm
    left = start - alpha * first
    direction = left + beta * start
    across(1)
    c_start, c_first = 1.0 + beta, -alpha
    bend = dot(direction, c_start * own_first + c_first * own_second)
    given = jnp.zeros((8, HALF), F32)
    for place in range(GAPS):
        if place != REACH:
            theirs = [
                jnp.concatenate([vals[it, 8 * place + half] for half in range(8)], axis=0) for it in range(2)
            ]
            given = given + (c_start * theirs[0] + c_first * theirs[1]) * (
                c_start * zsend[0, place] + c_first * zsend[1, place]
            )
    top = jnp.zeros((1, 128), F32)
    for part, row in enumerate(by_part(c_start * wsend[0] + c_first * wsend[1])):
        top = top + row * (c_start * ufull[0, part] + c_first * ufull[1, part])
    bend = bend + total_of(given) * (1.0 / SLOTS) + total_of(top) * FAR
    sum_first(1, pack(bend, dot(left, left)))
    down(1)
    far_second = rows_of_acc()
    sum_second(1)
    second = own_second + far_second + near_back(1)
    image = c_start * first + c_first * second
    curve, norm_next = sum_last(1, 2)
    step = norm_next / curve
    x_rows = alpha * start + step * direction
    r_rows = left - step * image
    for half in range(HALVES):
        x_out[pl.ds(half * HALF, HALF)] = x_rows[half]
        r_out[pl.ds(half * HALF, HALF)] = r_rows[half]


def on_device(points, right_side, near_list, leaf_skeleton, top_index):
    vmem = pl.BlockSpec(memory_space=pltpu.VMEM)
    dma = pltpu.SemaphoreType.DMA
    out = jax.ShapeDtypeStruct((HALVES * HALF,), F32)
    solution_field, residual = pl.pallas_call(
        body,
        out_shape=(out, out),
        in_specs=[pl.BlockSpec(memory_space=pl.ANY)] * 5,
        out_specs=(vmem, vmem),
        scratch_shapes=[
            pltpu.VMEM((HALVES * HALF,), F32),
            pltpu.SMEM((LDEV, SLOTS), jnp.int32),
            pltpu.VMEM((LDEV, SKEL), jnp.int32),
            pltpu.SMEM((TSK,), jnp.int32),
            dma((4 + WAVES,)),
            *[pltpu.VMEM((ROWS, D, part), BF16) for part in PARTS],
            *[pltpu.VMEM((ROWS, 16, part), BF16) for part in PARTS],
            pltpu.VMEM((2, ROWS, 1, HALF), F32),
            pltpu.VMEM((HALVES, HALF, 256), BF16),
            pltpu.VMEM((HALVES, HALF, 128), F32),
            pltpu.VMEM((HALVES, HALF, 128), F32),
            *[pltpu.VMEM((HALVES, HALF, SLOTS * part), F32) for part in PARTS],
            pltpu.VMEM((LDEV, HALF, LEAF), F32),
            pltpu.VMEM((LDEV, HALF, HALF), F32),
            pltpu.VMEM((HALVES, HALF, SKEL), F32),
            pltpu.VMEM((GSKEL, LDEV * SKEL), F32),
            pltpu.VMEM((GSKEL, N_TX * TSK), F32),
            pltpu.VMEM((128, HALF), F32),
            pltpu.VMEM((ROWS, 128), F32),
            pltpu.VMEM((2, GAPS, 8, HALF), F32),
            pltpu.VMEM((2, GAPS, 8, HALF), F32),
            pltpu.VMEM((128, LDEV * SKEL), BF16),
            pltpu.VMEM((N_TY, TSK, 128), BF16),
            pltpu.VMEM((N_TX, TSK, 128), BF16),
            pltpu.VMEM((2, N_TY, 1, 128), F32),
            pltpu.VMEM((2, N_TY, N_TY, 1, 128), F32),
            pltpu.VMEM((2, N_TY, 1, 128), F32),
            pltpu.VMEM((2, 1, 128), F32),
            pltpu.VMEM((2, N_TX, 1, 128), F32),
            pltpu.VMEM((2, 1, GSKEL), F32),
            pltpu.VMEM((2, N_TY, 1, GSKEL), F32),
            pltpu.VMEM((2, 1, 128), F32),
            pltpu.VMEM((2, N_TY, 1, 128), F32),
            pltpu.VMEM((2, N_TX, 1, 128), F32),
            pltpu.VMEM((2, 1, 128), F32),
            dma((WAVES,)), dma((WAVES, 3, LDEV)),
            *[dma((2,))] * 16,
        ],
        compiler_params=pltpu.CompilerParams(
            collective_id=0, has_side_effects=True, vmem_limit_bytes=64 * 1024 * 1024 - 512 * 1024
        ),
        name="ridge_cg",
    )(points, right_side, near_list, leaf_skeleton, top_index)
    return solution_field, residual


def solution(mesh):
    placed = (
        P(None, ("tx", "ty")),
        P(("tx", "ty")),
        P(("tx", "ty"), None),
        P(("tx", "ty"), None),
        P(("tx", "ty")),
    )
    return jax.shard_map(
        on_device,
        mesh=mesh,
        in_specs=placed,
        out_specs=(P(("tx", "ty")), P(("tx", "ty"))),
        check_vma=False,
    )
```

```python
import functools
import math

import jax
import jax.numpy as jnp
from jax import lax
from jax.experimental import pallas as pl
from jax.experimental.pallas import tpu as pltpu
from jax.sharding import PartitionSpec as P

F32 = jnp.float32
BF16 = jnp.bfloat16
HI = lax.Precision.HIGHEST

D = 64
LEAF = 1024
HALF = 512
SKEL = 256
LDEV = 3
HALVES = LDEV * 2
SLOTS = 6
TSK = 32
N_TX = 16
N_TY = 8
GSKEL = TSK * N_TY
REACH = 2
GAPS = 2 * REACH + 1
ROWS = 8 * GAPS
MINE = 8 * REACH
QUADS = 8 * HALVES
SPARE = 64
CHUNK = 128
PARTS = (128, 128, 128, 128)
STARTS = (0, 128, 256, 384)
WAVES = len(PARTS)

SCALE = 2.0 * math.log2(math.e) / 20.0
A_LEAF = 0.25
E_GROUP = LEAF / (LDEV * N_TY * SKEL)
E_TOP = LEAF / (N_TX * GSKEL)
FAR = 32.0


def split3(x):
    high = x.astype(BF16)
    rest = x - high.astype(F32)
    mid = rest.astype(BF16)
    low = (rest - mid.astype(F32)).astype(BF16)
    return high, mid, low


def aux_rows(coords, first):
    wide = coords.astype(F32)
    norm = (-0.5 * SCALE) * jnp.sum(wide * wide, axis=0, keepdims=True)
    high, mid, low = [t.astype(F32) for t in split3(norm)]
    row = lax.broadcasted_iota(jnp.int32, (16, coords.shape[1]), 0)
    lead = 0 if first else 3
    ones = jnp.where((row >= 3 - lead) & (row < 6 - lead), 1.0, 0.0)
    parts = jnp.where(row == lead, high, jnp.where(row == lead + 1, mid, jnp.where(row == lead + 2, low, ones)))
    return parts


def aux_of_many(coords):
    wide = coords.astype(F32)
    norm = (-0.5 * SCALE) * jnp.sum(wide * wide, axis=1, keepdims=True)
    high, mid, low = [t.astype(F32) for t in split3(norm)]
    row = lax.broadcasted_iota(jnp.int32, (coords.shape[0], 16, coords.shape[2]), 1)
    ones = jnp.where(row < 3, 1.0, 0.0)
    parts = jnp.where(row == 3, high, jnp.where(row == 4, mid, jnp.where(row == 5, low, ones)))
    return parts.astype(BF16)


def source_form(coords, aux):
    pad = jnp.zeros((48, coords.shape[1]), BF16)
    return jnp.concatenate([coords, coords, coords, aux, pad], axis=0)


def target_form(coords):
    high, mid, low = split3(coords.astype(F32) * SCALE)
    pad = jnp.zeros((48, coords.shape[1]), F32)
    aux = aux_rows(coords, True)
    stack = jnp.concatenate([high.astype(F32), mid.astype(F32), low.astype(F32), aux, pad], axis=0)
    return stack.T.astype(BF16)


def lane_aux(wide, first):
    norm = (-0.5 * SCALE) * jnp.sum(wide * wide, axis=1, keepdims=True)
    high, mid, low = [t.astype(F32) for t in split3(norm)]
    lane = lax.broadcasted_iota(jnp.int32, wide.shape, 1) - D
    lead = 0 if first else 3
    ones = jnp.where((lane >= 3 - lead) & (lane < 6 - lead), 1.0, 0.0)
    return jnp.where(lane == lead, high, jnp.where(lane == lead + 1, mid, jnp.where(lane == lead + 2, low, ones)))


def row_targets(raw):
    wide = raw.astype(F32)
    high, mid, low = [t.astype(F32) for t in split3(wide * SCALE)]
    left = high + pltpu.roll(mid, D, 1)
    right = low + lane_aux(wide, True)
    return jnp.concatenate([left, right], axis=1).astype(BF16)


def row_sources(raw):
    wide = raw.astype(F32)
    left = wide + pltpu.roll(wide, D, 1)
    right = wide + lane_aux(wide, False)
    return jnp.concatenate([left, right], axis=1).astype(BF16)


def to_row(columns):
    ones = jnp.ones((8, 384), BF16)
    parts = jnp.concatenate(split3(columns), axis=1)
    return lax.dot_general(
        ones, parts, (((1,), (1,)), ((), ())), preferred_element_type=F32
    )[0:1]


def to_column(row):
    parts = []
    for start in range(0, row.shape[1], 128):
        piece = jnp.broadcast_to(row[:, start : start + 128], (128, 128))
        parts.append(piece.T)
    return jnp.concatenate(parts, axis=0) if len(parts) > 1 else parts[0]


def fold_lanes(tile):
    total = tile[:, 0:128]
    for start in range(128, tile.shape[1], 128):
        total = total + tile[:, start : start + 128]
    return total


def fold_rows(tile):
    return jnp.sum(tile.reshape(tile.shape[0] // 8, 8, tile.shape[1]), axis=0)


def tile_lanes(column, width):
    return jnp.concatenate([column] * (width // 128), axis=1)


def body(
    pts_hbm, rhs_hbm, near_hbm, skel_hbm, top_hbm, x_out, r_out,
    rhs_in, near, skel_in, top_in, in_s,
    pts_a, pts_b, pts_c, pts_d, aux_a, aux_b, aux_c, aux_d, vals, taug, vb, acc, kq_a, kq_b, kq_c, kq_d, kd, ke, ka, ku, kc, cbuf, moh,
    zsend, zin, skp, gg, gt, psend, pin, ufull, usend, uin, wsend, win, s_one, s_ty, s_tx, s_two,
    pt_s, pt_r, va_s, va_r, z_s, z_r, g_s, g_r, p_s, p_r, u_s, u_r, w_s, w_r, a_s, a_r, b_s, b_r,
):
    my_tx = lax.axis_index("tx")
    my_ty = lax.axis_index("ty")
    pts = (pts_a, pts_b, pts_c, pts_d)
    aux = (aux_a, aux_b, aux_c, aux_d)
    kq = (kq_a, kq_b, kq_c, kq_d)

    def tx_at(step):
        return lax.rem(my_tx + (step + N_TX), N_TX)

    def ty_at(step):
        return lax.rem(my_ty + (step + N_TY), N_TY)

    def send(src, dst, s_sem, r_sem, **where):
        copy = pltpu.make_async_remote_copy(
            src_ref=src, dst_ref=dst, send_sem=s_sem, recv_sem=r_sem,
            device_id=where, device_id_type=pl.DeviceIdType.MESH,
        )
        return copy

    def settle(space, sem):
        pltpu.make_async_copy(space, space, sem).wait()

    def settle_both(space, pair):
        settle(space, pair[0])
        settle(space, pair[1])

    barrier = pltpu.get_barrier_semaphore()
    for step in range(1, N_TX):
        pl.semaphore_signal(barrier, inc=1, device_id={"tx": tx_at(step)}, device_id_type=pl.DeviceIdType.MESH)
    for step in range(1, N_TY):
        pl.semaphore_signal(barrier, inc=1, device_id={"ty": ty_at(step)}, device_id_type=pl.DeviceIdType.MESH)
    loads = [
        pltpu.make_async_copy(near_hbm, near, in_s.at[0]),
        pltpu.make_async_copy(top_hbm, top_in, in_s.at[1]),
        pltpu.make_async_copy(skel_hbm, skel_in, in_s.at[2]),
        pltpu.make_async_copy(rhs_hbm, rhs_in, in_s.at[3]),
    ]
    for copy in loads:
        copy.start()
    for wave in range(WAVES):
        for half in range(HALVES):
            start = half * HALF + STARTS[wave]
            pltpu.make_async_copy(
                pts_hbm.at[:, pl.ds(start, PARTS[wave])], pts[wave].at[MINE + half], in_s.at[4 + wave]
            ).start()
    for half in range(HALVES, 8):
        vals[0, MINE + half] = jnp.zeros((1, HALF), F32)
        vals[1, MINE + half] = jnp.zeros((1, HALF), F32)
    for copy in loads:
        copy.wait()
    for wave in range(WAVES):
        settle(pts[wave].at[pl.ds(MINE, HALVES)], in_s.at[4 + wave])
    for half in range(HALVES):
        vals[0, MINE + half] = rhs_in[pl.ds(half * HALF, HALF)].reshape(1, HALF)

    remote_gaps = [1, -1, 2, -2]

    def point_copy(wave, number):
        gap = remote_gaps[number]
        source = 8 * (REACH if number < 2 else REACH + gap // 2)
        place = 8 * (gap + REACH)
        return send(
            pts[wave].at[pl.ds(source, HALVES)], pts[wave].at[pl.ds(place, HALVES)],
            pt_s.at[wave], pt_r.at[wave, min(number, 2)], tx=tx_at(-1 if gap > 0 else 1),
        )

    points_out = {}

    def send_points(wave):
        for number in range(2):
            copy = point_copy(wave, number)
            copy.start()
            points_out[wave, number] = copy

    def pass_on(wave):
        for number in range(2):
            points_out[wave, number].wait_recv()
            point_copy(wave, number + 2).start()

    def points_here(wave):
        settle(pts[wave].at[pl.ds(0, 2 * HALVES)], pt_r.at[wave, 2])

    def points_gone(wave):
        settle(pts[wave].at[pl.ds(0, 4 * HALVES)], pt_s.at[wave])

    def send_values(it):
        for gap in remote_gaps:
            place = 8 * (gap + REACH)
            send(
                vals.at[it, pl.ds(MINE, 8)], vals.at[it, pl.ds(place, 8)], va_s.at[it], va_r.at[it], tx=tx_at(-gap)
            ).start()

    def values_here(it):
        four = vals.at[it, pl.ds(0, 8 * (GAPS - 1))]
        settle_both(four, (va_s.at[it], va_r.at[it]))

    def slot(leaf, number, half):
        named = near[leaf, number]
        live = named >= 0
        named = jnp.maximum(named, 0)
        place = lax.rem(lax.div(named, LDEV * N_TY) - my_tx + (N_TX + REACH), N_TX)
        other = lax.rem(named, LDEV)
        same = place == REACH
        itself = live & same & (other == leaf)
        use = live & jnp.logical_not(itself) & (place < GAPS)
        back = jnp.where((place < REACH) | (same & (other < leaf)), 1, 0)
        other_half = half + back - 2 * half * back
        index = jnp.where(use, 8 * place + 2 * other + other_half, MINE)
        return index, jnp.where(use, 1.0, 0.0), jnp.where(live, 1.0, 0.0) + jnp.where(itself, 1.0, 0.0)

    def degree(leaf):
        total = 0.0
        for number in range(SLOTS):
            total = total + slot(leaf, number, 0)[2]
        return total

    sub = lax.broadcasted_iota(jnp.int32, (ROWS, 128), 0)
    lane = lax.broadcasted_iota(jnp.int32, (ROWS, 128), 1)

    def mark(row, table):
        for number in range(SLOTS):
            index, use, unused = slot(lax.div(row, 2), number, lax.rem(row, 2))
            table = jnp.where((lane == 8 * row + number) & (sub == index), use, table)
        return table

    table = lax.fori_loop(0, HALVES, mark, jnp.zeros((ROWS, 128), F32))
    for leaf in range(LDEV):
        table = jnp.where((lane == QUADS + leaf) & (sub == MINE + 2 * leaf + 1), degree(leaf), table)
    moh[...] = table
    cbuf[pl.ds(QUADS, 128 - QUADS)] = jnp.zeros((128 - QUADS, HALF), F32)

    def own_half(half):
        return jnp.concatenate([pts[wave][MINE + half] for wave in range(WAVES)], axis=1)

    def own_forms(half, carry):
        taug[half] = target_form(own_half(half))
        for wave in range(WAVES):
            aux[wave][MINE + half] = aux_rows(pts[wave][MINE + half], False).astype(BF16)
        return carry

    skp[pl.ds(D, 128 - D)] = jnp.zeros((128 - D, LDEV * SKEL), BF16)
    for leaf in range(LDEV):
        chosen = skel_in[leaf : leaf + 1]
        picked = jnp.zeros((D, SKEL), F32)
        for half in range(2):
            place = lax.broadcasted_iota(jnp.int32, (HALF, SKEL), 0) + half * HALF
            hot = jnp.where(place == chosen, 1.0, 0.0).astype(BF16)
            picked = picked + jnp.dot(own_half(2 * leaf + half), hot, preferred_element_type=F32)
        skp[0:D, leaf * SKEL : (leaf + 1) * SKEL] = picked.astype(BF16)
    wide_lane = lax.broadcasted_iota(jnp.int32, (1, LDEV * SKEL), 1)
    hot_rows = [jnp.where(wide_lane == top_in[t], 1.0, 0.0) for t in range(TSK)]
    hot = jnp.concatenate(hot_rows, axis=0).astype(BF16)
    mine_top = lax.dot_general(
        hot, skp[...], (((1,), (1,)), ((), ())), preferred_element_type=F32
    ).astype(BF16)
    gg[my_ty] = mine_top
    gt[my_tx] = mine_top

    def send_top_near():
        for step in range(1, N_TY):
            send(gg.at[my_ty], gg.at[my_ty], g_s.at[0], g_r.at[0], ty=ty_at(step)).start()

    def send_top_far():
        for step in range(1, N_TX):
            send(gt.at[my_tx], gt.at[my_tx], g_s.at[1], g_r.at[1], tx=tx_at(step)).start()

    def spread(it):
        def step(half, carry):
            vb[half] = to_column(vals[it, MINE + half])
            return carry
        lax.fori_loop(0, HALVES, step, 0)

    def skeleton_form(leaf):
        coords = skp[0:D, leaf * SKEL : (leaf + 1) * SKEL]
        return source_form(coords, aux_rows(coords, False).astype(BF16))

    def up_leaf(it):
        parts = []
        for leaf in range(LDEV):
            if it == 0:
                form = skeleton_form(leaf)
            total = jnp.zeros((8, SKEL), F32)
            for half in range(2):
                row = 2 * leaf + half
                if it == 0:
                    ka[row] = jnp.exp2(jnp.dot(taug[row], form, preferred_element_type=F32))
                total = total + fold_rows(ka[row] * tile_lanes(vb[row], SKEL))
            parts.append(jnp.sum(total, axis=0, keepdims=True))
        return jnp.concatenate(parts, axis=1) * A_LEAF

    narrow = lax.broadcasted_iota(jnp.int32, (1, 128), 1)

    def by_part(row):
        rows = []
        for part in range(N_TY):
            tile = row[:, 128 * (part // 4) : 128 * (part // 4) + 128]
            shift = (128 - TSK * (part % 4)) % 128
            if shift:
                tile = pltpu.roll(tile, shift, 1)
            rows.append(jnp.where(narrow < TSK, tile, 0.0))
        return rows

    def up_group(it, weights, extra):
        partial = to_row(fold_lanes(ku[...] * weights)) * E_GROUP
        for part, row in enumerate(by_part(partial)):
            psend[it, part] = row
            pin[it, my_ty, part] = row
        psend[it, N_TY] = extra
        pin[it, my_ty, N_TY] = extra
        for step in range(1, N_TY):
            send(psend.at[it], pin.at[it, my_ty], p_s.at[it], p_r.at[it], ty=ty_at(step)).start()

    def over_top(it):
        settle_both(pin.at[it, pl.ds(0, N_TY - 1)], (p_s.at[it], p_r.at[it]))
        ufull[it] = jnp.sum(pin[it], axis=0)
        usend[it] = ufull[it, my_ty] + ufull[it, N_TY]
        uin[it, my_tx] = usend[it]
        for step in range(1, N_TX):
            send(usend.at[it], uin.at[it, my_tx], u_s.at[it], u_r.at[it], tx=tx_at(step)).start()

    def across(it):
        settle_both(uin.at[it, pl.ds(0, N_TX - 1)], (u_s.at[it], u_r.at[it]))
        tiles = []
        for tile in range(4):
            total = jnp.where(narrow < TSK, uin[it, 4 * tile], 0.0)
            for k in range(1, 4):
                total = total + pltpu.roll(jnp.where(narrow < TSK, uin[it, 4 * tile + k], 0.0), TSK * k, 1)
            tiles.append(total)
        upper = jnp.concatenate(tiles, axis=1)
        wsend[it] = to_row(fold_lanes(kc[...] * upper)) * E_TOP
        win[it, my_ty] = wsend[it]

    def send_middle(it):
        for step in range(1, N_TY):
            send(wsend.at[it], win.at[it, my_ty], w_s.at[it], w_r.at[it], ty=ty_at(step)).start()

    def down(it):
        settle_both(win.at[it, pl.ds(0, N_TY - 1)], (w_s.at[it], w_r.at[it]))
        middle = to_column(jnp.sum(win[it], axis=0))
        lower = fold_rows(ku[...] * tile_lanes(middle, LDEV * SKEL))
        lower = jnp.sum(lower, axis=0, keepdims=True) * (E_GROUP * A_LEAF * FAR * SLOTS)
        for leaf in range(LDEV):
            weights = lower[:, leaf * SKEL : (leaf + 1) * SKEL]
            for half in range(2):
                row = 2 * leaf + half
                acc[row] = fold_lanes(ka[row] * weights)

    def stretch(it, store, row, form, values, fresh, first):
        width = values.shape[1]
        total = jnp.zeros((8, width - first), F32)
        for start in range(0, HALF, CHUNK):
            rows = pl.ds(start, CHUNK)
            if it == 0:
                tile = jnp.exp2(jnp.dot(taug[row, rows], form, preferred_element_type=F32))
                store[rows] = tile
            else:
                tile = store[rows]
            part = fold_lanes(tile * values)
            if fresh:
                acc[row, rows] = part
            else:
                acc[row, rows] += part
            if first < width:
                total = total + fold_rows(tile[:, first:] * tile_lanes(vb[row, rows], width - first))
        return jnp.sum(total, axis=0, keepdims=True) if first < width else None

    def form_of(wave, index):
        return source_form(pts[wave][index], aux[wave][index])

    def diagonal(it):
        def step(leaf, carry):
            weight = degree(leaf)
            low, high = 2 * leaf, 2 * leaf + 1
            form = None
            if it == 0:
                form = jnp.concatenate(
                    [form_of(wave, MINE + half) for half in (low, high) for wave in range(WAVES)], axis=1
                )
            values = jnp.concatenate([vals[it, MINE + low], vals[it, MINE + high]], axis=1) * weight
            cbuf[pl.ds(QUADS + leaf, 1)] = stretch(it, kd.at[leaf], low, form, values, True, HALF)
            if it == 0:
                form = form[:, HALF:]
            stretch(it, ke.at[leaf], high, form, values[:, HALF:], True, HALF)
            return carry
        lax.fori_loop(0, LDEV, step, 0)

    def slots(it, wave, start, stop):
        part = PARTS[wave]

        def step(row, carry):
            leaf, half = lax.div(row, 2), lax.rem(row, 2)
            forms, values = [], []
            for number in range(SLOTS):
                index, use, unused = slot(leaf, number, half)
                if it == 0:
                    forms.append(form_of(wave, index))
                values.append(vals[it, index][:, STARTS[wave] : STARTS[wave] + PARTS[wave]] * use)
            form = jnp.concatenate(forms, axis=1) if it == 0 else None
            total = stretch(it, kq[wave].at[row], row, form, jnp.concatenate(values, axis=1), False, 0)
            rows = [total[:, number * part : (number + 1) * part] for number in range(SLOTS)]
            rows.append(jnp.zeros((8 - SLOTS, part), F32))
            cbuf[pl.ds(pl.multiple_of(8 * row, 8), 8), STARTS[wave] : STARTS[wave] + part] = jnp.concatenate(rows, axis=0)
            return carry
        lax.fori_loop(start, stop, step, 0)

    def send_back(it):
        table = moh[...].astype(BF16)
        parts = jnp.dot(
            jnp.concatenate([table] * 3, axis=1),
            jnp.concatenate(split3(cbuf[...]), axis=0),
            preferred_element_type=F32,
        )
        for place in range(GAPS):
            zsend[it, place] = parts[8 * place : 8 * place + 8]
        for gap in remote_gaps:
            send(zsend.at[it, gap + REACH], zin.at[it, REACH - gap], z_s.at[it], z_r.at[it], tx=tx_at(gap)).start()

    def rows_of_acc():
        rows = [to_row(acc[half]) for half in range(HALVES)]
        return jnp.concatenate(rows + [jnp.zeros((8 - HALVES, HALF), F32)], axis=0) * (1.0 / SLOTS)

    def near_rows(it):
        return rows_of_acc() + zsend[it, REACH] * (1.0 / SLOTS)

    def near_back(it):
        settle_both(zin.at[it, pl.ds(0, GAPS - 1)], (z_s.at[it], z_r.at[it]))
        total = zin[it, 0]
        for place in range(1, GAPS):
            if place != REACH:
                total = total + zin[it, place]
        return total * (1.0 / SLOTS)

    def own_rows(it):
        return jnp.concatenate([vals[it, MINE + half] for half in range(8)], axis=0)

    def pack(*sums):
        row = jnp.zeros((1, 128), F32)
        for number, value in enumerate(sums):
            row = jnp.where(narrow == SPARE + number, value, row)
        return row

    def unpack(row, count):
        return [jnp.sum(jnp.where(narrow == SPARE + k, row, 0.0), axis=1, keepdims=True) for k in range(count)]

    def sum_first(number, row):
        s_one[number] = row
        s_ty[number, my_ty] = row
        for step in range(1, N_TY):
            send(s_one.at[number], s_ty.at[number, my_ty], a_s.at[number], a_r.at[number], ty=ty_at(step)).start()

    def sum_second(number):
        settle_both(s_ty.at[number, pl.ds(0, N_TY - 1)], (a_s.at[number], a_r.at[number]))
        row = jnp.sum(s_ty[number], axis=0)
        s_two[number] = row
        s_tx[number, my_tx] = row
        for step in range(1, N_TX):
            send(s_two.at[number], s_tx.at[number, my_tx], b_s.at[number], b_r.at[number], tx=tx_at(step)).start()

    def sum_last(number, count):
        settle_both(s_tx.at[number, pl.ds(0, N_TX - 1)], (b_s.at[number], b_r.at[number]))
        return unpack(jnp.sum(s_tx[number], axis=0), count)

    def total_of(tile):
        return jnp.sum(jnp.sum(tile, axis=0, keepdims=True), axis=1, keepdims=True)

    def dot(one, two):
        return total_of(one * two)

    def remote_aux(wave):
        for place in range(GAPS):
            if place != REACH:
                six = pl.ds(8 * place, HALVES)
                aux[wave][six] = aux_of_many(pts[wave][six])

    lax.fori_loop(0, HALVES, own_forms, 0)
    spread(0)
    start = own_rows(0)
    pl.semaphore_wait(barrier, N_TX - 1 + N_TY - 1)

    send_points(0)
    send_top_near()
    send_points(1)
    send_points(2)
    send_values(0)
    weights = up_leaf(0)
    pass_on(0)
    send_points(3)
    send_top_far()
    settle_both(gg.at[pl.ds(0, N_TY - 1)], (g_s.at[0], g_r.at[0]))
    group_targets = row_targets(gg[...].reshape(GSKEL, 128))
    for leaf in range(LDEV):
        ku[:, leaf * SKEL : (leaf + 1) * SKEL] = jnp.exp2(
            jnp.dot(group_targets, skeleton_form(leaf), preferred_element_type=F32)
        )
    up_group(0, weights, jnp.zeros((1, 128), F32))
    pass_on(1)
    diagonal(0)
    pass_on(2)
    over_top(0)
    values_here(0)
    points_here(0)
    remote_aux(0)
    slots(0, 0, 0, 4)
    pass_on(3)
    slots(0, 0, 4, HALVES)
    points_here(1)
    remote_aux(1)
    slots(0, 1, 0, HALVES)
    settle_both(gt.at[pl.ds(0, N_TX - 1)], (g_s.at[1], g_r.at[1]))
    group_sources = row_sources(gt[...].reshape(N_TX * TSK, 128))
    kc[...] = jnp.exp2(
        lax.dot_general(group_targets, group_sources, (((1,), (1,)), ((), ())), preferred_element_type=F32)
    )
    across(0)
    send_middle(0)
    points_here(2)
    remote_aux(2)
    slots(0, 2, 0, HALVES)
    points_here(3)
    remote_aux(3)
    slots(0, 3, 0, HALVES)
    send_back(0)
    own_first = start + near_rows(0)
    down(0)
    first = own_first + rows_of_acc() + near_back(0)
    for half in range(HALVES):
        vals[1, MINE + half] = first[half : half + 1]

    for wave in range(WAVES):
        points_gone(wave)

    send_values(1)
    spread(1)
    up_group(1, up_leaf(1), pack(dot(start, start), dot(start, first), dot(first, first)))
    diagonal(1)
    values_here(1)
    slots(1, 0, 0, 3)
    over_top(1)
    slots(1, 0, 3, HALVES)
    slots(1, 1, 0, HALVES)
    for wave in range(2, WAVES):
        slots(1, wave, 0, HALVES)
    send_back(1)
    own_second = first + near_rows(1)
    across(1)
    norm, curve, square = unpack(jnp.sum(uin[1], axis=0), 3)
    alpha = norm / curve
    beta = (alpha * alpha * square - norm) / norm
    left = start - alpha * first
    direction = left + beta * start
    c_start, c_first = 1.0 + beta, -alpha
    bend = dot(direction, c_start * own_first + c_first * own_second)
    given = jnp.zeros((8, HALF), F32)
    for place in range(GAPS):
        if place != REACH:
            theirs = [
                jnp.concatenate([vals[it, 8 * place + half] for half in range(8)], axis=0) for it in range(2)
            ]
            given = given + (c_start * theirs[0] + c_first * theirs[1]) * (
                c_start * zsend[0, place] + c_first * zsend[1, place]
            )
    top = jnp.zeros((1, 128), F32)
    for part, row in enumerate(by_part(c_start * wsend[0] + c_first * wsend[1])):
        top = top + row * (c_start * ufull[0, part] + c_first * ufull[1, part])
    bend = bend + total_of(given) * (1.0 / SLOTS) + total_of(top) * FAR
    sum_first(0, pack(bend, dot(left, left)))
    send_middle(1)
    from_others = near_back(1)
    sum_second(0)
    down(1)
    far_second = rows_of_acc()
    second = own_second + far_second + from_others
    image = c_start * first + c_first * second
    curve, norm_next = sum_last(0, 2)
    step = norm_next / curve
    x_rows = alpha * start + step * direction
    r_rows = left - step * image
    for half in range(HALVES):
        x_out[pl.ds(half * HALF, HALF)] = x_rows[half]
        r_out[pl.ds(half * HALF, HALF)] = r_rows[half]


def on_device(points, right_side, near_list, leaf_skeleton, top_index):
    vmem = pl.BlockSpec(memory_space=pltpu.VMEM)
    dma = pltpu.SemaphoreType.DMA
    out = jax.ShapeDtypeStruct((HALVES * HALF,), F32)
    solution_field, residual = pl.pallas_call(
        body,
        out_shape=(out, out),
        in_specs=[pl.BlockSpec(memory_space=pl.ANY)] * 5,
        out_specs=(vmem, vmem),
        scratch_shapes=[
            pltpu.VMEM((HALVES * HALF,), F32),
            pltpu.SMEM((LDEV, SLOTS), jnp.int32),
            pltpu.VMEM((LDEV, SKEL), jnp.int32),
            pltpu.SMEM((TSK,), jnp.int32),
            dma((4 + WAVES,)),
            *[pltpu.VMEM((ROWS, D, part), BF16) for part in PARTS],
            *[pltpu.VMEM((ROWS, 16, part), BF16) for part in PARTS],
            pltpu.VMEM((2, ROWS, 1, HALF), F32),
            pltpu.VMEM((HALVES, HALF, 256), BF16),
            pltpu.VMEM((HALVES, HALF, 128), F32),
            pltpu.VMEM((HALVES, HALF, 128), F32),
            *[pltpu.VMEM((HALVES, HALF, SLOTS * part), F32) for part in PARTS],
            pltpu.VMEM((LDEV, HALF, LEAF), F32),
            pltpu.VMEM((LDEV, HALF, HALF), F32),
            pltpu.VMEM((HALVES, HALF, SKEL), F32),
            pltpu.VMEM((GSKEL, LDEV * SKEL), F32),
            pltpu.VMEM((GSKEL, N_TX * TSK), F32),
            pltpu.VMEM((128, HALF), F32),
            pltpu.VMEM((ROWS, 128), F32),
            pltpu.VMEM((2, GAPS, 8, HALF), F32),
            pltpu.VMEM((2, GAPS, 8, HALF), F32),
            pltpu.VMEM((128, LDEV * SKEL), BF16),
            pltpu.VMEM((N_TY, TSK, 128), BF16),
            pltpu.VMEM((N_TX, TSK, 128), BF16),
            pltpu.VMEM((2, N_TY + 1, 1, 128), F32),
            pltpu.VMEM((2, N_TY, N_TY + 1, 1, 128), F32),
            pltpu.VMEM((2, N_TY + 1, 1, 128), F32),
            pltpu.VMEM((2, 1, 128), F32),
            pltpu.VMEM((2, N_TX, 1, 128), F32),
            pltpu.VMEM((2, 1, GSKEL), F32),
            pltpu.VMEM((2, N_TY, 1, GSKEL), F32),
            pltpu.VMEM((1, 1, 128), F32),
            pltpu.VMEM((1, N_TY, 1, 128), F32),
            pltpu.VMEM((1, N_TX, 1, 128), F32),
            pltpu.VMEM((1, 1, 128), F32),
            dma((WAVES,)), dma((WAVES, 3)),
            *[dma((2,))] * 16,
        ],
        compiler_params=pltpu.CompilerParams(
            collective_id=0, has_side_effects=True, vmem_limit_bytes=64 * 1024 * 1024 - 512 * 1024
        ),
        name="ridge_cg",
    )(points, right_side, near_list, leaf_skeleton, top_index)
    return solution_field, residual


def solution(mesh):
    placed = (
        P(None, ("tx", "ty")),
        P(("tx", "ty")),
        P(("tx", "ty"), None),
        P(("tx", "ty"), None),
        P(("tx", "ty")),
    )
    return jax.shard_map(
        on_device,
        mesh=mesh,
        in_specs=placed,
        out_specs=(P(("tx", "ty")), P(("tx", "ty"))),
        check_vma=False,
    )
```

```python
import functools
import math

import jax
import jax.numpy as jnp
from jax import lax
from jax.experimental import pallas as pl
from jax.experimental.pallas import tpu as pltpu
from jax.sharding import PartitionSpec as P

F32 = jnp.float32
BF16 = jnp.bfloat16
HI = lax.Precision.HIGHEST

D = 64
LEAF = 1024
HALF = 512
SKEL = 256
LDEV = 3
HALVES = LDEV * 2
SLOTS = 6
TSK = 32
N_TX = 16
N_TY = 8
GSKEL = TSK * N_TY
REACH = 2
GAPS = 2 * REACH + 1
ROWS = 8 * GAPS
MINE = 8 * REACH
QUADS = 8 * HALVES
SPARE = 64
CHUNK = 128
PARTS = (128, 128, 128, 128)
STARTS = (0, 128, 256, 384)
WAVES = len(PARTS)

SCALE = 2.0 * math.log2(math.e) / 20.0
A_LEAF = 0.25
E_GROUP = LEAF / (LDEV * N_TY * SKEL)
E_TOP = LEAF / (N_TX * GSKEL)
FAR = 32.0


def split3(x):
    high = x.astype(BF16)
    rest = x - high.astype(F32)
    mid = rest.astype(BF16)
    low = (rest - mid.astype(F32)).astype(BF16)
    return high, mid, low


def aux_rows(coords, first):
    wide = coords.astype(F32)
    norm = (-0.5 * SCALE) * jnp.sum(wide * wide, axis=0, keepdims=True)
    high, mid, low = [t.astype(F32) for t in split3(norm)]
    row = lax.broadcasted_iota(jnp.int32, (16, coords.shape[1]), 0)
    lead = 0 if first else 3
    ones = jnp.where((row >= 3 - lead) & (row < 6 - lead), 1.0, 0.0)
    parts = jnp.where(row == lead, high, jnp.where(row == lead + 1, mid, jnp.where(row == lead + 2, low, ones)))
    return parts


def aux_of_many(coords):
    wide = coords.astype(F32)
    norm = (-0.5 * SCALE) * jnp.sum(wide * wide, axis=1, keepdims=True)
    high, mid, low = [t.astype(F32) for t in split3(norm)]
    row = lax.broadcasted_iota(jnp.int32, (coords.shape[0], 16, coords.shape[2]), 1)
    ones = jnp.where(row < 3, 1.0, 0.0)
    parts = jnp.where(row == 3, high, jnp.where(row == 4, mid, jnp.where(row == 5, low, ones)))
    return parts.astype(BF16)


def source_form(coords, aux):
    pad = jnp.zeros((48, coords.shape[1]), BF16)
    return jnp.concatenate([coords, coords, coords, aux, pad], axis=0)


def target_form(coords):
    high, mid, low = split3(coords.astype(F32) * SCALE)
    pad = jnp.zeros((48, coords.shape[1]), F32)
    aux = aux_rows(coords, True)
    stack = jnp.concatenate([high.astype(F32), mid.astype(F32), low.astype(F32), aux, pad], axis=0)
    return stack.T.astype(BF16)


def lane_aux(wide, first):
    norm = (-0.5 * SCALE) * jnp.sum(wide * wide, axis=1, keepdims=True)
    high, mid, low = [t.astype(F32) for t in split3(norm)]
    lane = lax.broadcasted_iota(jnp.int32, wide.shape, 1) - D
    lead = 0 if first else 3
    ones = jnp.where((lane >= 3 - lead) & (lane < 6 - lead), 1.0, 0.0)
    return jnp.where(lane == lead, high, jnp.where(lane == lead + 1, mid, jnp.where(lane == lead + 2, low, ones)))


def row_targets(raw):
    wide = raw.astype(F32)
    high, mid, low = [t.astype(F32) for t in split3(wide * SCALE)]
    left = high + pltpu.roll(mid, D, 1)
    right = low + lane_aux(wide, True)
    return jnp.concatenate([left, right], axis=1).astype(BF16)


def row_sources(raw):
    wide = raw.astype(F32)
    left = wide + pltpu.roll(wide, D, 1)
    right = wide + lane_aux(wide, False)
    return jnp.concatenate([left, right], axis=1).astype(BF16)


def to_row(columns):
    ones = jnp.ones((8, 384), BF16)
    parts = jnp.concatenate(split3(columns), axis=1)
    return lax.dot_general(
        ones, parts, (((1,), (1,)), ((), ())), preferred_element_type=F32
    )[0:1]


def to_column(row):
    parts = []
    for start in range(0, row.shape[1], 128):
        piece = jnp.broadcast_to(row[:, start : start + 128], (128, 128))
        parts.append(piece.T)
    return jnp.concatenate(parts, axis=0) if len(parts) > 1 else parts[0]


def fold_lanes(tile):
    total = tile[:, 0:128]
    for start in range(128, tile.shape[1], 128):
        total = total + tile[:, start : start + 128]
    return total


def fold_rows(tile):
    return jnp.sum(tile.reshape(tile.shape[0] // 8, 8, tile.shape[1]), axis=0)


def tile_lanes(column, width):
    return jnp.concatenate([column] * (width // 128), axis=1)


def body(
    pts_hbm, rhs_hbm, near_hbm, skel_hbm, top_hbm, out,
    rhs_in, near, skel_in, top_in, in_s,
    pts_a, pts_b, pts_c, pts_d, aux_a, aux_b, aux_c, aux_d, vals, taug, vb, acc, kq_a, kq_b, kq_c, kq_d, kd, ke, ka, ku, kc, cbuf, moh,
    zsend, zin, skp, gg, gt, psend, pin, ufull, usend, uin, wsend, win, s_one, s_ty, s_tx, s_two,
    pt_s, pt_r, va_s, va_r, z_s, z_r, g_s, g_r, p_s, p_r, u_s, u_r, w_s, w_r, a_s, a_r, b_s, b_r,
):
    my_tx = lax.axis_index("tx")
    my_ty = lax.axis_index("ty")
    pts = (pts_a, pts_b, pts_c, pts_d)
    aux = (aux_a, aux_b, aux_c, aux_d)
    kq = (kq_a, kq_b, kq_c, kq_d)

    def tx_at(step):
        return lax.rem(my_tx + (step + N_TX), N_TX)

    def ty_at(step):
        return lax.rem(my_ty + (step + N_TY), N_TY)

    def send(src, dst, s_sem, r_sem, **where):
        copy = pltpu.make_async_remote_copy(
            src_ref=src, dst_ref=dst, send_sem=s_sem, recv_sem=r_sem,
            device_id=where, device_id_type=pl.DeviceIdType.MESH,
        )
        return copy

    def settle(space, sem):
        pltpu.make_async_copy(space, space, sem).wait()

    def settle_both(space, pair):
        settle(space, pair[0])
        settle(space, pair[1])

    barrier = pltpu.get_barrier_semaphore()
    for step in range(1, N_TX):
        pl.semaphore_signal(barrier, inc=1, device_id={"tx": tx_at(step)}, device_id_type=pl.DeviceIdType.MESH)
    for step in range(1, N_TY):
        pl.semaphore_signal(barrier, inc=1, device_id={"ty": ty_at(step)}, device_id_type=pl.DeviceIdType.MESH)
    loads = [
        pltpu.make_async_copy(near_hbm, near, in_s.at[0]),
        pltpu.make_async_copy(top_hbm, top_in, in_s.at[1]),
        pltpu.make_async_copy(skel_hbm, skel_in, in_s.at[2]),
        pltpu.make_async_copy(rhs_hbm, rhs_in, in_s.at[3]),
    ]
    for copy in loads:
        copy.start()
    for wave in range(WAVES):
        for half in range(HALVES):
            start = half * HALF + STARTS[wave]
            pltpu.make_async_copy(
                pts_hbm.at[:, pl.ds(start, PARTS[wave])], pts[wave].at[MINE + half], in_s.at[4 + wave]
            ).start()
    for half in range(HALVES, 8):
        vals[0, MINE + half] = jnp.zeros((1, HALF), F32)
        vals[1, MINE + half] = jnp.zeros((1, HALF), F32)
    for copy in loads:
        copy.wait()
    for wave in range(WAVES):
        settle(pts[wave].at[pl.ds(MINE, HALVES)], in_s.at[4 + wave])
    for half in range(HALVES):
        vals[0, MINE + half] = rhs_in[pl.ds(half * HALF, HALF)].reshape(1, HALF)

    remote_gaps = [1, -1, 2, -2]

    def point_copy(wave, number):
        gap = remote_gaps[number]
        source = 8 * (REACH if number < 2 else REACH + gap // 2)
        place = 8 * (gap + REACH)
        return send(
            pts[wave].at[pl.ds(source, HALVES)], pts[wave].at[pl.ds(place, HALVES)],
            pt_s.at[wave], pt_r.at[wave, min(number, 2)], tx=tx_at(-1 if gap > 0 else 1),
        )

    points_out = {}

    def send_points(wave):
        for number in range(2):
            copy = point_copy(wave, number)
            copy.start()
            points_out[wave, number] = copy

    def pass_on(wave):
        for number in range(2):
            points_out[wave, number].wait_recv()
            point_copy(wave, number + 2).start()

    def points_here(wave):
        settle(pts[wave].at[pl.ds(0, 2 * HALVES)], pt_r.at[wave, 2])

    def points_gone(wave):
        settle(pts[wave].at[pl.ds(0, 4 * HALVES)], pt_s.at[wave])

    def send_values(it):
        for gap in remote_gaps:
            place = 8 * (gap + REACH)
            send(
                vals.at[it, pl.ds(MINE, 8)], vals.at[it, pl.ds(place, 8)], va_s.at[it], va_r.at[it], tx=tx_at(-gap)
            ).start()

    def values_here(it):
        four = vals.at[it, pl.ds(0, 8 * (GAPS - 1))]
        settle_both(four, (va_s.at[it], va_r.at[it]))

    def slot(leaf, number, half):
        named = near[leaf, number]
        live = named >= 0
        named = jnp.maximum(named, 0)
        place = lax.rem(lax.div(named, LDEV * N_TY) - my_tx + (N_TX + REACH), N_TX)
        other = lax.rem(named, LDEV)
        same = place == REACH
        itself = live & same & (other == leaf)
        use = live & jnp.logical_not(itself) & (place < GAPS)
        back = jnp.where((place < REACH) | (same & (other < leaf)), 1, 0)
        other_half = half + back - 2 * half * back
        index = jnp.where(use, 8 * place + 2 * other + other_half, MINE)
        return index, jnp.where(use, 1.0, 0.0), jnp.where(live, 1.0, 0.0) + jnp.where(itself, 1.0, 0.0)

    def degree(leaf):
        total = 0.0
        for number in range(SLOTS):
            total = total + slot(leaf, number, 0)[2]
        return total

    sub = lax.broadcasted_iota(jnp.int32, (ROWS, 128), 0)
    lane = lax.broadcasted_iota(jnp.int32, (ROWS, 128), 1)

    def mark(row, table):
        for number in range(SLOTS):
            index, use, unused = slot(lax.div(row, 2), number, lax.rem(row, 2))
            table = jnp.where((lane == 8 * row + number) & (sub == index), use, table)
        return table

    table = lax.fori_loop(0, HALVES, mark, jnp.zeros((ROWS, 128), F32))
    for leaf in range(LDEV):
        table = jnp.where((lane == QUADS + leaf) & (sub == MINE + 2 * leaf + 1), degree(leaf), table)
    moh[...] = table
    cbuf[pl.ds(QUADS, 128 - QUADS)] = jnp.zeros((128 - QUADS, HALF), F32)

    def own_half(half):
        return jnp.concatenate([pts[wave][MINE + half] for wave in range(WAVES)], axis=1)

    def own_forms(half, carry):
        taug[half] = target_form(own_half(half))
        for wave in range(WAVES):
            aux[wave][MINE + half] = aux_rows(pts[wave][MINE + half], False).astype(BF16)
        return carry

    skp[pl.ds(D, 128 - D)] = jnp.zeros((128 - D, LDEV * SKEL), BF16)
    for leaf in range(LDEV):
        chosen = skel_in[leaf : leaf + 1]
        picked = jnp.zeros((D, SKEL), F32)
        for half in range(2):
            place = lax.broadcasted_iota(jnp.int32, (HALF, SKEL), 0) + half * HALF
            hot = jnp.where(place == chosen, 1.0, 0.0).astype(BF16)
            picked = picked + jnp.dot(own_half(2 * leaf + half), hot, preferred_element_type=F32)
        skp[0:D, leaf * SKEL : (leaf + 1) * SKEL] = picked.astype(BF16)
    wide_lane = lax.broadcasted_iota(jnp.int32, (1, LDEV * SKEL), 1)
    hot_rows = [jnp.where(wide_lane == top_in[t], 1.0, 0.0) for t in range(TSK)]
    hot = jnp.concatenate(hot_rows, axis=0).astype(BF16)
    mine_top = lax.dot_general(
        hot, skp[...], (((1,), (1,)), ((), ())), preferred_element_type=F32
    ).astype(BF16)
    gg[my_ty] = mine_top
    gt[my_tx] = mine_top

    def send_top_near():
        for step in range(1, N_TY):
            send(gg.at[my_ty], gg.at[my_ty], g_s.at[0], g_r.at[0], ty=ty_at(step)).start()

    def send_top_far():
        for step in range(1, N_TX):
            send(gt.at[my_tx], gt.at[my_tx], g_s.at[1], g_r.at[1], tx=tx_at(step)).start()

    def spread(it):
        def step(half, carry):
            vb[half] = to_column(vals[it, MINE + half])
            return carry
        lax.fori_loop(0, HALVES, step, 0)

    def skeleton_form(leaf):
        coords = skp[0:D, leaf * SKEL : (leaf + 1) * SKEL]
        return source_form(coords, aux_rows(coords, False).astype(BF16))

    def up_leaf(it):
        parts = []
        for leaf in range(LDEV):
            if it == 0:
                form = skeleton_form(leaf)
            total = jnp.zeros((8, SKEL), F32)
            for half in range(2):
                row = 2 * leaf + half
                if it == 0:
                    ka[row] = jnp.exp2(jnp.dot(taug[row], form, preferred_element_type=F32))
                total = total + fold_rows(ka[row] * tile_lanes(vb[row], SKEL))
            parts.append(jnp.sum(total, axis=0, keepdims=True))
        return jnp.concatenate(parts, axis=1) * A_LEAF

    narrow = lax.broadcasted_iota(jnp.int32, (1, 128), 1)

    def by_part(row):
        rows = []
        for part in range(N_TY):
            tile = row[:, 128 * (part // 4) : 128 * (part // 4) + 128]
            shift = (128 - TSK * (part % 4)) % 128
            if shift:
                tile = pltpu.roll(tile, shift, 1)
            rows.append(jnp.where(narrow < TSK, tile, 0.0))
        return rows

    def up_group(it, weights, extra):
        partial = to_row(fold_lanes(ku[...] * weights)) * E_GROUP
        for part, row in enumerate(by_part(partial)):
            psend[it, part] = row
            pin[it, my_ty, part] = row
        psend[it, N_TY] = extra
        pin[it, my_ty, N_TY] = extra
        for step in range(1, N_TY):
            send(psend.at[it], pin.at[it, my_ty], p_s.at[it], p_r.at[it], ty=ty_at(step)).start()

    def over_top(it):
        settle_both(pin.at[it, pl.ds(0, N_TY - 1)], (p_s.at[it], p_r.at[it]))
        ufull[it] = jnp.sum(pin[it], axis=0)
        usend[it] = ufull[it, my_ty] + ufull[it, N_TY]
        uin[it, my_tx] = usend[it]
        for step in range(1, N_TX):
            send(usend.at[it], uin.at[it, my_tx], u_s.at[it], u_r.at[it], tx=tx_at(step)).start()

    def across(it):
        settle_both(uin.at[it, pl.ds(0, N_TX - 1)], (u_s.at[it], u_r.at[it]))
        tiles = []
        for tile in range(4):
            total = jnp.where(narrow < TSK, uin[it, 4 * tile], 0.0)
            for k in range(1, 4):
                total = total + pltpu.roll(jnp.where(narrow < TSK, uin[it, 4 * tile + k], 0.0), TSK * k, 1)
            tiles.append(total)
        upper = jnp.concatenate(tiles, axis=1)
        wsend[it] = to_row(fold_lanes(kc[...] * upper)) * E_TOP
        win[it, my_ty] = wsend[it]

    def send_middle(it):
        for step in range(1, N_TY):
            send(wsend.at[it], win.at[it, my_ty], w_s.at[it], w_r.at[it], ty=ty_at(step)).start()

    def down(it):
        settle_both(win.at[it, pl.ds(0, N_TY - 1)], (w_s.at[it], w_r.at[it]))
        middle = to_column(jnp.sum(win[it], axis=0))
        lower = fold_rows(ku[...] * tile_lanes(middle, LDEV * SKEL))
        lower = jnp.sum(lower, axis=0, keepdims=True) * (E_GROUP * A_LEAF * FAR * SLOTS)
        for leaf in range(LDEV):
            weights = lower[:, leaf * SKEL : (leaf + 1) * SKEL]
            for half in range(2):
                row = 2 * leaf + half
                acc[row] = fold_lanes(ka[row] * weights)

    def stretch(it, store, row, form, values, fresh, first):
        width = values.shape[1]
        total = jnp.zeros((8, width - first), F32)
        for start in range(0, HALF, CHUNK):
            rows = pl.ds(start, CHUNK)
            if it == 0:
                tile = jnp.exp2(jnp.dot(taug[row, rows], form, preferred_element_type=F32))
                store[rows] = tile
            else:
                tile = store[rows]
            part = fold_lanes(tile * values)
            if fresh:
                acc[row, rows] = part
            else:
                acc[row, rows] += part
            if first < width:
                total = total + fold_rows(tile[:, first:] * tile_lanes(vb[row, rows], width - first))
        return jnp.sum(total, axis=0, keepdims=True) if first < width else None

    def form_of(wave, index):
        return source_form(pts[wave][index], aux[wave][index])

    def diagonal(it):
        def step(leaf, carry):
            weight = degree(leaf)
            low, high = 2 * leaf, 2 * leaf + 1
            form = None
            if it == 0:
                form = jnp.concatenate(
                    [form_of(wave, MINE + half) for half in (low, high) for wave in range(WAVES)], axis=1
                )
            values = jnp.concatenate([vals[it, MINE + low], vals[it, MINE + high]], axis=1) * weight
            cbuf[pl.ds(QUADS + leaf, 1)] = stretch(it, kd.at[leaf], low, form, values, True, HALF)
            if it == 0:
                form = form[:, HALF:]
            stretch(it, ke.at[leaf], high, form, values[:, HALF:], True, HALF)
            return carry
        lax.fori_loop(0, LDEV, step, 0)

    def slots(it, wave, start, stop):
        part = PARTS[wave]

        def step(row, carry):
            leaf, half = lax.div(row, 2), lax.rem(row, 2)
            forms, values = [], []
            for number in range(SLOTS):
                index, use, unused = slot(leaf, number, half)
                if it == 0:
                    forms.append(form_of(wave, index))
                values.append(vals[it, index][:, STARTS[wave] : STARTS[wave] + PARTS[wave]] * use)
            form = jnp.concatenate(forms, axis=1) if it == 0 else None
            total = stretch(it, kq[wave].at[row], row, form, jnp.concatenate(values, axis=1), False, 0)
            rows = [total[:, number * part : (number + 1) * part] for number in range(SLOTS)]
            rows.append(jnp.zeros((8 - SLOTS, part), F32))
            cbuf[pl.ds(pl.multiple_of(8 * row, 8), 8), STARTS[wave] : STARTS[wave] + part] = jnp.concatenate(rows, axis=0)
            return carry
        lax.fori_loop(start, stop, step, 0)

    def send_back(it):
        table = moh[...].astype(BF16)
        parts = jnp.dot(
            jnp.concatenate([table] * 3, axis=1),
            jnp.concatenate(split3(cbuf[...]), axis=0),
            preferred_element_type=F32,
        )
        for place in range(GAPS):
            zsend[it, place] = parts[8 * place : 8 * place + 8]
        for gap in remote_gaps:
            send(zsend.at[it, gap + REACH], zin.at[it, REACH - gap], z_s.at[it], z_r.at[it], tx=tx_at(gap)).start()

    def rows_of_acc():
        rows = [to_row(acc[half]) for half in range(HALVES)]
        return jnp.concatenate(rows + [jnp.zeros((8 - HALVES, HALF), F32)], axis=0) * (1.0 / SLOTS)

    def near_rows(it):
        return rows_of_acc() + zsend[it, REACH] * (1.0 / SLOTS)

    def near_back(it):
        settle_both(zin.at[it, pl.ds(0, GAPS - 1)], (z_s.at[it], z_r.at[it]))
        total = zin[it, 0]
        for place in range(1, GAPS):
            if place != REACH:
                total = total + zin[it, place]
        return total * (1.0 / SLOTS)

    def own_rows(it):
        return jnp.concatenate([vals[it, MINE + half] for half in range(8)], axis=0)

    def pack(*sums):
        row = jnp.zeros((1, 128), F32)
        for number, value in enumerate(sums):
            row = jnp.where(narrow == SPARE + number, value, row)
        return row

    def unpack(row, count):
        return [jnp.sum(jnp.where(narrow == SPARE + k, row, 0.0), axis=1, keepdims=True) for k in range(count)]

    def sum_first(number, row):
        s_one[number] = row
        s_ty[number, my_ty] = row
        for step in range(1, N_TY):
            send(s_one.at[number], s_ty.at[number, my_ty], a_s.at[number], a_r.at[number], ty=ty_at(step)).start()

    def sum_second(number):
        settle_both(s_ty.at[number, pl.ds(0, N_TY - 1)], (a_s.at[number], a_r.at[number]))
        row = jnp.sum(s_ty[number], axis=0)
        s_two[number] = row
        s_tx[number, my_tx] = row
        for step in range(1, N_TX):
            send(s_two.at[number], s_tx.at[number, my_tx], b_s.at[number], b_r.at[number], tx=tx_at(step)).start()

    def sum_last(number, count):
        settle_both(s_tx.at[number, pl.ds(0, N_TX - 1)], (b_s.at[number], b_r.at[number]))
        return unpack(jnp.sum(s_tx[number], axis=0), count)

    def total_of(tile):
        return jnp.sum(jnp.sum(tile, axis=0, keepdims=True), axis=1, keepdims=True)

    def dot(one, two):
        return total_of(one * two)

    def remote_aux(wave):
        for place in range(GAPS):
            if place != REACH:
                six = pl.ds(8 * place, HALVES)
                aux[wave][six] = aux_of_many(pts[wave][six])

    lax.fori_loop(0, HALVES, own_forms, 0)
    spread(0)
    start = own_rows(0)
    pl.semaphore_wait(barrier, N_TX - 1 + N_TY - 1)

    send_points(0)
    send_top_near()
    send_points(1)
    send_points(2)
    send_values(0)
    pass_on(0)
    send_points(3)
    weights = up_leaf(0)
    settle_both(gg.at[pl.ds(0, N_TY - 1)], (g_s.at[0], g_r.at[0]))
    group_targets = row_targets(gg[...].reshape(GSKEL, 128))
    for leaf in range(LDEV):
        ku[:, leaf * SKEL : (leaf + 1) * SKEL] = jnp.exp2(
            jnp.dot(group_targets, skeleton_form(leaf), preferred_element_type=F32)
        )
    up_group(0, weights, jnp.zeros((1, 128), F32))
    pass_on(1)
    diagonal(0)
    pass_on(2)
    over_top(0)
    values_here(0)
    points_here(0)
    remote_aux(0)
    slots(0, 0, 0, 4)
    pass_on(3)
    send_top_far()
    slots(0, 0, 4, HALVES)
    points_here(1)
    remote_aux(1)
    slots(0, 1, 0, HALVES)
    points_here(2)
    remote_aux(2)
    slots(0, 2, 0, HALVES)
    settle_both(gt.at[pl.ds(0, N_TX - 1)], (g_s.at[1], g_r.at[1]))
    group_sources = row_sources(gt[...].reshape(N_TX * TSK, 128))
    kc[...] = jnp.exp2(
        lax.dot_general(group_targets, group_sources, (((1,), (1,)), ((), ())), preferred_element_type=F32)
    )
    across(0)
    send_middle(0)
    points_here(3)
    remote_aux(3)
    slots(0, 3, 0, HALVES)
    send_back(0)
    own_first = start + near_rows(0)
    down(0)
    first = own_first + rows_of_acc() + near_back(0)
    for half in range(HALVES):
        vals[1, MINE + half] = first[half : half + 1]

    for wave in range(WAVES):
        points_gone(wave)

    send_values(1)
    spread(1)
    up_group(1, up_leaf(1), pack(dot(start, start), dot(start, first), dot(first, first)))
    diagonal(1)
    values_here(1)
    slots(1, 0, 0, 3)
    over_top(1)
    slots(1, 0, 3, HALVES)
    slots(1, 1, 0, HALVES)
    for wave in range(2, WAVES):
        slots(1, wave, 0, HALVES)
    send_back(1)
    own_second = first + near_rows(1)
    across(1)
    norm, curve, square = unpack(jnp.sum(uin[1], axis=0), 3)
    alpha = norm / curve
    beta = (alpha * alpha * square - norm) / norm
    left = start - alpha * first
    direction = left + beta * start
    c_start, c_first = 1.0 + beta, -alpha
    bend = dot(direction, c_start * own_first + c_first * own_second)
    given = jnp.zeros((8, HALF), F32)
    for place in range(GAPS):
        if place != REACH:
            theirs = [
                jnp.concatenate([vals[it, 8 * place + half] for half in range(8)], axis=0) for it in range(2)
            ]
            given = given + (c_start * theirs[0] + c_first * theirs[1]) * (
                c_start * zsend[0, place] + c_first * zsend[1, place]
            )
    top = jnp.zeros((1, 128), F32)
    for part, row in enumerate(by_part(c_start * wsend[0] + c_first * wsend[1])):
        top = top + row * (c_start * ufull[0, part] + c_first * ufull[1, part])
    bend = bend + total_of(given) * (1.0 / SLOTS) + total_of(top) * FAR
    sum_first(0, pack(bend, dot(left, left)))
    send_middle(1)
    from_others = near_back(1)
    sum_second(0)
    down(1)
    far_second = rows_of_acc()
    second = own_second + far_second + from_others
    image = c_start * first + c_first * second
    curve, norm_next = sum_last(0, 2)
    step = norm_next / curve
    x_rows = alpha * start + step * direction
    r_rows = left - step * image
    for half in range(HALVES):
        out[pl.ds(half * HALF, HALF)] = x_rows[half]
        out[pl.ds((HALVES + half) * HALF, HALF)] = r_rows[half]


def on_device(points, right_side, near_list, leaf_skeleton, top_index):
    vmem = pl.BlockSpec(memory_space=pltpu.VMEM)
    dma = pltpu.SemaphoreType.DMA
    out = jax.ShapeDtypeStruct((2 * HALVES * HALF,), F32)
    both = pl.pallas_call(
        body,
        out_shape=out,
        in_specs=[pl.BlockSpec(memory_space=pl.ANY)] * 5,
        out_specs=vmem,
        scratch_shapes=[
            pltpu.VMEM((HALVES * HALF,), F32),
            pltpu.SMEM((LDEV, SLOTS), jnp.int32),
            pltpu.VMEM((LDEV, SKEL), jnp.int32),
            pltpu.SMEM((TSK,), jnp.int32),
            dma((4 + WAVES,)),
            *[pltpu.VMEM((ROWS, D, part), BF16) for part in PARTS],
            *[pltpu.VMEM((ROWS, 16, part), BF16) for part in PARTS],
            pltpu.VMEM((2, ROWS, 1, HALF), F32),
            pltpu.VMEM((HALVES, HALF, 256), BF16),
            pltpu.VMEM((HALVES, HALF, 128), F32),
            pltpu.VMEM((HALVES, HALF, 128), F32),
            *[pltpu.VMEM((HALVES, HALF, SLOTS * part), F32) for part in PARTS],
            pltpu.VMEM((LDEV, HALF, LEAF), F32),
            pltpu.VMEM((LDEV, HALF, HALF), F32),
            pltpu.VMEM((HALVES, HALF, SKEL), F32),
            pltpu.VMEM((GSKEL, LDEV * SKEL), F32),
            pltpu.VMEM((GSKEL, N_TX * TSK), F32),
            pltpu.VMEM((128, HALF), F32),
            pltpu.VMEM((ROWS, 128), F32),
            pltpu.VMEM((2, GAPS, 8, HALF), F32),
            pltpu.VMEM((2, GAPS, 8, HALF), F32),
            pltpu.VMEM((128, LDEV * SKEL), BF16),
            pltpu.VMEM((N_TY, TSK, 128), BF16),
            pltpu.VMEM((N_TX, TSK, 128), BF16),
            pltpu.VMEM((2, N_TY + 1, 1, 128), F32),
            pltpu.VMEM((2, N_TY, N_TY + 1, 1, 128), F32),
            pltpu.VMEM((2, N_TY + 1, 1, 128), F32),
            pltpu.VMEM((2, 1, 128), F32),
            pltpu.VMEM((2, N_TX, 1, 128), F32),
            pltpu.VMEM((2, 1, GSKEL), F32),
            pltpu.VMEM((2, N_TY, 1, GSKEL), F32),
            pltpu.VMEM((1, 1, 128), F32),
            pltpu.VMEM((1, N_TY, 1, 128), F32),
            pltpu.VMEM((1, N_TX, 1, 128), F32),
            pltpu.VMEM((1, 1, 128), F32),
            dma((WAVES,)), dma((WAVES, 3)),
            *[dma((2,))] * 16,
        ],
        compiler_params=pltpu.CompilerParams(
            collective_id=0, has_side_effects=True, vmem_limit_bytes=64 * 1024 * 1024 - 512 * 1024
        ),
        name="ridge_cg",
    )(points, right_side, near_list, leaf_skeleton, top_index)
    return both[: HALVES * HALF], both[HALVES * HALF :]


def solution(mesh):
    placed = (
        P(None, ("tx", "ty")),
        P(("tx", "ty")),
        P(("tx", "ty"), None),
        P(("tx", "ty"), None),
        P(("tx", "ty")),
    )
    return jax.shard_map(
        on_device,
        mesh=mesh,
        in_specs=placed,
        out_specs=(P(("tx", "ty")), P(("tx", "ty"))),
        check_vma=False,
    )
```

```python
import functools
import math

import jax
import jax.numpy as jnp
from jax import lax
from jax.experimental import pallas as pl
from jax.experimental.pallas import tpu as pltpu
from jax.sharding import PartitionSpec as P

F32 = jnp.float32
BF16 = jnp.bfloat16
HI = lax.Precision.HIGHEST

D = 64
LEAF = 1024
HALF = 512
SKEL = 256
LDEV = 3
HALVES = LDEV * 2
SLOTS = 6
TSK = 32
N_TX = 16
N_TY = 8
GSKEL = TSK * N_TY
REACH = 2
GAPS = 2 * REACH + 1
ROWS = 8 * GAPS
MINE = 8 * REACH
QUADS = 8 * HALVES
SPARE = 64
CHUNK = 128
PARTS = (128, 128, 128, 128)
STARTS = (0, 128, 256, 384)
WAVES = len(PARTS)

SCALE = 2.0 * math.log2(math.e) / 20.0
A_LEAF = 0.25
E_GROUP = LEAF / (LDEV * N_TY * SKEL)
E_TOP = LEAF / (N_TX * GSKEL)
FAR = 32.0


def split3(x):
    high = x.astype(BF16)
    rest = x - high.astype(F32)
    mid = rest.astype(BF16)
    low = (rest - mid.astype(F32)).astype(BF16)
    return high, mid, low


def aux_rows(coords, first):
    wide = coords.astype(F32)
    norm = (-0.5 * SCALE) * jnp.sum(wide * wide, axis=0, keepdims=True)
    high, mid, low = [t.astype(F32) for t in split3(norm)]
    row = lax.broadcasted_iota(jnp.int32, (16, coords.shape[1]), 0)
    lead = 0 if first else 3
    ones = jnp.where((row >= 3 - lead) & (row < 6 - lead), 1.0, 0.0)
    parts = jnp.where(row == lead, high, jnp.where(row == lead + 1, mid, jnp.where(row == lead + 2, low, ones)))
    return parts


def aux_of_many(coords):
    wide = coords.astype(F32)
    norm = (-0.5 * SCALE) * jnp.sum(wide * wide, axis=1, keepdims=True)
    high, mid, low = [t.astype(F32) for t in split3(norm)]
    row = lax.broadcasted_iota(jnp.int32, (coords.shape[0], 16, coords.shape[2]), 1)
    ones = jnp.where(row < 3, 1.0, 0.0)
    parts = jnp.where(row == 3, high, jnp.where(row == 4, mid, jnp.where(row == 5, low, ones)))
    return parts.astype(BF16)


def source_form(coords, aux):
    pad = jnp.zeros((48, coords.shape[1]), BF16)
    return jnp.concatenate([coords, coords, coords, aux, pad], axis=0)


def target_form(coords):
    high, mid, low = split3(coords.astype(F32) * SCALE)
    pad = jnp.zeros((48, coords.shape[1]), F32)
    aux = aux_rows(coords, True)
    stack = jnp.concatenate([high.astype(F32), mid.astype(F32), low.astype(F32), aux, pad], axis=0)
    return stack.T.astype(BF16)


def lane_aux(wide, first):
    norm = (-0.5 * SCALE) * jnp.sum(wide * wide, axis=1, keepdims=True)
    high, mid, low = [t.astype(F32) for t in split3(norm)]
    lane = lax.broadcasted_iota(jnp.int32, wide.shape, 1) - D
    lead = 0 if first else 3
    ones = jnp.where((lane >= 3 - lead) & (lane < 6 - lead), 1.0, 0.0)
    return jnp.where(lane == lead, high, jnp.where(lane == lead + 1, mid, jnp.where(lane == lead + 2, low, ones)))


def row_targets(raw):
    wide = raw.astype(F32)
    high, mid, low = [t.astype(F32) for t in split3(wide * SCALE)]
    left = high + pltpu.roll(mid, D, 1)
    right = low + lane_aux(wide, True)
    return jnp.concatenate([left, right], axis=1).astype(BF16)


def row_sources(raw):
    wide = raw.astype(F32)
    left = wide + pltpu.roll(wide, D, 1)
    right = wide + lane_aux(wide, False)
    return jnp.concatenate([left, right], axis=1).astype(BF16)


def to_row(columns):
    ones = jnp.ones((8, 384), BF16)
    parts = jnp.concatenate(split3(columns), axis=1)
    return lax.dot_general(
        ones, parts, (((1,), (1,)), ((), ())), preferred_element_type=F32
    )[0:1]


def to_column(row):
    parts = []
    for start in range(0, row.shape[1], 128):
        piece = jnp.broadcast_to(row[:, start : start + 128], (128, 128))
        parts.append(piece.T)
    return jnp.concatenate(parts, axis=0) if len(parts) > 1 else parts[0]


def fold_lanes(tile):
    total = tile[:, 0:128]
    for start in range(128, tile.shape[1], 128):
        total = total + tile[:, start : start + 128]
    return total


def fold_rows(tile):
    return jnp.sum(tile.reshape(tile.shape[0] // 8, 8, tile.shape[1]), axis=0)


def tile_lanes(column, width):
    return jnp.concatenate([column] * (width // 128), axis=1)


def body(
    pts_hbm, rhs_hbm, near_hbm, skel_hbm, top_hbm, out,
    rhs_in, near, skel_in, top_in, in_s,
    pts_a, pts_b, pts_c, pts_d, aux_a, aux_b, aux_c, aux_d, vals, taug, vb, acc, kq_a, kq_b, kq_c, kq_d, kd, ke, ka, ku, kc, cbuf, moh,
    zsend, zin, skp, gg, gt, psend, pin, ufull, usend, uin, wsend, win, s_one, s_ty, s_tx, s_two,
    pt_s, pt_r, va_s, va_r, z_s, z_r, g_s, g_r, p_s, p_r, u_s, u_r, w_s, w_r, a_s, a_r, b_s, b_r,
):
    my_tx = lax.axis_index("tx")
    my_ty = lax.axis_index("ty")
    pts = (pts_a, pts_b, pts_c, pts_d)
    aux = (aux_a, aux_b, aux_c, aux_d)
    kq = (kq_a, kq_b, kq_c, kq_d)

    def tx_at(step):
        return lax.rem(my_tx + (step + N_TX), N_TX)

    def ty_at(step):
        return lax.rem(my_ty + (step + N_TY), N_TY)

    def send(src, dst, s_sem, r_sem, **where):
        copy = pltpu.make_async_remote_copy(
            src_ref=src, dst_ref=dst, send_sem=s_sem, recv_sem=r_sem,
            device_id=where, device_id_type=pl.DeviceIdType.MESH,
        )
        return copy

    def settle(space, sem):
        pltpu.make_async_copy(space, space, sem).wait()

    def settle_both(space, pair):
        settle(space, pair[0])
        settle(space, pair[1])

    barrier = pltpu.get_barrier_semaphore()
    for step in range(1, N_TX):
        pl.semaphore_signal(barrier, inc=1, device_id={"tx": tx_at(step)}, device_id_type=pl.DeviceIdType.MESH)
    for step in range(1, N_TY):
        pl.semaphore_signal(barrier, inc=1, device_id={"ty": ty_at(step)}, device_id_type=pl.DeviceIdType.MESH)
    loads = [
        pltpu.make_async_copy(near_hbm, near, in_s.at[0]),
        pltpu.make_async_copy(top_hbm, top_in, in_s.at[1]),
        pltpu.make_async_copy(skel_hbm, skel_in, in_s.at[2]),
        pltpu.make_async_copy(rhs_hbm, rhs_in, in_s.at[3]),
    ]
    for copy in loads:
        copy.start()
    for wave in range(WAVES):
        for half in range(HALVES):
            start = half * HALF + STARTS[wave]
            pltpu.make_async_copy(
                pts_hbm.at[:, pl.ds(start, PARTS[wave])], pts[wave].at[MINE + half], in_s.at[4 + wave]
            ).start()
    for half in range(HALVES, 8):
        for place in range(GAPS):
            vals[0, 8 * place + half] = jnp.zeros((1, HALF), F32)
            vals[1, 8 * place + half] = jnp.zeros((1, HALF), F32)
    for copy in loads:
        copy.wait()
    for wave in range(WAVES):
        settle(pts[wave].at[pl.ds(MINE, HALVES)], in_s.at[4 + wave])
    for half in range(HALVES):
        vals[0, MINE + half] = rhs_in[pl.ds(half * HALF, HALF)].reshape(1, HALF)

    remote_gaps = [1, -1, 2, -2]

    def point_copy(wave, number):
        gap = remote_gaps[number]
        source = 8 * (REACH if number < 2 else REACH + gap // 2)
        place = 8 * (gap + REACH)
        return send(
            pts[wave].at[pl.ds(source, HALVES)], pts[wave].at[pl.ds(place, HALVES)],
            pt_s.at[wave], pt_r.at[wave, min(number, 2)], tx=tx_at(-1 if gap > 0 else 1),
        )

    points_out = {}

    def send_points(wave):
        for number in range(2):
            copy = point_copy(wave, number)
            copy.start()
            points_out[wave, number] = copy

    def pass_on(wave):
        for number in range(2):
            points_out[wave, number].wait_recv()
            point_copy(wave, number + 2).start()

    def points_here(wave):
        settle(pts[wave].at[pl.ds(0, 2 * HALVES)], pt_r.at[wave, 2])

    def points_gone(wave):
        settle(pts[wave].at[pl.ds(0, 4 * HALVES)], pt_s.at[wave])

    def send_values(it):
        for gap in remote_gaps:
            place = 8 * (gap + REACH)
            send(
                vals.at[it, pl.ds(MINE, HALVES)], vals.at[it, pl.ds(place, HALVES)], va_s.at[it], va_r.at[it], tx=tx_at(-gap)
            ).start()

    def values_here(it):
        four = vals.at[it, pl.ds(0, HALVES * (GAPS - 1))]
        settle_both(four, (va_s.at[it], va_r.at[it]))

    def slot(leaf, number, half):
        named = near[leaf, number]
        live = named >= 0
        named = jnp.maximum(named, 0)
        place = lax.rem(lax.div(named, LDEV * N_TY) - my_tx + (N_TX + REACH), N_TX)
        other = lax.rem(named, LDEV)
        same = place == REACH
        itself = live & same & (other == leaf)
        use = live & jnp.logical_not(itself) & (place < GAPS)
        back = jnp.where((place < REACH) | (same & (other < leaf)), 1, 0)
        other_half = half + back - 2 * half * back
        index = jnp.where(use, 8 * place + 2 * other + other_half, MINE)
        return index, jnp.where(use, 1.0, 0.0), jnp.where(live, 1.0, 0.0) + jnp.where(itself, 1.0, 0.0)

    def degree(leaf):
        total = 0.0
        for number in range(SLOTS):
            total = total + slot(leaf, number, 0)[2]
        return total

    sub = lax.broadcasted_iota(jnp.int32, (ROWS, 128), 0)
    lane = lax.broadcasted_iota(jnp.int32, (ROWS, 128), 1)

    def mark(row, table):
        for number in range(SLOTS):
            index, use, unused = slot(lax.div(row, 2), number, lax.rem(row, 2))
            table = jnp.where((lane == 8 * row + number) & (sub == index), use, table)
        return table

    table = lax.fori_loop(0, HALVES, mark, jnp.zeros((ROWS, 128), F32))
    for leaf in range(LDEV):
        table = jnp.where((lane == QUADS + leaf) & (sub == MINE + 2 * leaf + 1), degree(leaf), table)
    moh[...] = table
    cbuf[pl.ds(QUADS, 128 - QUADS)] = jnp.zeros((128 - QUADS, HALF), F32)

    def own_half(half):
        return jnp.concatenate([pts[wave][MINE + half] for wave in range(WAVES)], axis=1)

    def own_forms(half, carry):
        taug[half] = target_form(own_half(half))
        for wave in range(WAVES):
            aux[wave][MINE + half] = aux_rows(pts[wave][MINE + half], False).astype(BF16)
        return carry

    skp[pl.ds(D, 128 - D)] = jnp.zeros((128 - D, LDEV * SKEL), BF16)
    for leaf in range(LDEV):
        chosen = skel_in[leaf : leaf + 1]
        picked = jnp.zeros((D, SKEL), F32)
        for half in range(2):
            place = lax.broadcasted_iota(jnp.int32, (HALF, SKEL), 0) + half * HALF
            hot = jnp.where(place == chosen, 1.0, 0.0).astype(BF16)
            picked = picked + jnp.dot(own_half(2 * leaf + half), hot, preferred_element_type=F32)
        skp[0:D, leaf * SKEL : (leaf + 1) * SKEL] = picked.astype(BF16)
    wide_lane = lax.broadcasted_iota(jnp.int32, (1, LDEV * SKEL), 1)
    hot_rows = [jnp.where(wide_lane == top_in[t], 1.0, 0.0) for t in range(TSK)]
    hot = jnp.concatenate(hot_rows, axis=0).astype(BF16)
    mine_top = lax.dot_general(
        hot, skp[...], (((1,), (1,)), ((), ())), preferred_element_type=F32
    ).astype(BF16)
    gg[my_ty] = mine_top
    gt[my_tx] = mine_top

    def send_top_near():
        for step in range(1, N_TY):
            send(gg.at[my_ty], gg.at[my_ty], g_s.at[0], g_r.at[0], ty=ty_at(step)).start()

    def send_top_far():
        for step in range(1, N_TX):
            send(gt.at[my_tx], gt.at[my_tx], g_s.at[1], g_r.at[1], tx=tx_at(step)).start()

    def spread(it):
        def step(half, carry):
            vb[half] = to_column(vals[it, MINE + half])
            return carry
        lax.fori_loop(0, HALVES, step, 0)

    def skeleton_form(leaf):
        coords = skp[0:D, leaf * SKEL : (leaf + 1) * SKEL]
        return source_form(coords, aux_rows(coords, False).astype(BF16))

    def up_leaf(it):
        parts = []
        for leaf in range(LDEV):
            if it == 0:
                form = skeleton_form(leaf)
            total = jnp.zeros((8, SKEL), F32)
            for half in range(2):
                row = 2 * leaf + half
                if it == 0:
                    ka[row] = jnp.exp2(jnp.dot(taug[row], form, preferred_element_type=F32))
                total = total + fold_rows(ka[row] * tile_lanes(vb[row], SKEL))
            parts.append(jnp.sum(total, axis=0, keepdims=True))
        return jnp.concatenate(parts, axis=1) * A_LEAF

    narrow = lax.broadcasted_iota(jnp.int32, (1, 128), 1)

    def by_part(row):
        rows = []
        for part in range(N_TY):
            tile = row[:, 128 * (part // 4) : 128 * (part // 4) + 128]
            shift = (128 - TSK * (part % 4)) % 128
            if shift:
                tile = pltpu.roll(tile, shift, 1)
            rows.append(jnp.where(narrow < TSK, tile, 0.0))
        return rows

    def up_group(it, weights, extra):
        partial = to_row(fold_lanes(ku[...] * weights)) * E_GROUP
        for part, row in enumerate(by_part(partial)):
            psend[it, part] = row
            pin[it, my_ty, part] = row
        psend[it, N_TY] = extra
        pin[it, my_ty, N_TY] = extra
        for step in range(1, N_TY):
            send(psend.at[it], pin.at[it, my_ty], p_s.at[it], p_r.at[it], ty=ty_at(step)).start()

    def over_top(it):
        settle_both(pin.at[it, pl.ds(0, N_TY - 1)], (p_s.at[it], p_r.at[it]))
        ufull[it] = jnp.sum(pin[it], axis=0)
        usend[it] = ufull[it, my_ty] + ufull[it, N_TY]
        uin[it, my_tx] = usend[it]
        for step in range(1, N_TX):
            send(usend.at[it], uin.at[it, my_tx], u_s.at[it], u_r.at[it], tx=tx_at(step)).start()

    def across(it):
        settle_both(uin.at[it, pl.ds(0, N_TX - 1)], (u_s.at[it], u_r.at[it]))
        tiles = []
        for tile in range(4):
            total = jnp.where(narrow < TSK, uin[it, 4 * tile], 0.0)
            for k in range(1, 4):
                total = total + pltpu.roll(jnp.where(narrow < TSK, uin[it, 4 * tile + k], 0.0), TSK * k, 1)
            tiles.append(total)
        upper = jnp.concatenate(tiles, axis=1)
        wsend[it] = to_row(fold_lanes(kc[...] * upper)) * E_TOP
        win[it, my_ty] = wsend[it]

    def send_middle(it):
        for step in range(1, N_TY):
            send(wsend.at[it], win.at[it, my_ty], w_s.at[it], w_r.at[it], ty=ty_at(step)).start()

    def down(it):
        settle_both(win.at[it, pl.ds(0, N_TY - 1)], (w_s.at[it], w_r.at[it]))
        middle = to_column(jnp.sum(win[it], axis=0))
        lower = fold_rows(ku[...] * tile_lanes(middle, LDEV * SKEL))
        lower = jnp.sum(lower, axis=0, keepdims=True) * (E_GROUP * A_LEAF * FAR * SLOTS)
        for leaf in range(LDEV):
            weights = lower[:, leaf * SKEL : (leaf + 1) * SKEL]
            for half in range(2):
                row = 2 * leaf + half
                acc[row] = fold_lanes(ka[row] * weights)

    def stretch(it, store, row, form, values, fresh, first):
        width = values.shape[1]
        total = jnp.zeros((8, width - first), F32)
        for start in range(0, HALF, CHUNK):
            rows = pl.ds(start, CHUNK)
            if it == 0:
                tile = jnp.exp2(jnp.dot(taug[row, rows], form, preferred_element_type=F32))
                store[rows] = tile
            else:
                tile = store[rows]
            part = fold_lanes(tile * values)
            if fresh:
                acc[row, rows] = part
            else:
                acc[row, rows] += part
            if first < width:
                total = total + fold_rows(tile[:, first:] * tile_lanes(vb[row, rows], width - first))
        return jnp.sum(total, axis=0, keepdims=True) if first < width else None

    def form_of(wave, index):
        return source_form(pts[wave][index], aux[wave][index])

    def diagonal(it):
        def step(leaf, carry):
            weight = degree(leaf)
            low, high = 2 * leaf, 2 * leaf + 1
            form = None
            if it == 0:
                form = jnp.concatenate(
                    [form_of(wave, MINE + half) for half in (low, high) for wave in range(WAVES)], axis=1
                )
            values = jnp.concatenate([vals[it, MINE + low], vals[it, MINE + high]], axis=1) * weight
            cbuf[pl.ds(QUADS + leaf, 1)] = stretch(it, kd.at[leaf], low, form, values, True, HALF)
            if it == 0:
                form = form[:, HALF:]
            stretch(it, ke.at[leaf], high, form, values[:, HALF:], True, HALF)
            return carry
        lax.fori_loop(0, LDEV, step, 0)

    def slots(it, wave, start, stop):
        part = PARTS[wave]

        def step(row, carry):
            leaf, half = lax.div(row, 2), lax.rem(row, 2)
            forms, values = [], []
            for number in range(SLOTS):
                index, use, unused = slot(leaf, number, half)
                if it == 0:
                    forms.append(form_of(wave, index))
                values.append(vals[it, index][:, STARTS[wave] : STARTS[wave] + PARTS[wave]] * use)
            form = jnp.concatenate(forms, axis=1) if it == 0 else None
            total = stretch(it, kq[wave].at[row], row, form, jnp.concatenate(values, axis=1), False, 0)
            rows = [total[:, number * part : (number + 1) * part] for number in range(SLOTS)]
            rows.append(jnp.zeros((8 - SLOTS, part), F32))
            cbuf[pl.ds(pl.multiple_of(8 * row, 8), 8), STARTS[wave] : STARTS[wave] + part] = jnp.concatenate(rows, axis=0)
            return carry
        lax.fori_loop(start, stop, step, 0)

    def send_back(it):
        table = moh[...].astype(BF16)
        parts = jnp.dot(
            jnp.concatenate([table] * 3, axis=1),
            jnp.concatenate(split3(cbuf[...]), axis=0),
            preferred_element_type=F32,
        )
        for place in range(GAPS):
            zsend[it, place] = parts[8 * place : 8 * place + 8]
        for gap in remote_gaps:
            send(zsend.at[it, gap + REACH], zin.at[it, REACH - gap], z_s.at[it], z_r.at[it], tx=tx_at(gap)).start()

    def rows_of_acc():
        rows = [to_row(acc[half]) for half in range(HALVES)]
        return jnp.concatenate(rows + [jnp.zeros((8 - HALVES, HALF), F32)], axis=0) * (1.0 / SLOTS)

    def near_rows(it):
        return rows_of_acc() + zsend[it, REACH] * (1.0 / SLOTS)

    def near_back(it):
        settle_both(zin.at[it, pl.ds(0, GAPS - 1)], (z_s.at[it], z_r.at[it]))
        total = zin[it, 0]
        for place in range(1, GAPS):
            if place != REACH:
                total = total + zin[it, place]
        return total * (1.0 / SLOTS)

    def own_rows(it):
        return jnp.concatenate([vals[it, MINE + half] for half in range(8)], axis=0)

    def pack(*sums):
        row = jnp.zeros((1, 128), F32)
        for number, value in enumerate(sums):
            row = jnp.where(narrow == SPARE + number, value, row)
        return row

    def unpack(row, count):
        return [jnp.sum(jnp.where(narrow == SPARE + k, row, 0.0), axis=1, keepdims=True) for k in range(count)]

    def sum_first(number, row):
        s_one[number] = row
        s_ty[number, my_ty] = row
        for step in range(1, N_TY):
            send(s_one.at[number], s_ty.at[number, my_ty], a_s.at[number], a_r.at[number], ty=ty_at(step)).start()

    def sum_second(number):
        settle_both(s_ty.at[number, pl.ds(0, N_TY - 1)], (a_s.at[number], a_r.at[number]))
        row = jnp.sum(s_ty[number], axis=0)
        s_two[number] = row
        s_tx[number, my_tx] = row
        for step in range(1, N_TX):
            send(s_two.at[number], s_tx.at[number, my_tx], b_s.at[number], b_r.at[number], tx=tx_at(step)).start()

    def sum_last(number, count):
        settle_both(s_tx.at[number, pl.ds(0, N_TX - 1)], (b_s.at[number], b_r.at[number]))
        return unpack(jnp.sum(s_tx[number], axis=0), count)

    def total_of(tile):
        return jnp.sum(jnp.sum(tile, axis=0, keepdims=True), axis=1, keepdims=True)

    def dot(one, two):
        return total_of(one * two)

    def remote_aux(wave):
        for place in range(GAPS):
            if place != REACH:
                six = pl.ds(8 * place, HALVES)
                aux[wave][six] = aux_of_many(pts[wave][six])

    lax.fori_loop(0, HALVES, own_forms, 0)
    spread(0)
    start = own_rows(0)
    pl.semaphore_wait(barrier, N_TX - 1 + N_TY - 1)

    send_points(0)
    send_top_near()
    send_points(1)
    send_points(2)
    send_values(0)
    pass_on(0)
    send_points(3)
    weights = up_leaf(0)
    settle_both(gg.at[pl.ds(0, N_TY - 1)], (g_s.at[0], g_r.at[0]))
    group_targets = row_targets(gg[...].reshape(GSKEL, 128))
    for leaf in range(LDEV):
        ku[:, leaf * SKEL : (leaf + 1) * SKEL] = jnp.exp2(
            jnp.dot(group_targets, skeleton_form(leaf), preferred_element_type=F32)
        )
    up_group(0, weights, jnp.zeros((1, 128), F32))
    pass_on(1)
    diagonal(0)
    pass_on(2)
    over_top(0)
    values_here(0)
    points_here(0)
    remote_aux(0)
    slots(0, 0, 0, 4)
    pass_on(3)
    send_top_far()
    slots(0, 0, 4, HALVES)
    points_here(1)
    remote_aux(1)
    slots(0, 1, 0, HALVES)
    points_here(2)
    remote_aux(2)
    slots(0, 2, 0, 3)
    settle_both(gt.at[pl.ds(0, N_TX - 1)], (g_s.at[1], g_r.at[1]))
    group_sources = row_sources(gt[...].reshape(N_TX * TSK, 128))
    kc[...] = jnp.exp2(
        lax.dot_general(group_targets, group_sources, (((1,), (1,)), ((), ())), preferred_element_type=F32)
    )
    across(0)
    send_middle(0)
    slots(0, 2, 3, HALVES)
    points_here(3)
    remote_aux(3)
    slots(0, 3, 0, HALVES)
    send_back(0)
    own_first = start + near_rows(0)
    down(0)
    first = own_first + rows_of_acc() + near_back(0)
    for half in range(HALVES):
        vals[1, MINE + half] = first[half : half + 1]

    for wave in range(WAVES):
        points_gone(wave)

    send_values(1)
    spread(1)
    up_group(1, up_leaf(1), pack(dot(start, start), dot(start, first), dot(first, first)))
    diagonal(1)
    values_here(1)
    slots(1, 0, 0, 3)
    over_top(1)
    slots(1, 0, 3, HALVES)
    slots(1, 1, 0, HALVES)
    for wave in range(2, WAVES):
        slots(1, wave, 0, HALVES)
    send_back(1)
    own_second = first + near_rows(1)
    across(1)
    norm, curve, square = unpack(jnp.sum(uin[1], axis=0), 3)
    alpha = norm / curve
    beta = (alpha * alpha * square - norm) / norm
    left = start - alpha * first
    direction = left + beta * start
    c_start, c_first = 1.0 + beta, -alpha
    bend = dot(direction, c_start * own_first + c_first * own_second)
    given = jnp.zeros((8, HALF), F32)
    for place in range(GAPS):
        if place != REACH:
            theirs = [
                jnp.concatenate([vals[it, 8 * place + half] for half in range(8)], axis=0) for it in range(2)
            ]
            given = given + (c_start * theirs[0] + c_first * theirs[1]) * (
                c_start * zsend[0, place] + c_first * zsend[1, place]
            )
    top = jnp.zeros((1, 128), F32)
    for part, row in enumerate(by_part(c_start * wsend[0] + c_first * wsend[1])):
        top = top + row * (c_start * ufull[0, part] + c_first * ufull[1, part])
    bend = bend + total_of(given) * (1.0 / SLOTS) + total_of(top) * FAR
    sum_first(0, pack(bend, dot(left, left)))
    send_middle(1)
    from_others = near_back(1)
    sum_second(0)
    down(1)
    far_second = rows_of_acc()
    second = own_second + far_second + from_others
    image = c_start * first + c_first * second
    curve, norm_next = sum_last(0, 2)
    step = norm_next / curve
    x_rows = alpha * start + step * direction
    r_rows = left - step * image
    for half in range(HALVES):
        out[pl.ds(half * HALF, HALF)] = x_rows[half]
        out[pl.ds((HALVES + half) * HALF, HALF)] = r_rows[half]


def on_device(points, right_side, near_list, leaf_skeleton, top_index):
    vmem = pl.BlockSpec(memory_space=pltpu.VMEM)
    dma = pltpu.SemaphoreType.DMA
    out = jax.ShapeDtypeStruct((2 * HALVES * HALF,), F32)
    both = pl.pallas_call(
        body,
        out_shape=out,
        in_specs=[pl.BlockSpec(memory_space=pl.ANY)] * 5,
        out_specs=vmem,
        scratch_shapes=[
            pltpu.VMEM((HALVES * HALF,), F32),
            pltpu.SMEM((LDEV, SLOTS), jnp.int32),
            pltpu.VMEM((LDEV, SKEL), jnp.int32),
            pltpu.SMEM((TSK,), jnp.int32),
            dma((4 + WAVES,)),
            *[pltpu.VMEM((ROWS, D, part), BF16) for part in PARTS],
            *[pltpu.VMEM((ROWS, 16, part), BF16) for part in PARTS],
            pltpu.VMEM((2, ROWS, 1, HALF), F32),
            pltpu.VMEM((HALVES, HALF, 256), BF16),
            pltpu.VMEM((HALVES, HALF, 128), F32),
            pltpu.VMEM((HALVES, HALF, 128), F32),
            *[pltpu.VMEM((HALVES, HALF, SLOTS * part), F32) for part in PARTS],
            pltpu.VMEM((LDEV, HALF, LEAF), F32),
            pltpu.VMEM((LDEV, HALF, HALF), F32),
            pltpu.VMEM((HALVES, HALF, SKEL), F32),
            pltpu.VMEM((GSKEL, LDEV * SKEL), F32),
            pltpu.VMEM((GSKEL, N_TX * TSK), F32),
            pltpu.VMEM((128, HALF), F32),
            pltpu.VMEM((ROWS, 128), F32),
            pltpu.VMEM((2, GAPS, 8, HALF), F32),
            pltpu.VMEM((2, GAPS, 8, HALF), F32),
            pltpu.VMEM((128, LDEV * SKEL), BF16),
            pltpu.VMEM((N_TY, TSK, 128), BF16),
            pltpu.VMEM((N_TX, TSK, 128), BF16),
            pltpu.VMEM((2, N_TY + 1, 1, 128), F32),
            pltpu.VMEM((2, N_TY, N_TY + 1, 1, 128), F32),
            pltpu.VMEM((2, N_TY + 1, 1, 128), F32),
            pltpu.VMEM((2, 1, 128), F32),
            pltpu.VMEM((2, N_TX, 1, 128), F32),
            pltpu.VMEM((2, 1, GSKEL), F32),
            pltpu.VMEM((2, N_TY, 1, GSKEL), F32),
            pltpu.VMEM((1, 1, 128), F32),
            pltpu.VMEM((1, N_TY, 1, 128), F32),
            pltpu.VMEM((1, N_TX, 1, 128), F32),
            pltpu.VMEM((1, 1, 128), F32),
            dma((WAVES,)), dma((WAVES, 3)),
            *[dma((2,))] * 16,
        ],
        compiler_params=pltpu.CompilerParams(
            collective_id=0, has_side_effects=True, vmem_limit_bytes=64 * 1024 * 1024 - 512 * 1024
        ),
        name="ridge_cg",
    )(points, right_side, near_list, leaf_skeleton, top_index)
    return both[: HALVES * HALF], both[HALVES * HALF :]


def solution(mesh):
    placed = (
        P(None, ("tx", "ty")),
        P(("tx", "ty")),
        P(("tx", "ty"), None),
        P(("tx", "ty"), None),
        P(("tx", "ty")),
    )
    return jax.shard_map(
        on_device,
        mesh=mesh,
        in_specs=placed,
        out_specs=(P(("tx", "ty")), P(("tx", "ty"))),
        check_vma=False,
    )
```
